256 devices in a mesh: outer: 16 (over x, y), ctx: 16 (over z, core).
Axes of the slice: x: 4, y: 4, z: 8, core: 2. Of those that a mesh axis runs over, the one named last changes fastest.
Arguments:
- hidden_rows: float32 [2048, 8192], P('outer'), may hold values from -6 to 6
- query_weight: float32 [8192, 4096], P('outer', 'ctx'), may hold values from -0.0625 to 0.0625
- key_cache: float32 [4096, 512], P('ctx')
- value_cache: float32 [4096, 512], P('ctx'), may hold values from -6 to 6
- vertical_blocks: int32 [32, 16], replicated, may hold values from 0 to 63, as said below
- vertical_count: int32 [32], replicated, may hold values from 1 to 16
- slash_offsets: int32 [32, 16], replicated, may hold values from 0 to 63, as said below
- slash_count: int32 [32], replicated, may hold values from 1 to 16
- output_weight: float32 [4096, 8192], P('ctx', 'outer'), may hold values from -2.4 to 2.4
Outputs:
- mixed: float32 [2048, 8192], P('outer', 'ctx')
The draws below stay inside these ranges and needn't reach their ends.
Inputs may be any that keep to these rules, and one draw needn't show every extreme that they name: `vertical_blocks`: slot 0 of every head holds block 0; slots at or past a head's vertical_count are unused. `slash_offsets`: slot 0 of every head holds offset 0; slots at or past a head's slash_count are unused.
All inputs are finite; a program needn't handle non-finite values.
Results may differ from the reference program's by a relative error of at most 0.0003.
Values sent between devices are 32-bit elements; how exact they have to be, the bound alone decides.
No kernel may reach another device: no remote copies, remote signals or barrier semaphores. Data moves between devices by JAX's collectives and lax.ppermute only.
A program may use at most 192 MiB of HBM per device.

```python
import math
import jax
import jax.numpy as jnp
from jax import lax

D = 8192
HQ = 32
KVH = 4
HD = 128
BLOCK = 64
NV = 16
NS = 16
QTOK = 2048
SEQ = 4096
NB = 64


def draw_key_cache(key, part):
    key = jax.random.fold_in(key, 11)
    base = jax.random.normal(key, (SEQ, KVH * HD), jnp.float32)
    return base


def draw_vertical_blocks(key, part):
    key = jax.random.fold_in(key, 21)
    picks = jax.random.randint(key, (HQ, NV), 0, NB)
    return picks.at[:, 0].set(0)


def draw_slash_offsets(key, part):
    key = jax.random.fold_in(key, 22)
    picks = jax.random.randint(key, (HQ, NS), 0, NB)
    return picks.at[:, 0].set(0)


def touch_ends(values, rng, low, high):
    longest = values.shape.index(max(values.shape))
    spots = []
    for shift in (0, 1):
        where = [jax.random.randint(jax.random.fold_in(rng, axis), (), 0, length) for axis, length in enumerate(values.shape)]
        where[longest] = (where[longest] + shift) % values.shape[longest]
        spots.append(tuple(where))
    return values.at[spots[0]].set(low).at[spots[1]].set(high)


def level_of(key, shape, split, low, largest):
    gain, own = 1.0, jax.random.fold_in(key, 6)
    for axis_at, shards_of in split:
        heights = jnp.exp(jax.random.uniform(jax.random.fold_in(own, axis_at), (shards_of,), jnp.float32, low / len(split), largest / len(split)))
        gain = gain * jnp.repeat(heights, shape[axis_at] // shards_of).reshape([-1 if axis == axis_at else 1 for axis in range(len(shape))])
    return gain


def noise(own_key, dims, width, reach, pieces=(), held_as=jnp.bfloat16):
    loudness = level_of(own_key, dims, pieces, -0.22, 0.18) if pieces else 1.0
    entries = jax.random.normal(own_key, dims, jnp.float32) * width * loudness
    return jnp.minimum(jnp.maximum(entries, -reach), reach).astype(held_as)


def setup_inputs(seed: int = 0) -> dict:
    seeds = jax.random.split(jax.random.key(seed), 10)
    return {
        "hidden_rows": noise(seeds[0], (QTOK, D), 1.0, 6.0, ((0, 16),), jnp.float32),
        "query_weight": noise(seeds[1], (D, HQ * HD), D ** -0.5, 0.0625, ((0, 16), (1, 16)), jnp.float32),
        "key_cache": draw_key_cache(jax.random.fold_in(seeds[9], 71), 0),
        "value_cache": noise(seeds[3], (SEQ, KVH * HD), 1.0, 6.0, ((0, 16),), jnp.float32),
        "vertical_blocks": draw_vertical_blocks(jax.random.fold_in(seeds[9], 71), 0),
        "vertical_count": touch_ends(jax.random.randint(seeds[5], (HQ,), 1, NV + 1), jax.random.fold_in(seeds[5], 1), 1, NV).astype(jnp.int32),
        "slash_offsets": draw_slash_offsets(jax.random.fold_in(seeds[9], 71), 0),
        "slash_count": touch_ends(jax.random.randint(seeds[7], (HQ,), 1, NS + 1), jax.random.fold_in(seeds[7], 1), 1, NS).astype(jnp.int32),
        "output_weight": noise(seeds[8], (HQ * HD, D), 0.4, 2.4, ((0, 16), (1, 16)), jnp.float32),
    }


def reference(hidden_rows, query_weight, key_cache, value_cache, vertical_blocks, vertical_count, slash_offsets, slash_count, output_weight):
    highest = lax.Precision.HIGHEST
    query_all = jnp.dot(hidden_rows, query_weight, precision=highest, preferred_element_type=jnp.float32).reshape(QTOK, HQ, HD)
    key_pos = jnp.arange(SEQ, dtype=jnp.int32)
    query_pos = SEQ - QTOK + jnp.arange(QTOK, dtype=jnp.int32)
    distance = query_pos[:, None] - key_pos[None, :]
    causal = distance >= 0
    band_index = jnp.clip(distance // BLOCK, 0, NB - 1)
    key_block = key_pos // BLOCK
    slot_vertical = jnp.arange(NV, dtype=jnp.int32)
    slot_slash = jnp.arange(NS, dtype=jnp.int32)
    block_ids = jnp.arange(NB, dtype=jnp.int32)
    score_scale = 1.0 / math.sqrt(HD)

    def one_head(head):
        kv_index = (head // (HQ // KVH)).astype(jnp.int32)
        vert_valid = slot_vertical < vertical_count[head]
        vert_mask = jnp.any((vertical_blocks[head][:, None] == key_block[None, :]) & vert_valid[:, None], axis=0)
        slash_valid = slot_slash < slash_count[head]
        slash_table = jnp.any((slash_offsets[head][:, None] == block_ids[None, :]) & slash_valid[:, None], axis=0)
        allowed = causal & (vert_mask[None, :] | slash_table[band_index])
        key_rows = lax.dynamic_slice_in_dim(key_cache, kv_index * HD, HD, 1)
        value_rows = lax.dynamic_slice_in_dim(value_cache, kv_index * HD, HD, 1)
        scores = jnp.dot(query_all[:, head], key_rows.T, precision=highest, preferred_element_type=jnp.float32) * score_scale
        row_max = lax.optimization_barrier(jnp.max(jnp.where(allowed, scores, -jnp.inf), axis=1, keepdims=True))
        weights = jnp.exp(jnp.where(allowed, scores - row_max, -jnp.inf))
        summed = jnp.dot(weights, value_rows, precision=highest, preferred_element_type=jnp.float32)
        return summed / lax.optimization_barrier(jnp.sum(weights, axis=1, keepdims=True))
    attended = lax.map(one_head, jnp.arange(HQ, dtype=jnp.int32))
    attended = jnp.transpose(attended, (1, 0, 2)).reshape(QTOK, HQ * HD)
    return jnp.dot(attended, output_weight, precision=highest, preferred_element_type=jnp.float32)
```

```python
import functools
import math

import jax
import jax.numpy as jnp
from jax import lax
from jax.experimental import pallas as pl
from jax.experimental.pallas import tpu as pltpu
from jax.sharding import Mesh
from jax.sharding import PartitionSpec as P

HD = 128
BLOCK = 64
NX, NY, NZ, NK = 4, 4, 8, 2
ALL = ("x", "y", "z", "k")
VMEM = pl.BlockSpec(memory_space=pltpu.VMEM)
SMEM = pl.BlockSpec(memory_space=pltpu.SMEM)


def split(value):
    high = value.astype(jnp.bfloat16)
    low = (value - high.astype(jnp.float32)).astype(jnp.bfloat16)
    return high, low


def dot3(left, right, dims):
    (lh, ll), (rh, rl) = left, right
    one = functools.partial(
        lax.dot_general, dimension_numbers=dims, preferred_element_type=jnp.float32
    )
    return one(lh, rh) + (one(lh, rl) + one(ll, rh))


MM = (((1,), (0,)), ((), ()))
MT = (((1,), (1,)), ((), ()))


def project_kernel(where, hidden, *refs):
    weights, out = refs[:8], refs[8]
    y, k = where[0], where[1]
    totals = [None, None]
    for shift in range(NY):
        owner = lax.rem(y - shift + NY, NY)
        left = split(hidden[:, pl.ds(pl.multiple_of(owner * 512, 512), 512)])
        for other in range(2):
            term = dot3(left, split(weights[2 * shift + other][...]), MM)
            totals[other] = term if totals[other] is None else totals[other] + term
    for other in range(2):
        core = k if other == 0 else 1 - k
        for b in range(2):
            out[2 * core + b] = totals[other][:, b * HD : (b + 1) * HD]


def project(where, hidden, weights):
    return pl.pallas_call(
        project_kernel,
        out_shape=jax.ShapeDtypeStruct((NX, 256, HD), jnp.float32),
        in_specs=[SMEM] + [VMEM] * 9,
        out_specs=VMEM,
        compiler_params=pltpu.CompilerParams(vmem_limit_bytes=40 << 20),
        cost_estimate=pl.CostEstimate(
            flops=6 * 256 * 2048 * 512, bytes_accessed=7 << 20, transcendentals=0
        ),
        name="project",
    )(where, hidden, *weights)


def attend_kernel(query, kv, low, up, out, scores):
    tiles = kv.shape[0]
    width = kv.shape[2]
    row = lax.broadcasted_iota(jnp.int32, (BLOCK, width), 0)
    col = lax.broadcasted_iota(jnp.int32, (BLOCK, width), 1)
    lower = row >= lax.rem(col, BLOCK)
    left = split(query[...] * (math.log2(math.e) / math.sqrt(HD)))
    top = None
    for tile in range(tiles):
        s = dot3(left, split(kv[tile, 0]), MT)
        cols = slice(tile * width, (tile + 1) * width)
        bias = jnp.concatenate(
            [
                jnp.where(lower, low[b : b + 1, cols], up[b : b + 1, cols])
                for b in range(low.shape[0])
            ],
            axis=0,
        )
        s = s + bias
        scores[tile] = s
        top = s if top is None else jnp.maximum(top, s)
    top = jnp.max(top, axis=1, keepdims=True)
    total, summed = None, None
    for tile in range(tiles):
        weight = jnp.exp2(scores[tile] - top)
        term = dot3(split(weight), split(kv[tile, 1]), MM)
        total = weight if total is None else total + weight
        summed = term if summed is None else summed + term
    out[...] = summed / jnp.sum(total, axis=1, keepdims=True)


def attend(query, kv, low, up):
    tiles, _, width, _ = kv.shape
    return pl.pallas_call(
        attend_kernel,
        out_shape=jax.ShapeDtypeStruct(query.shape, jnp.float32),
        in_specs=[VMEM] * 4,
        out_specs=VMEM,
        scratch_shapes=[pltpu.VMEM((tiles, query.shape[0], width), jnp.float32)],
        compiler_params=pltpu.CompilerParams(vmem_limit_bytes=48 << 20),
        cost_estimate=pl.CostEstimate(
            flops=12 * 256 * 4096 * HD, bytes_accessed=5 << 20, transcendentals=256 * 4096
        ),
        name="attend",
    )(query, kv, low, up)


def mix_kernel(attended, weights, out):
    for core in range(NK):
        total = None
        for y in range(NY):
            left = jnp.concatenate([attended[2 * y], attended[2 * y + 1]], axis=1)
            term = dot3(split(left), split(weights[2 * y + core]), MM)
            total = term if total is None else total + term
        for x in range(NX):
            out[x, :, core * 512 : (core + 1) * 512] = total[x * BLOCK : (x + 1) * BLOCK]


def mix(attended, weights):
    return pl.pallas_call(
        mix_kernel,
        out_shape=jax.ShapeDtypeStruct((NX, BLOCK, 1024), jnp.float32),
        in_specs=[VMEM] * 2,
        out_specs=VMEM,
        compiler_params=pltpu.CompilerParams(vmem_limit_bytes=40 << 20),
        cost_estimate=pl.CostEstimate(
            flops=6 * 256 * 1024 * 1024, bytes_accessed=6 << 20, transcendentals=0
        ),
        name="mix",
    )(attended, weights)


def allowed_rows(x, y, z, k, vertical_blocks, vertical_count, slash_offsets, slash_count):
    head = 8 * x + z
    slots = jnp.arange(vertical_blocks.shape[1], dtype=jnp.int32)
    used_v = slots < vertical_count[head]
    used_s = slots < slash_count[head]
    verticals = jnp.where(used_v, vertical_blocks[head], -1)
    slashes = jnp.where(used_s, slash_offsets[head], -1)
    query_block = 32 + 8 * jnp.arange(NX, dtype=jnp.int32) + 2 * y + k
    key_block = jnp.arange(64 * BLOCK, dtype=jnp.int32) // BLOCK
    offset = query_block[:, None] - key_block[None, :]
    vert = jnp.any(key_block[:, None] == verticals[None, :], axis=1)[None, :]
    low_slash = jnp.any(offset[:, :, None] == slashes, axis=2)
    up_slash = jnp.any((offset - 1)[:, :, None] == slashes, axis=2)
    low = (offset >= 0) & (vert | low_slash)
    up = (offset >= 1) & (vert | up_slash)
    return jnp.where(low, 0.0, -jnp.inf), jnp.where(up, 0.0, -jnp.inf)


def place(x, y, z, k):
    return ((x * NY + y) * NZ + z) * NK + k


CORES = [(0, 1), (1, 0)]
OTHERS = [
    (place(x, y, z, k), place(z >> 1, y, 4 * (z & 1) + x, k))
    for x in range(NX)
    for y in range(NY)
    for z in range(NZ)
    for k in range(NK)
]
FLIPPED = [(a * 16 + b, b * 16 + a) for a in range(16) for b in range(16)]


def shards(
    hidden_rows,
    query_weight,
    key_cache,
    value_cache,
    vertical_blocks,
    vertical_count,
    slash_offsets,
    slash_count,
    output_weight,
):
    x, y, z, k = (lax.axis_index(name) for name in ALL)
    kv_own = jnp.stack(
        [
            lax.dynamic_slice_in_dim(key_cache, x * HD, HD, 1),
            lax.dynamic_slice_in_dim(value_cache, x * HD, HD, 1),
        ]
    )
    kv = lax.all_gather(kv_own, ("z", "k"), axis=0)
    flipped = lax.ppermute(output_weight, ALL, FLIPPED)
    out_weight = lax.all_gather(flipped, ("y", "k"), axis=0)
    weights = []
    for shift in range(NY):
        piece = query_weight
        if shift:
            piece = lax.ppermute(
                query_weight, "y", [(i, (i + shift) % NY) for i in range(NY)]
            )
        weights += [piece, lax.ppermute(piece, "k", CORES)]
    half = lax.dynamic_slice_in_dim(hidden_rows, k * BLOCK, BLOCK, 0)
    half = half.reshape(BLOCK, NX, 2048).transpose(1, 0, 2)
    hidden = lax.all_to_all(half, "x", 0, 0).reshape(NX * BLOCK, 2048)
    partial = project(jnp.stack([y, k]).astype(jnp.int32), hidden, weights)
    summed = jnp.sum(lax.all_to_all(partial, "x", 0, 0), axis=0)
    query = lax.ppermute(summed, ALL, OTHERS)
    low, up = allowed_rows(
        x, y, z, k, vertical_blocks, vertical_count, slash_offsets, slash_count
    )
    attended = attend(query, kv, low, up)
    heads = lax.all_to_all(jnp.broadcast_to(attended, (NZ,) + attended.shape), "z", 0, 0)
    mixed = mix(heads, out_weight)
    rows = jnp.sum(lax.all_to_all(mixed, "x", 0, 0), axis=0)
    own = lax.dynamic_slice_in_dim(rows, k * 512, 512, 1)
    other = lax.ppermute(lax.dynamic_slice_in_dim(rows, (1 - k) * 512, 512, 1), "k", CORES)
    first = jnp.where(k == 0, own, other)
    second = jnp.where(k == 0, other, own)
    return jnp.concatenate([first, second], axis=0)


def solution(mesh):
    grid = Mesh(mesh.devices.reshape(NX, NY, NZ, NK), ALL)
    outer, ctx = ("x", "y"), ("z", "k")
    placed = (
        P(outer, None),
        P(outer, ctx),
        P(ctx, None),
        P(ctx, None),
        P(),
        P(),
        P(),
        P(),
        P(ctx, outer),
    )
    return jax.shard_map(
        shards, mesh=grid, in_specs=placed, out_specs=P(outer, ctx), check_vma=False
    )
```

```python
import functools
import math

import jax
import jax.numpy as jnp
from jax import lax
from jax.experimental import pallas as pl
from jax.experimental.pallas import tpu as pltpu
from jax.sharding import Mesh
from jax.sharding import PartitionSpec as P

HD = 128
BLOCK = 64
NX, NY, NZ, NK = 4, 4, 8, 2
ALL = ("x", "y", "z", "k")
VMEM = pl.BlockSpec(memory_space=pltpu.VMEM)
SMEM = pl.BlockSpec(memory_space=pltpu.SMEM)
ANY = pl.BlockSpec(memory_space=pl.ANY)


def split(value):
    high = value.astype(jnp.bfloat16)
    low = (value - high.astype(jnp.float32)).astype(jnp.bfloat16)
    return high, low


def dot3(left, right, dims):
    (lh, ll), (rh, rl) = left, right
    one = functools.partial(
        lax.dot_general, dimension_numbers=dims, preferred_element_type=jnp.float32
    )
    return one(lh, rh) + (one(lh, rl) + one(ll, rh))


MM = (((1,), (0,)), ((), ()))
MT = (((1,), (1,)), ((), ()))


def pick_kernel(where, rows, out):
    out[0] = rows[...]


def pick(k, hidden_rows):
    return pl.pallas_call(
        pick_kernel,
        out_shape=jax.ShapeDtypeStruct((NX, BLOCK, 2048), jnp.float32),
        grid_spec=pltpu.PrefetchScalarGridSpec(
            num_scalar_prefetch=1,
            grid=(NX,),
            in_specs=[pl.BlockSpec((BLOCK, 2048), lambda i, where: (where[0], i))],
            out_specs=pl.BlockSpec((1, BLOCK, 2048), lambda i, where: (i, 0, 0)),
        ),
        name="pick",
    )(k, hidden_rows)


def project_kernel(hidden, weights, out, left_buf, right_buf, left_sem, right_sem):
    copies = []
    for y in range(NY):
        cols = pl.ds(y * 512, 512)
        copies.append(
            (
                pltpu.make_async_copy(hidden.at[:, :, cols], left_buf.at[y], left_sem.at[y]),
                pltpu.make_async_copy(
                    weights.at[pl.ds(2 * y, 2)], right_buf.at[y], right_sem.at[y]
                ),
            )
        )
        for copy in copies[y]:
            copy.start()
    totals = [None, None]
    for y in range(NY):
        for copy in copies[y]:
            copy.wait()
        left = split(left_buf[y].reshape(NX * BLOCK, 512))
        for core in range(NK):
            term = dot3(left, split(right_buf[y, core]), MM)
            totals[core] = term if totals[core] is None else totals[core] + term
    for core in range(NK):
        for b in range(2):
            out[2 * core + b] = totals[core][:, b * HD : (b + 1) * HD]


def project(hidden, weights):
    return pl.pallas_call(
        project_kernel,
        out_shape=jax.ShapeDtypeStruct((NX, NX * BLOCK, HD), jnp.float32),
        in_specs=[ANY, ANY],
        out_specs=VMEM,
        scratch_shapes=[
            pltpu.VMEM((NY, NX, BLOCK, 512), jnp.float32),
            pltpu.VMEM((NY, NK, 512, 256), jnp.float32),
            pltpu.SemaphoreType.DMA((NY,)),
            pltpu.SemaphoreType.DMA((NY,)),
        ],
        compiler_params=pltpu.CompilerParams(vmem_limit_bytes=32 << 20),
        cost_estimate=pl.CostEstimate(
            flops=6 * 256 * 2048 * 512, bytes_accessed=7 << 20, transcendentals=0
        ),
        name="project",
    )(hidden, weights)


def attend_kernel(partial, low, up, *refs):
    pieces, (out, kv, scores, sem) = refs[:8], refs[8:]
    tiles = len(pieces)
    copies = [
        pltpu.make_async_copy(piece, kv.at[tile], sem.at[tile])
        for tile, piece in enumerate(pieces)
    ]
    for copy in copies:
        copy.start()
    width = NZ * BLOCK
    row = lax.broadcasted_iota(jnp.int32, (BLOCK, width), 0)
    col = lax.broadcasted_iota(jnp.int32, (BLOCK, width), 1)
    lower = row >= lax.rem(col, BLOCK)
    query = (partial[0] + partial[1]) + (partial[2] + partial[3])
    left = split(query * (math.log2(math.e) / math.sqrt(HD)))
    top = None
    for tile in range(tiles):
        copies[tile].wait()
        s = dot3(left, split(kv[tile, :, 0].reshape(width, HD)), MT)
        cols = slice(tile * width, (tile + 1) * width)
        bias = jnp.concatenate(
            [
                jnp.where(lower, low[b : b + 1, cols], up[b : b + 1, cols])
                for b in range(NX)
            ],
            axis=0,
        )
        s = s + bias
        scores[tile] = s
        top = s if top is None else jnp.maximum(top, s)
    top = jnp.max(top, axis=1, keepdims=True)
    total, summed = None, None
    for tile in range(tiles):
        weight = jnp.exp2(scores[tile] - top)
        term = dot3(split(weight), split(kv[tile, :, 1].reshape(width, HD)), MM)
        total = weight if total is None else total + weight
        summed = term if summed is None else summed + term
    attended = summed / jnp.sum(total, axis=1, keepdims=True)
    for z in range(NZ):
        out[z] = attended


def attend(partial, low, up, pieces):
    rows = NX * BLOCK
    return pl.pallas_call(
        attend_kernel,
        out_shape=jax.ShapeDtypeStruct((NZ, rows, HD), jnp.float32),
        in_specs=[VMEM] * 3 + [ANY] * 8,
        out_specs=VMEM,
        scratch_shapes=[
            pltpu.VMEM((8, NZ, 2, BLOCK, HD), jnp.float32),
            pltpu.VMEM((8, rows, NZ * BLOCK), jnp.float32),
            pltpu.SemaphoreType.DMA((8,)),
        ],
        compiler_params=pltpu.CompilerParams(vmem_limit_bytes=48 << 20),
        cost_estimate=pl.CostEstimate(
            flops=12 * 256 * 4096 * HD, bytes_accessed=6 << 20, transcendentals=256 * 4096
        ),
        name="attend",
    )(partial, low, up, *pieces)


def mix_kernel(where, heads, weights, out, buf, sem):
    copies = []
    for step in range(8):
        copies.append(pltpu.make_async_copy(weights.at[step], buf.at[step], sem.at[step]))
        copies[step].start()
    totals = [None, None]
    swap = where[0]
    for step in range(8):
        y, core = step // 2, step % 2
        spot = (y + NY - (where[1] + core)) & 3
        left = jnp.concatenate(
            [heads[spot + 4 * swap], heads[spot + 4 * (1 - swap)]], axis=1
        )
        left = split(left)
        copies[step].wait()
        term = dot3(left, split(buf[step].reshape(2 * HD, 512)), MM)
        totals[core] = term if totals[core] is None else totals[core] + term
    for core in range(NK):
        for x in range(NX):
            out[2 * x + core] = totals[core][x * BLOCK : (x + 1) * BLOCK]


def mix(where, heads, weights):
    return pl.pallas_call(
        mix_kernel,
        out_shape=jax.ShapeDtypeStruct((NX * NK, BLOCK, 512), jnp.float32),
        in_specs=[SMEM, VMEM, ANY],
        out_specs=VMEM,
        scratch_shapes=[
            pltpu.VMEM((8, 2, HD, 512), jnp.float32),
            pltpu.SemaphoreType.DMA((8,)),
        ],
        compiler_params=pltpu.CompilerParams(vmem_limit_bytes=32 << 20),
        cost_estimate=pl.CostEstimate(
            flops=6 * 256 * 1024 * 1024, bytes_accessed=6 << 20, transcendentals=0
        ),
        name="mix",
    )(where, heads, weights)


def allowed_rows(
    head, key_block, query_block, vertical_blocks, vertical_count, slash_offsets, slash_count
):
    slots = jnp.arange(vertical_blocks.shape[1], dtype=jnp.int32)
    verticals = jnp.where(slots < vertical_count[head], vertical_blocks[head], -1)
    slashes = jnp.where(slots < slash_count[head], slash_offsets[head], -1)
    offset = query_block[:, None] - key_block[None, :]
    vert = jnp.any(key_block[:, None] == verticals[None, :], axis=1)[None, :]
    low_slash = jnp.any(offset[:, :, None] == slashes, axis=2)
    up_slash = jnp.any((offset - 1)[:, :, None] == slashes, axis=2)
    low = (offset >= 0) & (vert | low_slash)
    up = (offset >= 1) & (vert | up_slash)
    bias = jnp.where(jnp.stack([low, up]), 0.0, -jnp.inf)
    bias = jnp.repeat(bias, BLOCK, axis=2)
    return bias[0], bias[1]


def place(x, y, z, k):
    return ((x * NY + y) * NZ + z) * NK + k


def every():
    return [
        (x, y, z, k)
        for x in range(NX)
        for y in range(NY)
        for z in range(NZ)
        for k in range(NK)
    ]


CORES = [(0, 1), (1, 0)]


def row_moves(number):
    moves = []
    for x, y, z, k in every():
        half = number ^ (z >> 2)
        moves.append(
            (place(x, y, z, k), place(2 * k + half, (y + z) % NY, 2 * x + (y >> 1), y & 1))
        )
    return moves


def shards(
    hidden_rows,
    query_weight,
    key_cache,
    value_cache,
    vertical_blocks,
    vertical_count,
    slash_offsets,
    slash_count,
    output_weight,
):
    x, y, z, k = (lax.axis_index(name) for name in ALL)
    weights = lax.all_gather(query_weight, ("y", "k"), axis=0)
    quarters = [
        lax.dynamic_slice_in_dim(cache, y * BLOCK, BLOCK, 0)
        for cache in (key_cache, value_cache)
    ]
    sent = jnp.stack(
        [
            jnp.stack([quarter[:, (to // 2) * HD : (to // 2 + 1) * HD] for quarter in quarters])
            for to in range(NZ)
        ]
    )
    near = lax.all_to_all(sent, "z", 0, 0)
    halves = pick(k.reshape(1).astype(jnp.int32), hidden_rows)
    hidden = lax.all_to_all(halves, "x", 0, 0)
    pieces = []
    key_block = []
    for shift in range(NY):
        piece = near
        if shift:
            piece = lax.ppermute(near, "y", [(i, (i + shift) % NY) for i in range(NY)])
        pieces += [piece, lax.ppermute(piece, "k", CORES)]
        for core in (k, 1 - k):
            key_block.append(
                4 * (2 * jnp.arange(NZ, dtype=jnp.int32) + core) + (y - shift) % NY
            )
    rows, _ = lax.optimization_barrier((output_weight, near))
    moved = jnp.stack(
        [
            lax.ppermute(
                lax.dynamic_slice_in_dim(rows, (number ^ (z >> 2)) * HD, HD, 0),
                ALL,
                row_moves(number),
            )
            for number in range(2)
        ]
    )
    partial = project(hidden, weights)
    moved, partial = lax.optimization_barrier((moved, partial))
    out_weight = lax.all_gather(moved, ("y", "k"), axis=0)
    partial = lax.all_to_all(partial, "x", 0, 0)
    low, up = allowed_rows(
        4 * z + x,
        jnp.concatenate(key_block),
        32 + 8 * jnp.arange(NX, dtype=jnp.int32) + 2 * y + k,
        vertical_blocks,
        vertical_count,
        slash_offsets,
        slash_count,
    )
    heads = attend(partial, low, up, pieces)
    heads = lax.all_to_all(heads, "z", 0, 0)
    where = jnp.stack([x & 1, 2 * (z & 1)]).astype(jnp.int32)
    mixed = mix(where, heads, out_weight)
    mixed = lax.all_to_all(mixed, ("x", "k"), 0, 0)
    return jnp.sum(mixed.reshape(NX, NK * BLOCK, 512), axis=0)


def solution(mesh):
    grid = Mesh(mesh.devices.reshape(NX, NY, NZ, NK), ALL)
    outer, ctx = ("x", "y"), ("z", "k")
    placed = (
        P(outer, None),
        P(outer, ctx),
        P(ctx, None),
        P(ctx, None),
        P(),
        P(),
        P(),
        P(),
        P(ctx, outer),
    )
    return jax.shard_map(
        shards, mesh=grid, in_specs=placed, out_specs=P(outer, ctx), check_vma=False
    )
```

```python
import functools
import math

import jax
import jax.numpy as jnp
from jax import lax
from jax.experimental import pallas as pl
from jax.experimental.pallas import tpu as pltpu
from jax.sharding import Mesh
from jax.sharding import PartitionSpec as P

HD = 128
BLOCK = 64
NX, NY, NZ, NK = 4, 4, 8, 2
ALL = ("x", "y", "z", "k")
VMEM = pl.BlockSpec(memory_space=pltpu.VMEM)
SMEM = pl.BlockSpec(memory_space=pltpu.SMEM)
ANY = pl.BlockSpec(memory_space=pl.ANY)


def split(value):
    high = value.astype(jnp.bfloat16)
    low = (value - high.astype(jnp.float32)).astype(jnp.bfloat16)
    return high, low


def dot3(left, right, dims):
    (lh, ll), (rh, rl) = left, right
    one = functools.partial(
        lax.dot_general, dimension_numbers=dims, preferred_element_type=jnp.float32
    )
    return one(lh, rh) + (one(lh, rl) + one(ll, rh))


MM = (((1,), (0,)), ((), ()))
MT = (((1,), (1,)), ((), ()))


def pick_kernel(where, rows, out):
    out[0] = rows[...]


def pick(k, hidden_rows):
    return pl.pallas_call(
        pick_kernel,
        out_shape=jax.ShapeDtypeStruct((NX, BLOCK, 2048), jnp.float32),
        grid_spec=pltpu.PrefetchScalarGridSpec(
            num_scalar_prefetch=1,
            grid=(NX,),
            in_specs=[pl.BlockSpec((BLOCK, 2048), lambda i, where: (where[0], i))],
            out_specs=pl.BlockSpec((1, BLOCK, 2048), lambda i, where: (i, 0, 0)),
        ),
        name="pick",
    )(k, hidden_rows)


def project_kernel(hidden, weights, out, left_buf, right_buf, left_sem, right_sem):
    copies = []
    for y in range(NY):
        cols = pl.ds(y * 512, 512)
        copies.append(
            (
                pltpu.make_async_copy(hidden.at[:, :, cols], left_buf.at[y], left_sem.at[y]),
                pltpu.make_async_copy(
                    weights.at[pl.ds(2 * y, 2)], right_buf.at[y], right_sem.at[y]
                ),
            )
        )
        for copy in copies[y]:
            copy.start()
    totals = [None, None]
    for y in range(NY):
        for copy in copies[y]:
            copy.wait()
        left = split(left_buf[y].reshape(NX * BLOCK, 512))
        for core in range(NK):
            term = dot3(left, split(right_buf[y, core]), MM)
            totals[core] = term if totals[core] is None else totals[core] + term
    for core in range(NK):
        for b in range(2):
            out[2 * core + b] = totals[core][:, b * HD : (b + 1) * HD]


def project(hidden, weights):
    return pl.pallas_call(
        project_kernel,
        out_shape=jax.ShapeDtypeStruct((NX, NX * BLOCK, HD), jnp.float32),
        in_specs=[ANY, ANY],
        out_specs=VMEM,
        scratch_shapes=[
            pltpu.VMEM((NY, NX, BLOCK, 512), jnp.float32),
            pltpu.VMEM((NY, NK, 512, 256), jnp.float32),
            pltpu.SemaphoreType.DMA((NY,)),
            pltpu.SemaphoreType.DMA((NY,)),
        ],
        compiler_params=pltpu.CompilerParams(vmem_limit_bytes=32 << 20),
        cost_estimate=pl.CostEstimate(
            flops=6 * 256 * 2048 * 512, bytes_accessed=7 << 20, transcendentals=0
        ),
        name="project",
    )(hidden, weights)


def attend_kernel(partial, low, up, *refs):
    pieces, (out, kv, scores, sem) = refs[:8], refs[8:]
    tiles = len(pieces)
    copies = [
        pltpu.make_async_copy(piece, kv.at[tile], sem.at[tile])
        for tile, piece in enumerate(pieces)
    ]
    for copy in copies:
        copy.start()
    width = NZ * BLOCK
    row = lax.broadcasted_iota(jnp.int32, (BLOCK, width), 0)
    col = lax.broadcasted_iota(jnp.int32, (BLOCK, width), 1)
    lower = row >= lax.rem(col, BLOCK)
    query = (partial[0] + partial[1]) + (partial[2] + partial[3])
    left = split(query * (math.log2(math.e) / math.sqrt(HD)))
    top = None
    for tile in range(tiles):
        copies[tile].wait()
        s = dot3(left, split(kv[tile, :, 0].reshape(width, HD)), MT)
        cols = slice(tile * width, (tile + 1) * width)
        bias = jnp.concatenate(
            [
                jnp.where(lower, low[b : b + 1, cols], up[b : b + 1, cols])
                for b in range(NX)
            ],
            axis=0,
        )
        s = s + bias
        scores[tile] = s
        top = s if top is None else jnp.maximum(top, s)
    top = jnp.max(top, axis=1, keepdims=True)
    total, summed = None, None
    for tile in range(tiles):
        weight = jnp.exp2(scores[tile] - top)
        term = dot3(split(weight), split(kv[tile, :, 1].reshape(width, HD)), MM)
        total = weight if total is None else total + weight
        summed = term if summed is None else summed + term
    attended = summed / jnp.sum(total, axis=1, keepdims=True)
    for z in range(NZ):
        out[z] = attended


def attend(partial, low, up, pieces):
    rows = NX * BLOCK
    return pl.pallas_call(
        attend_kernel,
        out_shape=jax.ShapeDtypeStruct((NZ, rows, HD), jnp.float32),
        in_specs=[VMEM] * 3 + [ANY] * 8,
        out_specs=VMEM,
        scratch_shapes=[
            pltpu.VMEM((8, NZ, 2, BLOCK, HD), jnp.float32),
            pltpu.VMEM((8, rows, NZ * BLOCK), jnp.float32),
            pltpu.SemaphoreType.DMA((8,)),
        ],
        compiler_params=pltpu.CompilerParams(vmem_limit_bytes=48 << 20),
        cost_estimate=pl.CostEstimate(
            flops=12 * 256 * 4096 * HD, bytes_accessed=6 << 20, transcendentals=256 * 4096
        ),
        name="attend",
    )(partial, low, up, *pieces)


def mix_kernel(heads, weights, out, buf, sem):
    steps = NZ // 2
    copies = []
    for step in range(steps):
        copies.append(
            pltpu.make_async_copy(
                weights.at[:, pl.ds(2 * step, 2)], buf.at[step], sem.at[step]
            )
        )
        copies[step].start()
    totals = [None, None]
    for step in range(steps):
        left = split(jnp.concatenate([heads[2 * step], heads[2 * step + 1]], axis=1))
        copies[step].wait()
        for core in range(NK):
            right = jnp.concatenate(
                [buf[step, :, z, core].reshape(HD, 512) for z in range(2)], axis=0
            )
            term = dot3(left, split(right), MM)
            totals[core] = term if totals[core] is None else totals[core] + term
    for core in range(NK):
        for x in range(NX):
            out[2 * x + core] = totals[core][x * BLOCK : (x + 1) * BLOCK]


def mix(heads, weights):
    return pl.pallas_call(
        mix_kernel,
        out_shape=jax.ShapeDtypeStruct((NX * NK, BLOCK, 512), jnp.float32),
        in_specs=[VMEM, ANY],
        out_specs=VMEM,
        scratch_shapes=[
            pltpu.VMEM((NZ // 2, 8, 2, NK, 16, 512), jnp.float32),
            pltpu.SemaphoreType.DMA((NZ // 2,)),
        ],
        compiler_params=pltpu.CompilerParams(vmem_limit_bytes=32 << 20),
        cost_estimate=pl.CostEstimate(
            flops=6 * 256 * 1024 * 1024, bytes_accessed=6 << 20, transcendentals=0
        ),
        name="mix",
    )(heads, weights)


def allowed_rows(
    head, key_block, query_block, vertical_blocks, vertical_count, slash_offsets, slash_count
):
    slots = jnp.arange(vertical_blocks.shape[1], dtype=jnp.int32)
    verticals = jnp.where(slots < vertical_count[head], vertical_blocks[head], -1)
    slashes = jnp.where(slots < slash_count[head], slash_offsets[head], -1)
    offset = query_block[:, None] - key_block[None, :]
    vert = jnp.any(key_block[:, None] == verticals[None, :], axis=1)[None, :]
    low_slash = jnp.any(offset[:, :, None] == slashes, axis=2)
    up_slash = jnp.any((offset - 1)[:, :, None] == slashes, axis=2)
    low = (offset >= 0) & (vert | low_slash)
    up = (offset >= 1) & (vert | up_slash)
    bias = jnp.where(jnp.stack([low, up]), 0.0, -jnp.inf)
    bias = jnp.repeat(bias, BLOCK, axis=2)
    return bias[0], bias[1]


CORES = [(0, 1), (1, 0)]


def shards(
    hidden_rows,
    query_weight,
    key_cache,
    value_cache,
    vertical_blocks,
    vertical_count,
    slash_offsets,
    slash_count,
    output_weight,
):
    x, y, z, k = (lax.axis_index(name) for name in ALL)
    weights = lax.all_gather(query_weight, ("y", "k"), axis=0)
    rows = output_weight.reshape(2, NY, NK, 16, 512).transpose(2, 0, 1, 3, 4)
    rows = lax.all_to_all(rows, "k", 0, 0)
    rows = rows.reshape(NX * NY, 16, 512)
    rows = lax.all_to_all(rows, ("x", "y"), 0, 0)
    rows = lax.all_to_all(rows.reshape(NZ, NK, 16, 512), "z", 0, 0)
    out_weight = lax.all_gather(rows, ("y", "k"), axis=0)
    quarters = [
        lax.dynamic_slice_in_dim(cache, y * BLOCK, BLOCK, 0)
        for cache in (key_cache, value_cache)
    ]
    sent = jnp.stack(
        [
            jnp.stack([quarter[:, (to // 2) * HD : (to // 2 + 1) * HD] for quarter in quarters])
            for to in range(NZ)
        ]
    )
    near = lax.all_to_all(sent, "z", 0, 0)
    halves = pick(k.reshape(1).astype(jnp.int32), hidden_rows)
    hidden = lax.all_to_all(halves, "x", 0, 0)
    pieces = []
    key_block = []
    for shift in range(NY):
        piece = near
        if shift:
            piece = lax.ppermute(near, "y", [(i, (i + shift) % NY) for i in range(NY)])
        pieces += [piece, lax.ppermute(piece, "k", CORES)]
        for core in (k, 1 - k):
            key_block.append(
                4 * (2 * jnp.arange(NZ, dtype=jnp.int32) + core) + (y - shift) % NY
            )
    partial = project(hidden, weights)
    partial = lax.all_to_all(partial, "x", 0, 0)
    low, up = allowed_rows(
        4 * z + x,
        jnp.concatenate(key_block),
        32 + 8 * jnp.arange(NX, dtype=jnp.int32) + 2 * y + k,
        vertical_blocks,
        vertical_count,
        slash_offsets,
        slash_count,
    )
    heads = attend(partial, low, up, pieces)
    heads = lax.all_to_all(heads, "z", 0, 0)
    mixed = mix(heads, out_weight)
    mixed = lax.all_to_all(mixed, ("x", "k"), 0, 0)
    return jnp.sum(mixed.reshape(NX, NK * BLOCK, 512), axis=0)


def solution(mesh):
    grid = Mesh(mesh.devices.reshape(NX, NY, NZ, NK), ALL)
    outer, ctx = ("x", "y"), ("z", "k")
    placed = (
        P(outer, None),
        P(outer, ctx),
        P(ctx, None),
        P(ctx, None),
        P(),
        P(),
        P(),
        P(),
        P(ctx, outer),
    )
    return jax.shard_map(
        shards, mesh=grid, in_specs=placed, out_specs=P(outer, ctx), check_vma=False
    )
```

```python
import functools
import math

import jax
import jax.numpy as jnp
from jax import lax
from jax.experimental import pallas as pl
from jax.experimental.pallas import tpu as pltpu
from jax.sharding import Mesh
from jax.sharding import PartitionSpec as P

HD = 128
BLOCK = 64
NX, NY, NZ, NK = 4, 4, 8, 2
ALL = ("x", "y", "z", "k")
VMEM = pl.BlockSpec(memory_space=pltpu.VMEM)
SMEM = pl.BlockSpec(memory_space=pltpu.SMEM)
ANY = pl.BlockSpec(memory_space=pl.ANY)
HBM = pl.BlockSpec(memory_space=pltpu.HBM)


def split(value):
    high = value.astype(jnp.bfloat16)
    low = (value - high.astype(jnp.float32)).astype(jnp.bfloat16)
    return high, low


def dot3(left, right, dims):
    (lh, ll), (rh, rl) = left, right
    one = functools.partial(
        lax.dot_general, dimension_numbers=dims, preferred_element_type=jnp.float32
    )
    return one(lh, rh) + (one(lh, rl) + one(ll, rh))


MM = (((1,), (0,)), ((), ()))
MT = (((1,), (1,)), ((), ()))


def pick_kernel(where, rows, *refs):
    outs, sem = refs[:3], refs[3]
    copies = []
    for shift in range(1, NX):
        cols = pl.multiple_of(lax.rem(where[0] + shift, NX) * 2048, 2048)
        part = rows.at[pl.ds(pl.multiple_of(where[1] * BLOCK, BLOCK), BLOCK), pl.ds(cols, 2048)]
        copies.append(pltpu.make_async_copy(part, outs[shift - 1], sem.at[shift - 1]))
    for copy in copies:
        copy.start()
    for copy in copies:
        copy.wait()


def pick(where, hidden_rows):
    return pl.pallas_call(
        pick_kernel,
        out_shape=[jax.ShapeDtypeStruct((BLOCK, 2048), jnp.float32)] * 3,
        in_specs=[SMEM, HBM],
        out_specs=[HBM] * 3,
        scratch_shapes=[pltpu.SemaphoreType.DMA((3,))],
        name="pick",
    )(where, hidden_rows)


def project_kernel(where, rows, first, second, third, weights, out, left_buf, right_buf, sems):
    x, k = where[0], where[1]
    copies = []
    for y in range(NY):
        own = rows.at[
            pl.ds(pl.multiple_of(k * BLOCK, BLOCK), BLOCK),
            pl.ds(pl.multiple_of(x * 2048 + y * 512, 512), 512),
        ]
        parts = [own] + [part.at[:, pl.ds(y * 512, 512)] for part in (first, second, third)]
        group = [
            pltpu.make_async_copy(
                part, left_buf.at[y, lax.rem(x + NX - shift, NX)], sems.at[y, shift]
            )
            for shift, part in enumerate(parts)
        ]
        group.append(
            pltpu.make_async_copy(weights.at[pl.ds(2 * y, 2)], right_buf.at[y], sems.at[y, NX])
        )
        for copy in group:
            copy.start()
        copies.append(group)
    totals = [None, None]
    for y in range(NY):
        for copy in copies[y]:
            copy.wait()
        left = split(left_buf[y].reshape(NX * BLOCK, 512))
        for core in range(NK):
            term = dot3(left, split(right_buf[y, core]), MM)
            totals[core] = term if totals[core] is None else totals[core] + term
    for core in range(NK):
        for b in range(2):
            out[2 * core + b] = totals[core][:, b * HD : (b + 1) * HD]


def project(where, rows, moved, weights):
    return pl.pallas_call(
        project_kernel,
        out_shape=jax.ShapeDtypeStruct((NX, NX * BLOCK, HD), jnp.float32),
        in_specs=[SMEM, HBM, ANY, ANY, ANY, HBM],
        out_specs=VMEM,
        scratch_shapes=[
            pltpu.VMEM((NY, NX, BLOCK, 512), jnp.float32),
            pltpu.VMEM((NY, NK, 512, 256), jnp.float32),
            pltpu.SemaphoreType.DMA((NY, NX + 1)),
        ],
        compiler_params=pltpu.CompilerParams(vmem_limit_bytes=32 << 20),
        cost_estimate=pl.CostEstimate(
            flops=6 * 256 * 2048 * 512, bytes_accessed=7 << 20, transcendentals=0
        ),
        name="project",
    )(where, rows, *moved, weights)


def attend_kernel(partial, low, up, *refs):
    pieces, (out, kv, scores, sem) = refs[:8], refs[8:]
    tiles = len(pieces)
    copies = [
        pltpu.make_async_copy(piece, kv.at[tile], sem.at[tile])
        for tile, piece in enumerate(pieces)
    ]
    for copy in copies:
        copy.start()
    width = NZ * BLOCK
    row = lax.broadcasted_iota(jnp.int32, (BLOCK, width), 0)
    col = lax.broadcasted_iota(jnp.int32, (BLOCK, width), 1)
    lower = row >= lax.rem(col, BLOCK)
    query = (partial[0] + partial[1]) + (partial[2] + partial[3])
    left = split(query * (math.log2(math.e) / math.sqrt(HD)))
    top = None
    for tile in range(tiles):
        copies[tile].wait()
        s = dot3(left, split(kv[tile, :, 0].reshape(width, HD)), MT)
        cols = slice(tile * width, (tile + 1) * width)
        bias = jnp.concatenate(
            [
                jnp.where(lower, low[b : b + 1, cols], up[b : b + 1, cols])
                for b in range(NX)
            ],
            axis=0,
        )
        s = s + bias
        scores[tile] = s
        top = s if top is None else jnp.maximum(top, s)
    top = jnp.max(top, axis=1, keepdims=True)
    total, summed = None, None
    for tile in range(tiles):
        weight = jnp.exp2(scores[tile] - top)
        term = dot3(split(weight), split(kv[tile, :, 1].reshape(width, HD)), MM)
        total = weight if total is None else total + weight
        summed = term if summed is None else summed + term
    attended = summed / jnp.sum(total, axis=1, keepdims=True)
    for z in range(NZ):
        out[z] = attended


def attend(partial, low, up, pieces):
    rows = NX * BLOCK
    return pl.pallas_call(
        attend_kernel,
        out_shape=jax.ShapeDtypeStruct((NZ, rows, HD), jnp.float32),
        in_specs=[VMEM] * 3 + [ANY] * 8,
        out_specs=VMEM,
        scratch_shapes=[
            pltpu.VMEM((8, NZ, 2, BLOCK, HD), jnp.float32),
            pltpu.VMEM((8, rows, NZ * BLOCK), jnp.float32),
            pltpu.SemaphoreType.DMA((8,)),
        ],
        compiler_params=pltpu.CompilerParams(vmem_limit_bytes=48 << 20),
        cost_estimate=pl.CostEstimate(
            flops=12 * 256 * 4096 * HD, bytes_accessed=6 << 20, transcendentals=256 * 4096
        ),
        name="attend",
    )(partial, low, up, *pieces)


def mix_kernel(heads, weights, out, buf, sem):
    steps = NZ // 2
    copies = []
    for step in range(steps):
        copies.append(
            pltpu.make_async_copy(
                weights.at[:, pl.ds(2 * step, 2)], buf.at[step], sem.at[step]
            )
        )
        copies[step].start()
    totals = [None, None]
    for step in range(steps):
        left = split(jnp.concatenate([heads[2 * step], heads[2 * step + 1]], axis=1))
        copies[step].wait()
        for core in range(NK):
            right = jnp.concatenate(
                [buf[step, :, z, core].reshape(HD, 512) for z in range(2)], axis=0
            )
            term = dot3(left, split(right), MM)
            totals[core] = term if totals[core] is None else totals[core] + term
    for core in range(NK):
        for x in range(NX):
            out[2 * x + core] = totals[core][x * BLOCK : (x + 1) * BLOCK]


def mix(heads, weights):
    return pl.pallas_call(
        mix_kernel,
        out_shape=jax.ShapeDtypeStruct((NX * NK, BLOCK, 512), jnp.float32),
        in_specs=[VMEM, HBM],
        out_specs=VMEM,
        scratch_shapes=[
            pltpu.VMEM((NZ // 2, 8, 2, NK, 16, 512), jnp.float32),
            pltpu.SemaphoreType.DMA((NZ // 2,)),
        ],
        compiler_params=pltpu.CompilerParams(vmem_limit_bytes=32 << 20),
        cost_estimate=pl.CostEstimate(
            flops=6 * 256 * 1024 * 1024, bytes_accessed=6 << 20, transcendentals=0
        ),
        name="mix",
    )(heads, weights)


def allowed_rows(
    head, key_block, query_block, vertical_blocks, vertical_count, slash_offsets, slash_count
):
    slots = jnp.arange(vertical_blocks.shape[1], dtype=jnp.int32)
    verticals = jnp.where(slots < vertical_count[head], vertical_blocks[head], -1)
    slashes = jnp.where(slots < slash_count[head], slash_offsets[head], -1)
    offset = query_block[:, None] - key_block[None, :]
    vert = jnp.any(key_block[:, None] == verticals[None, :], axis=1)[None, :]
    low_slash = jnp.any(offset[:, :, None] == slashes, axis=2)
    up_slash = jnp.any((offset - 1)[:, :, None] == slashes, axis=2)
    low = (offset >= 0) & (vert | low_slash)
    up = (offset >= 1) & (vert | up_slash)
    bias = jnp.where(jnp.stack([low, up]), 0.0, -jnp.inf)
    bias = jnp.repeat(bias, BLOCK, axis=2)
    return bias[0], bias[1]


CORES = [(0, 1), (1, 0)]


def shards(
    hidden_rows,
    query_weight,
    key_cache,
    value_cache,
    vertical_blocks,
    vertical_count,
    slash_offsets,
    slash_count,
    output_weight,
):
    x, y, z, k = (lax.axis_index(name) for name in ALL)
    where = jnp.stack([x, k]).astype(jnp.int32)
    weights = lax.all_gather(query_weight, ("y", "k"), axis=0)
    picked = pick(where, hidden_rows)
    hidden = [
        lax.ppermute(part, "x", [(i, (i + shift) % NX) for i in range(NX)])
        for shift, part in zip(range(1, NX), picked)
    ]
    quarters = [
        lax.dynamic_slice_in_dim(cache, y * BLOCK, BLOCK, 0)
        for cache in (key_cache, value_cache)
    ]
    sent = jnp.stack(
        [
            jnp.stack([quarter[:, (to // 2) * HD : (to // 2 + 1) * HD] for quarter in quarters])
            for to in range(NZ)
        ]
    )
    sent, _ = lax.optimization_barrier((sent, picked[0]))
    near = lax.all_to_all(sent, "z", 0, 0)
    pieces = []
    key_block = []
    for shift in range(NY):
        piece = near
        if shift:
            piece = lax.ppermute(near, "y", [(i, (i + shift) % NY) for i in range(NY)])
        pieces += [piece, lax.ppermute(piece, "k", CORES)]
        for core in (k, 1 - k):
            key_block.append(
                4 * (2 * jnp.arange(NZ, dtype=jnp.int32) + core) + (y - shift) % NY
            )
    rows = output_weight.reshape(2, NY, NK, 16, 512)
    kept = lax.dynamic_index_in_dim(rows, k, 2, keepdims=False)
    given = lax.dynamic_index_in_dim(rows, 1 - k, 2, keepdims=False)
    taken = lax.ppermute(given, "k", CORES)
    rows = jnp.where(k == 0, jnp.stack([kept, taken]), jnp.stack([taken, kept]))
    rows, near = lax.optimization_barrier((rows, near))
    rows = lax.all_to_all(rows.reshape(NX * NY, 16, 512), ("x", "y"), 0, 0)
    rows, hidden = lax.optimization_barrier((rows, hidden))
    rows = lax.all_to_all(rows.reshape(NZ, NK, 16, 512), "z", 0, 0)
    out_weight = lax.all_gather(rows, ("y", "k"), axis=0)
    hidden, pieces[2::2] = lax.optimization_barrier((hidden, pieces[2::2]))
    partial = project(where, hidden_rows, hidden, weights)
    partial = lax.all_to_all(partial, "x", 0, 0)
    low, up = allowed_rows(
        4 * z + x,
        jnp.concatenate(key_block),
        32 + 8 * jnp.arange(NX, dtype=jnp.int32) + 2 * y + k,
        vertical_blocks,
        vertical_count,
        slash_offsets,
        slash_count,
    )
    heads = attend(partial, low, up, pieces)
    heads = lax.all_to_all(heads, "z", 0, 0)
    mixed = mix(heads, out_weight)
    mixed = lax.all_to_all(mixed, ("x", "k"), 0, 0)
    return jnp.sum(mixed.reshape(NX, NK * BLOCK, 512), axis=0)


def solution(mesh):
    grid = Mesh(mesh.devices.reshape(NX, NY, NZ, NK), ALL)
    outer, ctx = ("x", "y"), ("z", "k")
    placed = (
        P(outer, None),
        P(outer, ctx),
        P(ctx, None),
        P(ctx, None),
        P(),
        P(),
        P(),
        P(),
        P(ctx, outer),
    )
    return jax.shard_map(
        shards, mesh=grid, in_specs=placed, out_specs=P(outer, ctx), check_vma=False
    )
```

```python
import functools
import math

import jax
import jax.numpy as jnp
from jax import lax
from jax.experimental import pallas as pl
from jax.experimental.pallas import tpu as pltpu
from jax.sharding import Mesh
from jax.sharding import PartitionSpec as P

HD = 128
BLOCK = 64
NX, NY, NZ, NK = 4, 4, 8, 2
ALL = ("x", "y", "z", "k")
VMEM = pl.BlockSpec(memory_space=pltpu.VMEM)
SMEM = pl.BlockSpec(memory_space=pltpu.SMEM)
ANY = pl.BlockSpec(memory_space=pl.ANY)
LIMIT = 60 << 20


def split(value):
    high = value.astype(jnp.bfloat16)
    low = (value - high.astype(jnp.float32)).astype(jnp.bfloat16)
    return high, low


def dot3(left, right, dims):
    (lh, ll), (rh, rl) = left, right
    one = functools.partial(
        lax.dot_general, dimension_numbers=dims, preferred_element_type=jnp.float32
    )
    return one(lh, rh) + (one(lh, rl) + one(ll, rh))


MM = (((1,), (0,)), ((), ()))
MT = (((1,), (1,)), ((), ()))


def pick_kernel(where, rows, *refs):
    outs, sem = refs[:3], refs[3]
    copies = []
    for shift in range(1, NX):
        cols = pl.multiple_of(lax.rem(where[0] + shift, NX) * 2048, 2048)
        part = rows.at[pl.ds(pl.multiple_of(where[2] * BLOCK, BLOCK), BLOCK), pl.ds(cols, 2048)]
        copies.append(pltpu.make_async_copy(part, outs[shift - 1], sem.at[shift - 1]))
    for copy in copies:
        copy.start()
    for copy in copies:
        copy.wait()


def pick(where, hidden_rows):
    return pl.pallas_call(
        pick_kernel,
        out_shape=[jax.ShapeDtypeStruct((BLOCK, 2048), jnp.float32)] * 3,
        in_specs=[SMEM, ANY],
        out_specs=[VMEM] * 3,
        scratch_shapes=[pltpu.SemaphoreType.DMA((3,))],
        compiler_params=pltpu.CompilerParams(vmem_limit_bytes=LIMIT),
        name="pick",
    )(where, hidden_rows)


def project_kernel(where, rows, *refs):
    moved, weights, outs = refs[:3], refs[3:11], refs[11:15]
    left_buf, right_buf, total_buf, sems = refs[15:]
    x, y, k = where[0], where[1], where[2]
    copies = []
    for turn in range(NY):
        slab = lax.rem(y + NY - turn, NY)
        cols = pl.multiple_of(slab * 512, 512)
        own = rows.at[
            pl.ds(pl.multiple_of(k * BLOCK, BLOCK), BLOCK),
            pl.ds(pl.multiple_of(x * 2048 + slab * 512, 512), 512),
        ]
        parts = [own] + [part.at[:, pl.ds(cols, 512)] for part in moved]
        group = [
            pltpu.make_async_copy(
                part, left_buf.at[turn, lax.rem(x + NX - shift, NX)], sems.at[turn, shift]
            )
            for shift, part in enumerate(parts)
        ]
        group += [
            pltpu.make_async_copy(
                weights[2 * turn + other], right_buf.at[turn, other], sems.at[turn, NX + other]
            )
            for other in range(NK)
        ]
        for copy in group:
            copy.start()
        copies.append(group)
    totals = [None, None]
    for turn in range(NY):
        for copy in copies[turn]:
            copy.wait()
        left = split(left_buf[turn].reshape(NX * BLOCK, 512))
        for other in range(NK):
            term = dot3(left, split(right_buf[turn, other]), MM)
            totals[other] = term if totals[other] is None else totals[other] + term
    for other in range(NK):
        core = k if other == 0 else 1 - k
        for b in range(2):
            total_buf[2 * core + b] = totals[other][:, b * HD : (b + 1) * HD]
    for shift in range(NX):
        outs[shift][...] = total_buf[lax.rem(x + shift, NX)]


def project(where, rows, moved, weights):
    return pl.pallas_call(
        project_kernel,
        out_shape=[jax.ShapeDtypeStruct((NX * BLOCK, HD), jnp.float32)] * NX,
        in_specs=[SMEM] + [ANY] * 12,
        out_specs=[VMEM] * NX,
        scratch_shapes=[
            pltpu.VMEM((NY, NX, BLOCK, 512), jnp.float32),
            pltpu.VMEM((NY, NK, 512, 256), jnp.float32),
            pltpu.VMEM((NX, NX * BLOCK, HD), jnp.float32),
            pltpu.SemaphoreType.DMA((NY, NX + NK)),
        ],
        compiler_params=pltpu.CompilerParams(vmem_limit_bytes=LIMIT),
        cost_estimate=pl.CostEstimate(
            flops=6 * 256 * 2048 * 512, bytes_accessed=7 << 20, transcendentals=0
        ),
        name="project",
    )(where, rows, *moved, *weights)


def attend_kernel(first, second, third, fourth, low, up, gathered, out, kv, scores, sem):
    tiles = gathered.shape[0]
    copies = [
        pltpu.make_async_copy(gathered.at[tile], kv.at[tile], sem.at[tile])
        for tile in range(tiles)
    ]
    for copy in copies:
        copy.start()
    width = NZ * BLOCK
    row = lax.broadcasted_iota(jnp.int32, (BLOCK, width), 0)
    col = lax.broadcasted_iota(jnp.int32, (BLOCK, width), 1)
    lower = row >= lax.rem(col, BLOCK)
    query = (first[...] + second[...]) + (third[...] + fourth[...])
    left = split(query * (math.log2(math.e) / math.sqrt(HD)))
    top = None
    for tile in range(tiles):
        copies[tile].wait()
        s = dot3(left, split(kv[tile, :, 0].reshape(width, HD)), MT)
        cols = slice(tile * width, (tile + 1) * width)
        bias = jnp.concatenate(
            [
                jnp.where(lower, low[b : b + 1, cols], up[b : b + 1, cols])
                for b in range(NX)
            ],
            axis=0,
        )
        s = s + bias
        scores[tile] = s
        top = s if top is None else jnp.maximum(top, s)
    top = jnp.max(top, axis=1, keepdims=True)
    total, summed = None, None
    for tile in range(tiles):
        weight = jnp.exp2(scores[tile] - top)
        term = dot3(split(weight), split(kv[tile, :, 1].reshape(width, HD)), MM)
        total = weight if total is None else total + weight
        summed = term if summed is None else summed + term
    attended = summed / jnp.sum(total, axis=1, keepdims=True)
    for z in range(NZ):
        out[z] = attended


def attend(partial, low, up, gathered):
    rows = NX * BLOCK
    return pl.pallas_call(
        attend_kernel,
        out_shape=jax.ShapeDtypeStruct((NZ, rows, HD), jnp.float32),
        in_specs=[VMEM] * 6 + [ANY],
        out_specs=VMEM,
        scratch_shapes=[
            pltpu.VMEM((8, NZ, 2, BLOCK, HD), jnp.float32),
            pltpu.VMEM((8, rows, NZ * BLOCK), jnp.float32),
            pltpu.SemaphoreType.DMA((8,)),
        ],
        compiler_params=pltpu.CompilerParams(vmem_limit_bytes=LIMIT),
        cost_estimate=pl.CostEstimate(
            flops=12 * 256 * 4096 * HD, bytes_accessed=6 << 20, transcendentals=256 * 4096
        ),
        name="attend",
    )(*partial, low, up, gathered)


def mix_kernel(heads, weights, out, buf, sem):
    steps = NZ // 2
    copies = []
    for step in range(steps):
        copies.append(
            pltpu.make_async_copy(
                weights.at[:, pl.ds(2 * step, 2)], buf.at[step], sem.at[step]
            )
        )
        copies[step].start()
    totals = [None, None]
    for step in range(steps):
        left = split(jnp.concatenate([heads[2 * step], heads[2 * step + 1]], axis=1))
        copies[step].wait()
        for core in range(NK):
            right = jnp.concatenate(
                [buf[step, :, z, core].reshape(HD, 512) for z in range(2)], axis=0
            )
            term = dot3(left, split(right), MM)
            totals[core] = term if totals[core] is None else totals[core] + term
    for core in range(NK):
        for x in range(NX):
            out[2 * x + core] = totals[core][x * BLOCK : (x + 1) * BLOCK]


def mix(heads, weights):
    return pl.pallas_call(
        mix_kernel,
        out_shape=jax.ShapeDtypeStruct((NX * NK, BLOCK, 512), jnp.float32),
        in_specs=[VMEM, ANY],
        out_specs=VMEM,
        scratch_shapes=[
            pltpu.VMEM((NZ // 2, 8, 2, NK, 16, 512), jnp.float32),
            pltpu.SemaphoreType.DMA((NZ // 2,)),
        ],
        compiler_params=pltpu.CompilerParams(vmem_limit_bytes=LIMIT),
        cost_estimate=pl.CostEstimate(
            flops=6 * 256 * 1024 * 1024, bytes_accessed=6 << 20, transcendentals=0
        ),
        name="mix",
    )(heads, weights)


def allowed_rows(
    head, key_block, query_block, vertical_blocks, vertical_count, slash_offsets, slash_count
):
    slots = jnp.arange(vertical_blocks.shape[1], dtype=jnp.int32)
    verticals = jnp.where(slots < vertical_count[head], vertical_blocks[head], -1)
    slashes = jnp.where(slots < slash_count[head], slash_offsets[head], -1)
    offset = query_block[:, None] - key_block[None, :]
    vert = jnp.any(key_block[:, None] == verticals[None, :], axis=1)[None, :]
    low_slash = jnp.any(offset[:, :, None] == slashes, axis=2)
    up_slash = jnp.any((offset - 1)[:, :, None] == slashes, axis=2)
    low = (offset >= 0) & (vert | low_slash)
    up = (offset >= 1) & (vert | up_slash)
    bias = jnp.where(jnp.stack([low, up]), 0.0, -jnp.inf)
    bias = jnp.repeat(bias, BLOCK, axis=2)
    return bias[0], bias[1]


CORES = [(0, 1), (1, 0)]


def along(axis, value, shift):
    count = lax.axis_size(axis)
    return lax.ppermute(value, axis, [(i, (i + shift) % count) for i in range(count)])


def shards(
    hidden_rows,
    query_weight,
    key_cache,
    value_cache,
    vertical_blocks,
    vertical_count,
    slash_offsets,
    slash_count,
    output_weight,
):
    x, y, z, k = (lax.axis_index(name) for name in ALL)
    where = jnp.stack([x, y, k]).astype(jnp.int32)
    picked = pick(where, hidden_rows)
    hidden = [along("x", part, shift) for shift, part in enumerate(picked, 1)]
    weights = []
    for shift in range(NY):
        piece = along("y", query_weight, shift) if shift else query_weight
        weights += [piece, lax.ppermute(piece, "k", CORES)]
    quarters = [
        lax.dynamic_slice_in_dim(cache, y * BLOCK, BLOCK, 0)
        for cache in (key_cache, value_cache)
    ]
    sent = jnp.stack(
        [
            jnp.stack([quarter[:, (to // 2) * HD : (to // 2 + 1) * HD] for quarter in quarters])
            for to in range(NZ)
        ]
    )
    near = lax.all_to_all(sent, "z", 0, 0)
    kv = lax.all_gather(near, ("y", "k"), axis=0)
    rows = output_weight.reshape(2, NY, NK, 16, 512)
    kept = lax.dynamic_index_in_dim(rows, k, 2, keepdims=False)
    given = lax.dynamic_index_in_dim(rows, 1 - k, 2, keepdims=False)
    taken = lax.ppermute(given, "k", CORES)
    rows = jnp.where(k == 0, jnp.stack([kept, taken]), jnp.stack([taken, kept]))
    rows, near = lax.optimization_barrier((rows, near))
    rows = lax.all_to_all(rows.reshape(NX * NY, 16, 512), ("x", "y"), 0, 0)
    rows, hidden, weights = lax.optimization_barrier((rows, hidden, weights))
    rows = lax.all_to_all(rows.reshape(NZ, NK, 16, 512), "z", 0, 0)
    out_weight = lax.all_gather(rows, ("y", "k"), axis=0)
    partial = project(where, hidden_rows, hidden, weights)
    partial = [partial[0]] + [along("x", partial[s], s) for s in range(1, NX)]
    key_block = jnp.arange(NY, dtype=jnp.int32)[:, None, None]
    key_block = key_block + 4 * jnp.arange(NK, dtype=jnp.int32)[None, :, None]
    key_block = key_block + 8 * jnp.arange(NZ, dtype=jnp.int32)[None, None, :]
    low, up = allowed_rows(
        4 * z + x,
        key_block.reshape(-1),
        32 + 8 * jnp.arange(NX, dtype=jnp.int32) + 2 * y + k,
        vertical_blocks,
        vertical_count,
        slash_offsets,
        slash_count,
    )
    heads = attend(partial, low, up, kv)
    heads = lax.all_to_all(heads, "z", 0, 0)
    mixed = mix(heads, out_weight)
    mixed = lax.all_to_all(mixed, ("x", "k"), 0, 0)
    return jnp.sum(mixed.reshape(NX, NK * BLOCK, 512), axis=0)


def solution(mesh):
    grid = Mesh(mesh.devices.reshape(NX, NY, NZ, NK), ALL)
    outer, ctx = ("x", "y"), ("z", "k")
    placed = (
        P(outer, None),
        P(outer, ctx),
        P(ctx, None),
        P(ctx, None),
        P(),
        P(),
        P(),
        P(),
        P(ctx, outer),
    )
    return jax.shard_map(
        shards, mesh=grid, in_specs=placed, out_specs=P(outer, ctx), check_vma=False
    )
```

```python
import functools
import math

import jax
import jax.numpy as jnp
from jax import lax
from jax.experimental import pallas as pl
from jax.experimental.pallas import tpu as pltpu
from jax.sharding import Mesh
from jax.sharding import PartitionSpec as P

HD = 128
BLOCK = 64
NX, NY, NZ, NK = 4, 4, 8, 2
ALL = ("x", "y", "z", "k")
VMEM = pl.BlockSpec(memory_space=pltpu.VMEM)
SMEM = pl.BlockSpec(memory_space=pltpu.SMEM)
ANY = pl.BlockSpec(memory_space=pl.ANY)
LIMIT = 60 << 20


def split(value):
    high = value.astype(jnp.bfloat16)
    low = (value - high.astype(jnp.float32)).astype(jnp.bfloat16)
    return high, low


def dot3(left, right, dims):
    (lh, ll), (rh, rl) = left, right
    one = functools.partial(
        lax.dot_general, dimension_numbers=dims, preferred_element_type=jnp.float32
    )
    return one(lh, rh) + (one(lh, rl) + one(ll, rh))


MM = (((1,), (0,)), ((), ()))
MT = (((1,), (1,)), ((), ()))


def pick_kernel(where, rows, *refs):
    outs, sem = refs[:3], refs[3]
    copies = []
    for shift in range(1, NX):
        cols = pl.multiple_of(lax.rem(where[0] + shift, NX) * 2048, 2048)
        part = rows.at[pl.ds(pl.multiple_of(where[1] * BLOCK, BLOCK), BLOCK), pl.ds(cols, 2048)]
        copies.append(pltpu.make_async_copy(part, outs[shift - 1], sem.at[shift - 1]))
    for copy in copies:
        copy.start()
    for copy in copies:
        copy.wait()


def pick(where, hidden_rows):
    return pl.pallas_call(
        pick_kernel,
        out_shape=[jax.ShapeDtypeStruct((BLOCK, 2048), jnp.float32)] * 3,
        in_specs=[SMEM, ANY],
        out_specs=[VMEM] * 3,
        scratch_shapes=[pltpu.SemaphoreType.DMA((3,))],
        compiler_params=pltpu.CompilerParams(vmem_limit_bytes=LIMIT),
        name="pick",
    )(where, hidden_rows)


def project_kernel(where, rows, first, second, third, weights, *refs):
    outs, (left_buf, right_buf, total_buf, sems) = refs[:NX], refs[NX:]
    x, k = where[0], where[1]
    copies = []
    for y in range(NY):
        own = rows.at[
            pl.ds(pl.multiple_of(k * BLOCK, BLOCK), BLOCK),
            pl.ds(pl.multiple_of(x * 2048 + y * 512, 512), 512),
        ]
        parts = [own] + [part.at[:, pl.ds(y * 512, 512)] for part in (first, second, third)]
        group = [
            pltpu.make_async_copy(
                part, left_buf.at[y, lax.rem(x + NX - shift, NX)], sems.at[y, shift]
            )
            for shift, part in enumerate(parts)
        ]
        group.append(
            pltpu.make_async_copy(weights.at[pl.ds(2 * y, 2)], right_buf.at[y], sems.at[y, NX])
        )
        for copy in group:
            copy.start()
        copies.append(group)
    totals = [None, None]
    for y in range(NY):
        for copy in copies[y]:
            copy.wait()
        left = split(left_buf[y].reshape(NX * BLOCK, 512))
        for core in range(NK):
            term = dot3(left, split(right_buf[y, core]), MM)
            totals[core] = term if totals[core] is None else totals[core] + term
    for core in range(NK):
        for b in range(2):
            total_buf[2 * core + b] = totals[core][:, b * HD : (b + 1) * HD]
    for shift in range(NX):
        outs[shift][...] = total_buf[lax.rem(x + shift, NX)]


def project(where, rows, moved, weights):
    return pl.pallas_call(
        project_kernel,
        out_shape=[jax.ShapeDtypeStruct((NX * BLOCK, HD), jnp.float32)] * NX,
        in_specs=[SMEM] + [ANY] * 5,
        out_specs=[VMEM] * NX,
        scratch_shapes=[
            pltpu.VMEM((NY, NX, BLOCK, 512), jnp.float32),
            pltpu.VMEM((NY, NK, 512, 256), jnp.float32),
            pltpu.VMEM((NX, NX * BLOCK, HD), jnp.float32),
            pltpu.SemaphoreType.DMA((NY, NX + 1)),
        ],
        compiler_params=pltpu.CompilerParams(vmem_limit_bytes=LIMIT),
        cost_estimate=pl.CostEstimate(
            flops=6 * 256 * 2048 * 512, bytes_accessed=7 << 20, transcendentals=0
        ),
        name="project",
    )(where, rows, *moved, weights)


def attend_kernel(first, second, third, fourth, low, up, *refs):
    pieces, (out, kv, scores, sem) = refs[:8], refs[8:]
    tiles = len(pieces)
    copies = [
        pltpu.make_async_copy(piece, kv.at[tile], sem.at[tile])
        for tile, piece in enumerate(pieces)
    ]
    for copy in copies:
        copy.start()
    width = NZ * BLOCK
    row = lax.broadcasted_iota(jnp.int32, (BLOCK, width), 0)
    col = lax.broadcasted_iota(jnp.int32, (BLOCK, width), 1)
    lower = row >= lax.rem(col, BLOCK)
    query = (first[...] + second[...]) + (third[...] + fourth[...])
    left = split(query * (math.log2(math.e) / math.sqrt(HD)))
    top = None
    for tile in range(tiles):
        copies[tile].wait()
        s = dot3(left, split(kv[tile, :, 0].reshape(width, HD)), MT)
        cols = slice(tile * width, (tile + 1) * width)
        bias = jnp.concatenate(
            [
                jnp.where(lower, low[b : b + 1, cols], up[b : b + 1, cols])
                for b in range(NX)
            ],
            axis=0,
        )
        s = s + bias
        scores[tile] = s
        top = s if top is None else jnp.maximum(top, s)
    top = jnp.max(top, axis=1, keepdims=True)
    total, summed = None, None
    for tile in range(tiles):
        weight = jnp.exp2(scores[tile] - top)
        term = dot3(split(weight), split(kv[tile, :, 1].reshape(width, HD)), MM)
        total = weight if total is None else total + weight
        summed = term if summed is None else summed + term
    attended = summed / jnp.sum(total, axis=1, keepdims=True)
    for z in range(NZ):
        out[z] = attended


def attend(partial, low, up, pieces):
    rows = NX * BLOCK
    return pl.pallas_call(
        attend_kernel,
        out_shape=jax.ShapeDtypeStruct((NZ, rows, HD), jnp.float32),
        in_specs=[VMEM] * 6 + [ANY] * 8,
        out_specs=VMEM,
        scratch_shapes=[
            pltpu.VMEM((8, NZ, 2, BLOCK, HD), jnp.float32),
            pltpu.VMEM((8, rows, NZ * BLOCK), jnp.float32),
            pltpu.SemaphoreType.DMA((8,)),
        ],
        compiler_params=pltpu.CompilerParams(vmem_limit_bytes=LIMIT),
        cost_estimate=pl.CostEstimate(
            flops=12 * 256 * 4096 * HD, bytes_accessed=6 << 20, transcendentals=256 * 4096
        ),
        name="attend",
    )(*partial, low, up, *pieces)


def mix_kernel(where, heads, weights, *refs):
    outs, (total_buf, buf, sem) = refs[:NX], refs[NX:]
    steps = NZ // 2
    copies = []
    for step in range(steps):
        copies.append(
            pltpu.make_async_copy(
                weights.at[:, pl.ds(2 * step, 2)], buf.at[step], sem.at[step]
            )
        )
        copies[step].start()
    totals = [None, None]
    for step in range(steps):
        left = split(jnp.concatenate([heads[2 * step], heads[2 * step + 1]], axis=1))
        copies[step].wait()
        for core in range(NK):
            right = jnp.concatenate(
                [buf[step, :, z, core].reshape(HD, 512) for z in range(2)], axis=0
            )
            term = dot3(left, split(right), MM)
            totals[core] = term if totals[core] is None else totals[core] + term
    for core in range(NK):
        for x in range(NX):
            total_buf[x, core] = totals[core][x * BLOCK : (x + 1) * BLOCK]
    for shift in range(NX):
        outs[shift][...] = total_buf[lax.rem(where[0] + shift, NX)]


def mix(where, heads, weights):
    return pl.pallas_call(
        mix_kernel,
        out_shape=[jax.ShapeDtypeStruct((NK, BLOCK, 512), jnp.float32)] * NX,
        in_specs=[SMEM, VMEM, ANY],
        out_specs=[VMEM] * NX,
        scratch_shapes=[
            pltpu.VMEM((NX, NK, BLOCK, 512), jnp.float32),
            pltpu.VMEM((NZ // 2, 8, 2, NK, 16, 512), jnp.float32),
            pltpu.SemaphoreType.DMA((NZ // 2,)),
        ],
        compiler_params=pltpu.CompilerParams(vmem_limit_bytes=LIMIT),
        cost_estimate=pl.CostEstimate(
            flops=6 * 256 * 1024 * 1024, bytes_accessed=6 << 20, transcendentals=0
        ),
        name="mix",
    )(where, heads, weights)


def allowed_rows(
    head, key_block, query_block, vertical_blocks, vertical_count, slash_offsets, slash_count
):
    slots = jnp.arange(vertical_blocks.shape[1], dtype=jnp.int32)
    verticals = jnp.where(slots < vertical_count[head], vertical_blocks[head], -1)
    slashes = jnp.where(slots < slash_count[head], slash_offsets[head], -1)
    offset = query_block[:, None] - key_block[None, :]
    vert = jnp.any(key_block[:, None] == verticals[None, :], axis=1)[None, :]
    low_slash = jnp.any(offset[:, :, None] == slashes, axis=2)
    up_slash = jnp.any((offset - 1)[:, :, None] == slashes, axis=2)
    low = (offset >= 0) & (vert | low_slash)
    up = (offset >= 1) & (vert | up_slash)
    bias = jnp.where(jnp.stack([low, up]), 0.0, -jnp.inf)
    bias = jnp.repeat(bias, BLOCK, axis=2)
    return bias[0], bias[1]


CORES = [(0, 1), (1, 0)]


def along(axis, value, shift):
    count = lax.axis_size(axis)
    return lax.ppermute(value, axis, [(i, (i + shift) % count) for i in range(count)])


def shards(
    hidden_rows,
    query_weight,
    key_cache,
    value_cache,
    vertical_blocks,
    vertical_count,
    slash_offsets,
    slash_count,
    output_weight,
):
    x, y, z, k = (lax.axis_index(name) for name in ALL)
    where = jnp.stack([x, k]).astype(jnp.int32)
    weights = lax.all_gather(query_weight, ("y", "k"), axis=0)
    picked = pick(where, hidden_rows)
    hidden = [along("x", part, shift) for shift, part in enumerate(picked, 1)]
    quarters = [
        lax.dynamic_slice_in_dim(cache, y * BLOCK, BLOCK, 0)
        for cache in (key_cache, value_cache)
    ]
    sent = jnp.stack(
        [
            jnp.stack([quarter[:, (to // 2) * HD : (to // 2 + 1) * HD] for quarter in quarters])
            for to in range(NZ)
        ]
    )
    sent, _ = lax.optimization_barrier((sent, picked[0]))
    near = lax.all_to_all(sent, "z", 0, 0)
    rows = output_weight.reshape(2, NY, NK, 16, 512)
    kept = lax.dynamic_index_in_dim(rows, k, 2, keepdims=False)
    given = lax.dynamic_index_in_dim(rows, 1 - k, 2, keepdims=False)
    taken = lax.ppermute(given, "k", CORES)
    rows = jnp.where(k == 0, jnp.stack([kept, taken]), jnp.stack([taken, kept]))
    rows, near = lax.optimization_barrier((rows, near))
    quarters = [near] + [along("y", near, shift) for shift in range(1, NY)]
    rows = lax.all_to_all(rows.reshape(NX * NY, 16, 512), ("x", "y"), 0, 0)
    rows, hidden, quarters = lax.optimization_barrier((rows, hidden, quarters))
    rows = lax.all_to_all(rows.reshape(NZ, NK, 16, 512), "z", 0, 0)
    out_weight = lax.all_gather(rows, ("y", "k"), axis=0)
    pieces = []
    for piece in quarters:
        pieces += [piece, lax.ppermute(piece, "k", CORES)]
    partial = project(where, hidden_rows, hidden, weights)
    partial = [partial[0]] + [along("x", partial[s], s) for s in range(1, NX)]
    key_block = (y - jnp.arange(NY, dtype=jnp.int32))[:, None, None] % NY
    key_block = key_block + 4 * jnp.stack([k, 1 - k])[None, :, None]
    key_block = key_block + 8 * jnp.arange(NZ, dtype=jnp.int32)[None, None, :]
    low, up = allowed_rows(
        4 * z + x,
        key_block.reshape(-1),
        32 + 8 * jnp.arange(NX, dtype=jnp.int32) + 2 * y + k,
        vertical_blocks,
        vertical_count,
        slash_offsets,
        slash_count,
    )
    heads = attend(partial, low, up, pieces)
    heads = lax.all_to_all(heads, "z", 0, 0)
    mixed = mix(where, heads, out_weight)
    mixed = [mixed[0]] + [along("x", mixed[s], s) for s in range(1, NX)]
    mixed = (mixed[0] + mixed[1]) + (mixed[2] + mixed[3])
    own = lax.dynamic_index_in_dim(mixed, k, 0, keepdims=False)
    other = lax.dynamic_index_in_dim(mixed, 1 - k, 0, keepdims=False)
    other = lax.ppermute(other, "k", CORES)
    return jnp.concatenate([jnp.where(k == 0, own, other), jnp.where(k == 0, other, own)])


def solution(mesh):
    grid = Mesh(mesh.devices.reshape(NX, NY, NZ, NK), ALL)
    outer, ctx = ("x", "y"), ("z", "k")
    placed = (
        P(outer, None),
        P(outer, ctx),
        P(ctx, None),
        P(ctx, None),
        P(),
        P(),
        P(),
        P(),
        P(ctx, outer),
    )
    return jax.shard_map(
        shards, mesh=grid, in_specs=placed, out_specs=P(outer, ctx), check_vma=False
    )
```

```python
import math

import jax
import jax.numpy as jnp
from jax import lax
from jax.experimental import pallas as pl
from jax.experimental.pallas import tpu as pltpu
from jax.sharding import Mesh
from jax.sharding import PartitionSpec as P

HD = 128
BLOCK = 64
NX, NY, NZ, NK = 4, 4, 8, 2
ALL = ("x", "y", "z", "k")
VMEM = pl.BlockSpec(memory_space=pltpu.VMEM)
SMEM = pl.BlockSpec(memory_space=pltpu.SMEM)
ANY = pl.BlockSpec(memory_space=pl.ANY)
LIMIT = 60 << 20


def split(value):
    high = value.astype(jnp.bfloat16)
    low = (value - high.astype(jnp.float32)).astype(jnp.bfloat16)
    return high, low


def dot(left, right, dims):
    return lax.dot_general(left, right, dims, preferred_element_type=jnp.float32)


def dot3(left, right, dims):
    (lh, ll), (rh, rl) = left, right
    return dot(lh, rh, dims) + (dot(lh, rl, dims) + dot(ll, rh, dims))


MM = (((1,), (0,)), ((), ()))
MT = (((1,), (1,)), ((), ()))


def pick_kernel(where, rows, keys, values, *refs):
    outs, sent, sem, kv_sem = refs[:3], refs[3], refs[4], refs[5]
    x, y, k = where[0], where[1], where[2]
    copies = []
    for to in range(NZ):
        cols = pl.ds((to // 2) * HD, HD)
        for index, cache in enumerate((keys, values)):
            part = cache.at[pl.ds(pl.multiple_of(y * BLOCK, BLOCK), BLOCK), cols]
            copies.append(
                pltpu.make_async_copy(part, sent.at[to, index], kv_sem.at[2 * to + index])
            )
    for shift in range(1, NX):
        cols = pl.multiple_of(lax.rem(x + shift, NX) * 2048, 2048)
        part = rows.at[pl.ds(pl.multiple_of(k * BLOCK, BLOCK), BLOCK), pl.ds(cols, 2048)]
        copies.append(pltpu.make_async_copy(part, outs[shift - 1], sem.at[shift - 1]))
    for copy in copies:
        copy.start()
    for copy in copies:
        copy.wait()


def pick(where, hidden_rows, key_cache, value_cache):
    return pl.pallas_call(
        pick_kernel,
        out_shape=[jax.ShapeDtypeStruct((BLOCK, 2048), jnp.float32)] * 3
        + [jax.ShapeDtypeStruct((NZ, 2, BLOCK, HD), jnp.float32)],
        in_specs=[SMEM, ANY, ANY, ANY],
        out_specs=[VMEM] * 4,
        scratch_shapes=[pltpu.SemaphoreType.DMA((3,)), pltpu.SemaphoreType.DMA((2 * NZ,))],
        compiler_params=pltpu.CompilerParams(vmem_limit_bytes=LIMIT),
        name="pick",
    )(where, hidden_rows, key_cache, value_cache)


def project_kernel(where, rows, first, second, third, weights, *refs):
    outs, (left_buf, right_buf, total_buf, sems) = refs[:NX], refs[NX:]
    x, k = where[0], where[2]
    copies = []
    for y in range(NY):
        own = rows.at[
            pl.ds(pl.multiple_of(k * BLOCK, BLOCK), BLOCK),
            pl.ds(pl.multiple_of(x * 2048 + y * 512, 512), 512),
        ]
        parts = [own] + [part.at[:, pl.ds(y * 512, 512)] for part in (first, second, third)]
        group = [
            pltpu.make_async_copy(
                part, left_buf.at[y, lax.rem(x + NX - shift, NX)], sems.at[y, shift]
            )
            for shift, part in enumerate(parts)
        ]
        group.append(
            pltpu.make_async_copy(weights.at[pl.ds(2 * y, 2)], right_buf.at[y], sems.at[y, NX])
        )
        for copy in group:
            copy.start()
        copies.append(group)
    totals = [None, None]
    for y in range(NY):
        for copy in copies[y]:
            copy.wait()
        left = split(left_buf[y].reshape(NX * BLOCK, 512))
        for core in range(NK):
            term = dot3(left, split(right_buf[y, core]), MM)
            totals[core] = term if totals[core] is None else totals[core] + term
    for core in range(NK):
        for b in range(2):
            total_buf[2 * core + b] = totals[core][:, b * HD : (b + 1) * HD]
    for shift in range(NX):
        outs[shift][...] = total_buf[lax.rem(x + shift, NX)]


def project(where, rows, moved, weights):
    return pl.pallas_call(
        project_kernel,
        out_shape=[jax.ShapeDtypeStruct((NX * BLOCK, HD), jnp.float32)] * NX,
        in_specs=[SMEM] + [ANY] * 5,
        out_specs=[VMEM] * NX,
        scratch_shapes=[
            pltpu.VMEM((NY, NX, BLOCK, 512), jnp.float32),
            pltpu.VMEM((NY, NK, 512, 256), jnp.float32),
            pltpu.VMEM((NX, NX * BLOCK, HD), jnp.float32),
            pltpu.SemaphoreType.DMA((NY, NX + 1)),
        ],
        compiler_params=pltpu.CompilerParams(vmem_limit_bytes=LIMIT),
        cost_estimate=pl.CostEstimate(
            flops=6 * 256 * 2048 * 512, bytes_accessed=7 << 20, transcendentals=0
        ),
        name="project",
    )(where, rows, *moved, weights)


def attend_kernel(first, second, third, fourth, low, up, gathered, out, kv, scores, sem):
    tiles = gathered.shape[0]
    copies = [
        pltpu.make_async_copy(gathered.at[tile], kv.at[tile], sem.at[tile])
        for tile in range(tiles)
    ]
    for copy in copies:
        copy.start()
    width = NZ * BLOCK
    row = lax.broadcasted_iota(jnp.int32, (BLOCK, width), 0)
    col = lax.broadcasted_iota(jnp.int32, (BLOCK, width), 1)
    lower = row >= lax.rem(col, BLOCK)
    query = (first[...] + second[...]) + (third[...] + fourth[...])
    high, low_part = split(query * (math.log2(math.e) / math.sqrt(HD)))
    both = jnp.concatenate([high, low_part], axis=1)
    top = None
    for tile in range(tiles):
        copies[tile].wait()
        key_high, key_low = split(kv[tile, :, 0].reshape(width, HD))
        s = dot(both, jnp.concatenate([key_high, key_high], axis=1), MT)
        s = s + dot(high, key_low, MT)
        cols = slice(tile * width, (tile + 1) * width)
        bias = jnp.concatenate(
            [
                jnp.where(lower, low[b : b + 1, cols], up[b : b + 1, cols])
                for b in range(NX)
            ],
            axis=0,
        )
        s = s + bias
        scores[tile] = s
        top = s if top is None else jnp.maximum(top, s)
    top = jnp.max(top, axis=1, keepdims=True)
    total, summed = None, None
    for tile in range(tiles):
        weight = jnp.exp2(scores[tile] - top)
        weight_high, weight_low = split(weight)
        value_high, value_low = split(kv[tile, :, 1].reshape(width, HD))
        term = dot(weight_high, jnp.concatenate([value_high, value_low], axis=1), MM)
        term = term[:, :HD] + (term[:, HD:] + dot(weight_low, value_high, MM))
        total = weight if total is None else total + weight
        summed = term if summed is None else summed + term
    attended = summed / jnp.sum(total, axis=1, keepdims=True)
    for z in range(NZ):
        out[z] = attended


def attend(partial, low, up, gathered):
    rows = NX * BLOCK
    return pl.pallas_call(
        attend_kernel,
        out_shape=jax.ShapeDtypeStruct((NZ, rows, HD), jnp.float32),
        in_specs=[VMEM] * 6 + [ANY],
        out_specs=VMEM,
        scratch_shapes=[
            pltpu.VMEM((8, NZ, 2, BLOCK, HD), jnp.float32),
            pltpu.VMEM((8, rows, NZ * BLOCK), jnp.float32),
            pltpu.SemaphoreType.DMA((8,)),
        ],
        compiler_params=pltpu.CompilerParams(vmem_limit_bytes=LIMIT),
        cost_estimate=pl.CostEstimate(
            flops=12 * 256 * 4096 * HD, bytes_accessed=6 << 20, transcendentals=256 * 4096
        ),
        name="attend",
    )(*partial, low, up, gathered)


def mix_kernel(where, heads, weights, *refs):
    outs, (total_buf, buf, sem) = refs[:NX], refs[NX:]
    steps = NZ // 2
    copies = []
    for step in range(steps):
        copies.append(
            pltpu.make_async_copy(
                weights.at[:, pl.ds(2 * step, 2)], buf.at[step], sem.at[step]
            )
        )
        copies[step].start()
    totals = [None, None]
    for step in range(steps):
        left = split(jnp.concatenate([heads[2 * step], heads[2 * step + 1]], axis=1))
        copies[step].wait()
        for core in range(NK):
            right = jnp.concatenate(
                [buf[step, :, z, core].reshape(HD, 512) for z in range(2)], axis=0
            )
            term = dot3(left, split(right), MM)
            totals[core] = term if totals[core] is None else totals[core] + term
    for core in range(NK):
        for x in range(NX):
            total_buf[x, core] = totals[core][x * BLOCK : (x + 1) * BLOCK]
    for shift in range(NX):
        outs[shift][...] = total_buf[lax.rem(where[0] + shift, NX)]


def mix(where, heads, weights):
    return pl.pallas_call(
        mix_kernel,
        out_shape=[jax.ShapeDtypeStruct((NK, BLOCK, 512), jnp.float32)] * NX,
        in_specs=[SMEM, VMEM, ANY],
        out_specs=[VMEM] * NX,
        scratch_shapes=[
            pltpu.VMEM((NX, NK, BLOCK, 512), jnp.float32),
            pltpu.VMEM((NZ // 2, 8, 2, NK, 16, 512), jnp.float32),
            pltpu.SemaphoreType.DMA((NZ // 2,)),
        ],
        compiler_params=pltpu.CompilerParams(vmem_limit_bytes=LIMIT),
        cost_estimate=pl.CostEstimate(
            flops=6 * 256 * 1024 * 1024, bytes_accessed=6 << 20, transcendentals=0
        ),
        name="mix",
    )(where, heads, weights)


def allowed_rows(
    head, key_block, query_block, vertical_blocks, vertical_count, slash_offsets, slash_count
):
    slots = jnp.arange(vertical_blocks.shape[1], dtype=jnp.int32)
    verticals = jnp.where(slots < vertical_count[head], vertical_blocks[head], -1)
    slashes = jnp.where(slots < slash_count[head], slash_offsets[head], -1)
    offset = query_block[:, None] - key_block[None, :]
    vert = jnp.any(key_block[:, None] == verticals[None, :], axis=1)[None, :]
    low_slash = jnp.any(offset[:, :, None] == slashes, axis=2)
    up_slash = jnp.any((offset - 1)[:, :, None] == slashes, axis=2)
    low = (offset >= 0) & (vert | low_slash)
    up = (offset >= 1) & (vert | up_slash)
    bias = jnp.where(jnp.stack([low, up]), 0.0, -jnp.inf)
    bias = jnp.repeat(bias, BLOCK, axis=2)
    return bias[0], bias[1]


CORES = [(0, 1), (1, 0)]


def along(axis, value, shift):
    count = lax.axis_size(axis)
    return lax.ppermute(value, axis, [(i, (i + shift) % count) for i in range(count)])


def shards(
    hidden_rows,
    query_weight,
    key_cache,
    value_cache,
    vertical_blocks,
    vertical_count,
    slash_offsets,
    slash_count,
    output_weight,
):
    x, y, z, k = (lax.axis_index(name) for name in ALL)
    where = jnp.stack([x, y, k]).astype(jnp.int32)
    weights = lax.all_gather(query_weight, ("y", "k"), axis=0)
    *picked, sent = pick(where, hidden_rows, key_cache, value_cache)
    hidden = [along("x", piece, shift) for shift, piece in enumerate(picked, 1)]
    near = lax.all_to_all(sent, "z", 0, 0)
    rows = output_weight.reshape(2, NY, NK, 16, 512)
    kept = lax.dynamic_index_in_dim(rows, k, 2, keepdims=False)
    given = lax.dynamic_index_in_dim(rows, 1 - k, 2, keepdims=False)
    taken = lax.ppermute(given, "k", CORES)
    rows = jnp.where(k == 0, jnp.stack([kept, taken]), jnp.stack([taken, kept]))
    rows, near = lax.optimization_barrier((rows, near))
    rows = lax.all_to_all(rows.reshape(NX * NY, 16, 512), ("x", "y"), 0, 0)
    rows = lax.all_to_all(rows.reshape(NZ, NK, 16, 512), "z", 0, 0)
    kv = lax.all_gather(near, ("y", "k"), axis=0)
    out_weight = lax.all_gather(rows, ("y", "k"), axis=0)
    partial = project(where, hidden_rows, hidden, weights)
    partial = [partial[0]] + [along("x", partial[s], s) for s in range(1, NX)]
    key_block = jnp.arange(NY, dtype=jnp.int32)[:, None, None]
    key_block = key_block + 4 * jnp.arange(NK, dtype=jnp.int32)[None, :, None]
    key_block = key_block + 8 * jnp.arange(NZ, dtype=jnp.int32)[None, None, :]
    low, up = allowed_rows(
        4 * z + x,
        key_block.reshape(-1),
        32 + 8 * jnp.arange(NX, dtype=jnp.int32) + 2 * y + k,
        vertical_blocks,
        vertical_count,
        slash_offsets,
        slash_count,
    )
    heads = attend(partial, low, up, kv)
    heads = lax.all_to_all(heads, "z", 0, 0)
    mixed = mix(where, heads, out_weight)
    mixed = [mixed[0]] + [along("x", mixed[s], s) for s in range(1, NX)]
    mixed = (mixed[0] + mixed[1]) + (mixed[2] + mixed[3])
    own = lax.dynamic_index_in_dim(mixed, k, 0, keepdims=False)
    other = lax.dynamic_index_in_dim(mixed, 1 - k, 0, keepdims=False)
    other = lax.ppermute(other, "k", CORES)
    return jnp.concatenate([jnp.where(k == 0, own, other), jnp.where(k == 0, other, own)])


def solution(mesh):
    grid = Mesh(mesh.devices.reshape(NX, NY, NZ, NK), ALL)
    outer, ctx = ("x", "y"), ("z", "k")
    placed = (
        P(outer, None),
        P(outer, ctx),
        P(ctx, None),
        P(ctx, None),
        P(),
        P(),
        P(),
        P(),
        P(ctx, outer),
    )
    return jax.shard_map(
        shards, mesh=grid, in_specs=placed, out_specs=P(outer, ctx), check_vma=False
    )
```

```python
import math

import jax
import jax.numpy as jnp
from jax import lax
from jax.experimental import pallas as pl
from jax.experimental.pallas import tpu as pltpu
from jax.sharding import Mesh
from jax.sharding import PartitionSpec as P

HD = 128
BLOCK = 64
NX, NY, NZ, NK = 4, 4, 8, 2
ALL = ("x", "y", "z", "k")
VMEM = pl.BlockSpec(memory_space=pltpu.VMEM)
SMEM = pl.BlockSpec(memory_space=pltpu.SMEM)
ANY = pl.BlockSpec(memory_space=pl.ANY)
LIMIT = 60 << 20


def split(value):
    high = value.astype(jnp.bfloat16)
    low = (value - high.astype(jnp.float32)).astype(jnp.bfloat16)
    return high, low


def dot(left, right, dims):
    return lax.dot_general(left, right, dims, preferred_element_type=jnp.float32)


def dot3(left, right, dims):
    (lh, ll), (rh, rl) = left, right
    return dot(lh, rh, dims) + (dot(lh, rl, dims) + dot(ll, rh, dims))


MM = (((1,), (0,)), ((), ()))
MT = (((1,), (1,)), ((), ()))


def pick_kernel(where, rows, keys, values, *refs):
    outs, sent, sem, kv_sem = refs[:3], refs[3], refs[4], refs[5]
    x, y, k = where[0], where[1], where[2]
    copies = []
    for to in range(NZ):
        cols = pl.ds((to // 2) * HD, HD)
        for index, cache in enumerate((keys, values)):
            part = cache.at[pl.ds(pl.multiple_of(y * BLOCK, BLOCK), BLOCK), cols]
            copies.append(
                pltpu.make_async_copy(part, sent.at[to, index], kv_sem.at[2 * to + index])
            )
    for shift in range(1, NX):
        cols = pl.multiple_of(lax.rem(x + shift, NX) * 2048, 2048)
        part = rows.at[pl.ds(pl.multiple_of(k * BLOCK, BLOCK), BLOCK), pl.ds(cols, 2048)]
        copies.append(pltpu.make_async_copy(part, outs[shift - 1], sem.at[shift - 1]))
    for copy in copies:
        copy.start()
    for copy in copies:
        copy.wait()


def pick(where, hidden_rows, key_cache, value_cache):
    return pl.pallas_call(
        pick_kernel,
        out_shape=[jax.ShapeDtypeStruct((BLOCK, 2048), jnp.float32)] * 3
        + [jax.ShapeDtypeStruct((NZ, 2, BLOCK, HD), jnp.float32)],
        in_specs=[SMEM, ANY, ANY, ANY],
        out_specs=[VMEM] * 4,
        scratch_shapes=[pltpu.SemaphoreType.DMA((3,)), pltpu.SemaphoreType.DMA((2 * NZ,))],
        compiler_params=pltpu.CompilerParams(vmem_limit_bytes=LIMIT),
        name="pick",
    )(where, hidden_rows, key_cache, value_cache)


def project_kernel(where, rows, first, second, third, weights, *refs):
    outs, (left_buf, right_buf, total_buf, sems) = refs[:NX], refs[NX:]
    x, k = where[0], where[2]
    copies = []
    for y in range(NY):
        own = rows.at[
            pl.ds(pl.multiple_of(k * BLOCK, BLOCK), BLOCK),
            pl.ds(pl.multiple_of(x * 2048 + y * 512, 512), 512),
        ]
        parts = [own] + [part.at[:, pl.ds(y * 512, 512)] for part in (first, second, third)]
        group = [
            pltpu.make_async_copy(
                part, left_buf.at[y, lax.rem(x + NX - shift, NX)], sems.at[y, shift]
            )
            for shift, part in enumerate(parts)
        ]
        group.append(
            pltpu.make_async_copy(weights.at[pl.ds(2 * y, 2)], right_buf.at[y], sems.at[y, NX])
        )
        for copy in group:
            copy.start()
        copies.append(group)
    totals = [None, None]
    for y in range(NY):
        for copy in copies[y]:
            copy.wait()
        left = split(left_buf[y].reshape(NX * BLOCK, 512))
        for core in range(NK):
            term = dot3(left, split(right_buf[y, core]), MM)
            totals[core] = term if totals[core] is None else totals[core] + term
    for core in range(NK):
        for b in range(2):
            total_buf[2 * core + b] = totals[core][:, b * HD : (b + 1) * HD]
    for shift in range(NX):
        outs[shift][...] = total_buf[lax.rem(x + shift, NX)]


def project(where, rows, moved, weights):
    return pl.pallas_call(
        project_kernel,
        out_shape=[jax.ShapeDtypeStruct((NX * BLOCK, HD), jnp.float32)] * NX,
        in_specs=[SMEM] + [ANY] * 5,
        out_specs=[VMEM] * NX,
        scratch_shapes=[
            pltpu.VMEM((NY, NX, BLOCK, 512), jnp.float32),
            pltpu.VMEM((NY, NK, 512, 256), jnp.float32),
            pltpu.VMEM((NX, NX * BLOCK, HD), jnp.float32),
            pltpu.SemaphoreType.DMA((NY, NX + 1)),
        ],
        compiler_params=pltpu.CompilerParams(vmem_limit_bytes=LIMIT),
        cost_estimate=pl.CostEstimate(
            flops=6 * 256 * 2048 * 512, bytes_accessed=7 << 20, transcendentals=0
        ),
        name="project",
    )(where, rows, *moved, weights)


def attend_kernel(first, second, third, fourth, low, up, gathered, out, kv, scores, sem):
    tiles = gathered.shape[0]
    copies = [
        pltpu.make_async_copy(gathered.at[tile], kv.at[tile], sem.at[tile])
        for tile in range(tiles)
    ]
    for copy in copies:
        copy.start()
    width = NZ * BLOCK
    row = lax.broadcasted_iota(jnp.int32, (BLOCK, width), 0)
    col = lax.broadcasted_iota(jnp.int32, (BLOCK, width), 1)
    lower = row >= lax.rem(col, BLOCK)
    query = (first[...] + second[...]) + (third[...] + fourth[...])
    high, low_part = split(query * (math.log2(math.e) / math.sqrt(HD)))
    both = jnp.concatenate([high, low_part], axis=1)
    top = None
    for tile in range(tiles):
        copies[tile].wait()
        key_high, key_low = split(kv[tile, :, 0].reshape(width, HD))
        s = dot(both, jnp.concatenate([key_high, key_high], axis=1), MT)
        s = s + dot(high, key_low, MT)
        cols = slice(tile * width, (tile + 1) * width)
        bias = jnp.concatenate(
            [
                jnp.where(lower, low[b : b + 1, cols], up[b : b + 1, cols])
                for b in range(NX)
            ],
            axis=0,
        )
        s = s + bias
        scores[tile] = s
        top = s if top is None else jnp.maximum(top, s)
    top = jnp.max(top, axis=1, keepdims=True)
    total, summed = None, None
    for tile in range(tiles):
        weight = jnp.exp2(scores[tile] - top)
        weight_high, weight_low = split(weight)
        value_high, value_low = split(kv[tile, :, 1].reshape(width, HD))
        term = dot(weight_high, jnp.concatenate([value_high, value_low], axis=1), MM)
        term = term[:, :HD] + (term[:, HD:] + dot(weight_low, value_high, MM))
        total = weight if total is None else total + weight
        summed = term if summed is None else summed + term
    attended = summed / jnp.sum(total, axis=1, keepdims=True)
    for z in range(NZ):
        out[z] = attended


def attend(partial, low, up, gathered):
    rows = NX * BLOCK
    return pl.pallas_call(
        attend_kernel,
        out_shape=jax.ShapeDtypeStruct((NZ, rows, HD), jnp.float32),
        in_specs=[VMEM] * 6 + [ANY],
        out_specs=VMEM,
        scratch_shapes=[
            pltpu.VMEM((8, NZ, 2, BLOCK, HD), jnp.float32),
            pltpu.VMEM((8, rows, NZ * BLOCK), jnp.float32),
            pltpu.SemaphoreType.DMA((8,)),
        ],
        compiler_params=pltpu.CompilerParams(vmem_limit_bytes=LIMIT),
        cost_estimate=pl.CostEstimate(
            flops=12 * 256 * 4096 * HD, bytes_accessed=6 << 20, transcendentals=256 * 4096
        ),
        name="attend",
    )(*partial, low, up, gathered)


def mix_kernel(where, heads, weights, *refs):
    outs, (total_buf, buf, sem) = refs[:NX], refs[NX:]
    steps = NZ // 2
    copies = []
    for step in range(steps):
        copies.append(
            [
                pltpu.make_async_copy(
                    weights.at[part, pl.ds(2 * step, 2)], buf.at[step, part], sem.at[step, part]
                )
                for part in range(8)
            ]
        )
        for copy in copies[step]:
            copy.start()
    totals = [None, None]
    for step in range(steps):
        left = split(jnp.concatenate([heads[2 * step], heads[2 * step + 1]], axis=1))
        for copy in copies[step]:
            copy.wait()
        for core in range(NK):
            right = jnp.concatenate(
                [buf[step, :, z, core].reshape(HD, 512) for z in range(2)], axis=0
            )
            term = dot3(left, split(right), MM)
            totals[core] = term if totals[core] is None else totals[core] + term
    for core in range(NK):
        for x in range(NX):
            total_buf[x, core] = totals[core][x * BLOCK : (x + 1) * BLOCK]
    for shift in range(NX):
        outs[shift][...] = total_buf[lax.rem(where[0] + shift, NX)]


def mix(where, heads, weights):
    return pl.pallas_call(
        mix_kernel,
        out_shape=[jax.ShapeDtypeStruct((NK, BLOCK, 512), jnp.float32)] * NX,
        in_specs=[SMEM, VMEM, ANY],
        out_specs=[VMEM] * NX,
        scratch_shapes=[
            pltpu.VMEM((NX, NK, BLOCK, 512), jnp.float32),
            pltpu.VMEM((NZ // 2, 8, 2, NK, 16, 512), jnp.float32),
            pltpu.SemaphoreType.DMA((NZ // 2, 8)),
        ],
        compiler_params=pltpu.CompilerParams(vmem_limit_bytes=LIMIT),
        cost_estimate=pl.CostEstimate(
            flops=6 * 256 * 1024 * 1024, bytes_accessed=6 << 20, transcendentals=0
        ),
        name="mix",
    )(where, heads, weights)


def allowed_rows(
    head, key_block, query_block, vertical_blocks, vertical_count, slash_offsets, slash_count
):
    slots = jnp.arange(vertical_blocks.shape[1], dtype=jnp.int32)
    verticals = jnp.where(slots < vertical_count[head], vertical_blocks[head], -1)
    slashes = jnp.where(slots < slash_count[head], slash_offsets[head], -1)
    offset = query_block[:, None] - key_block[None, :]
    vert = jnp.any(key_block[:, None] == verticals[None, :], axis=1)[None, :]
    low_slash = jnp.any(offset[:, :, None] == slashes, axis=2)
    up_slash = jnp.any((offset - 1)[:, :, None] == slashes, axis=2)
    low = (offset >= 0) & (vert | low_slash)
    up = (offset >= 1) & (vert | up_slash)
    bias = jnp.where(jnp.stack([low, up]), 0.0, -jnp.inf)
    bias = jnp.repeat(bias, BLOCK, axis=2)
    return bias[0], bias[1]


CORES = [(0, 1), (1, 0)]


def along(axis, value, shift):
    count = lax.axis_size(axis)
    return lax.ppermute(value, axis, [(i, (i + shift) % count) for i in range(count)])


def shards(
    hidden_rows,
    query_weight,
    key_cache,
    value_cache,
    vertical_blocks,
    vertical_count,
    slash_offsets,
    slash_count,
    output_weight,
):
    x, y, z, k = (lax.axis_index(name) for name in ALL)
    where = jnp.stack([x, y, k]).astype(jnp.int32)
    weights = lax.all_gather(query_weight, ("y", "k"), axis=0)
    *picked, sent = pick(where, hidden_rows, key_cache, value_cache)
    hidden = [along("x", piece, shift) for shift, piece in enumerate(picked, 1)]
    near = lax.all_to_all(sent, "z", 0, 0)
    rows = output_weight.reshape(2, NY, NK, 16, 512)
    kept = lax.dynamic_index_in_dim(rows, k, 2, keepdims=False)
    given = lax.dynamic_index_in_dim(rows, 1 - k, 2, keepdims=False)
    taken = lax.ppermute(given, "k", CORES)
    rows = jnp.where(k == 0, jnp.stack([kept, taken]), jnp.stack([taken, kept]))
    rows, near = lax.optimization_barrier((rows, near))
    rows = lax.all_to_all(rows.reshape(NX * NY, 16, 512), ("x", "y"), 0, 0)
    rows, hidden = lax.optimization_barrier((rows, hidden))
    rows = lax.all_to_all(rows.reshape(NZ, NK, 16, 512), "z", 0, 0)
    kv = lax.all_gather(near, ("y", "k"), axis=0)
    out_weight = lax.all_gather(rows, ("y", "k"), axis=0)
    partial = project(where, hidden_rows, hidden, weights)
    partial = [partial[0]] + [along("x", partial[s], s) for s in range(1, NX)]
    key_block = jnp.arange(NY, dtype=jnp.int32)[:, None, None]
    key_block = key_block + 4 * jnp.arange(NK, dtype=jnp.int32)[None, :, None]
    key_block = key_block + 8 * jnp.arange(NZ, dtype=jnp.int32)[None, None, :]
    low, up = allowed_rows(
        4 * z + x,
        key_block.reshape(-1),
        32 + 8 * jnp.arange(NX, dtype=jnp.int32) + 2 * y + k,
        vertical_blocks,
        vertical_count,
        slash_offsets,
        slash_count,
    )
    heads = attend(partial, low, up, kv)
    heads = lax.all_to_all(heads, "z", 0, 0)
    mixed = mix(where, heads, out_weight)
    mixed = [mixed[0]] + [along("x", mixed[s], s) for s in range(1, NX)]
    mixed = (mixed[0] + mixed[1]) + (mixed[2] + mixed[3])
    own = lax.dynamic_index_in_dim(mixed, k, 0, keepdims=False)
    other = lax.dynamic_index_in_dim(mixed, 1 - k, 0, keepdims=False)
    other = lax.ppermute(other, "k", CORES)
    return jnp.concatenate([jnp.where(k == 0, own, other), jnp.where(k == 0, other, own)])


def solution(mesh):
    grid = Mesh(mesh.devices.reshape(NX, NY, NZ, NK), ALL)
    outer, ctx = ("x", "y"), ("z", "k")
    placed = (
        P(outer, None),
        P(outer, ctx),
        P(ctx, None),
        P(ctx, None),
        P(),
        P(),
        P(),
        P(),
        P(ctx, outer),
    )
    return jax.shard_map(
        shards, mesh=grid, in_specs=placed, out_specs=P(outer, ctx), check_vma=False
    )
```

```python
import math

import jax
import jax.numpy as jnp
from jax import lax
from jax.experimental import pallas as pl
from jax.experimental.pallas import tpu as pltpu
from jax.sharding import Mesh
from jax.sharding import PartitionSpec as P

HD = 128
BLOCK = 64
NX, NY, NZ, NK = 4, 4, 8, 2
ALL = ("x", "y", "z", "k")
VMEM = pl.BlockSpec(memory_space=pltpu.VMEM)
SMEM = pl.BlockSpec(memory_space=pltpu.SMEM)
ANY = pl.BlockSpec(memory_space=pl.ANY)
LIMIT = 60 << 20


def split(value):
    high = value.astype(jnp.bfloat16)
    low = (value - high.astype(jnp.float32)).astype(jnp.bfloat16)
    return high, low


def dot(left, right, dims):
    return lax.dot_general(left, right, dims, preferred_element_type=jnp.float32)


def dot3(left, right, dims):
    (lh, ll), (rh, rl) = left, right
    return dot(lh, rh, dims) + (dot(lh, rl, dims) + dot(ll, rh, dims))


MM = (((1,), (0,)), ((), ()))
MT = (((1,), (1,)), ((), ()))


def pick_kernel(where, rows, *refs):
    outs, sem = refs[:3], refs[3]
    x, k = where[0], where[2]
    copies = []
    for shift in range(1, NX):
        cols = pl.multiple_of(lax.rem(x + shift, NX) * 2048, 2048)
        part = rows.at[pl.ds(pl.multiple_of(k * BLOCK, BLOCK), BLOCK), pl.ds(cols, 2048)]
        copies.append(pltpu.make_async_copy(part, outs[shift - 1], sem.at[shift - 1]))
    for copy in copies:
        copy.start()
    for copy in copies:
        copy.wait()


def pick(where, hidden_rows):
    return pl.pallas_call(
        pick_kernel,
        out_shape=[jax.ShapeDtypeStruct((BLOCK, 2048), jnp.float32)] * 3,
        in_specs=[SMEM, ANY],
        out_specs=[VMEM] * 3,
        scratch_shapes=[pltpu.SemaphoreType.DMA((3,))],
        compiler_params=pltpu.CompilerParams(vmem_limit_bytes=LIMIT),
        name="pick",
    )(where, hidden_rows)


def pick_keys_kernel(where, keys, values, out, sem):
    y = where[1]
    copies = []
    for to in range(NZ):
        for index, cache in enumerate((keys, values)):
            part = cache.at[
                pl.ds(pl.multiple_of(y * BLOCK, BLOCK), BLOCK), pl.ds((to // 2) * HD, HD)
            ]
            copies.append(pltpu.make_async_copy(part, out.at[to, index], sem.at[2 * to + index]))
    for copy in copies:
        copy.start()
    for copy in copies:
        copy.wait()


def pick_keys(where, key_cache, value_cache):
    return pl.pallas_call(
        pick_keys_kernel,
        out_shape=jax.ShapeDtypeStruct((NZ, 2, BLOCK, HD), jnp.float32),
        in_specs=[SMEM, ANY, ANY],
        out_specs=VMEM,
        scratch_shapes=[pltpu.SemaphoreType.DMA((2 * NZ,))],
        compiler_params=pltpu.CompilerParams(vmem_limit_bytes=56 << 20),
        cost_estimate=pl.CostEstimate(flops=0, bytes_accessed=64 << 20, transcendentals=0),
        name="pick_keys",
    )(where, key_cache, value_cache)


def project_kernel(where, rows, first, second, third, weights, *refs):
    outs, (left_buf, right_buf, total_buf, sems) = refs[:NX], refs[NX:]
    x, k = where[0], where[2]
    copies = []
    for y in range(NY):
        own = rows.at[
            pl.ds(pl.multiple_of(k * BLOCK, BLOCK), BLOCK),
            pl.ds(pl.multiple_of(x * 2048 + y * 512, 512), 512),
        ]
        parts = [own] + [part.at[:, pl.ds(y * 512, 512)] for part in (first, second, third)]
        group = [
            pltpu.make_async_copy(
                part, left_buf.at[y, lax.rem(x + NX - shift, NX)], sems.at[y, shift]
            )
            for shift, part in enumerate(parts)
        ]
        group.append(
            pltpu.make_async_copy(weights.at[pl.ds(2 * y, 2)], right_buf.at[y], sems.at[y, NX])
        )
        for copy in group:
            copy.start()
        copies.append(group)
    totals = [None, None]
    for y in range(NY):
        for copy in copies[y]:
            copy.wait()
        left = split(left_buf[y].reshape(NX * BLOCK, 512))
        for core in range(NK):
            term = dot3(left, split(right_buf[y, core]), MM)
            totals[core] = term if totals[core] is None else totals[core] + term
    for core in range(NK):
        for b in range(2):
            total_buf[2 * core + b] = totals[core][:, b * HD : (b + 1) * HD]
    for shift in range(NX):
        outs[shift][...] = total_buf[lax.rem(x + shift, NX)]


def project(where, rows, moved, weights):
    return pl.pallas_call(
        project_kernel,
        out_shape=[jax.ShapeDtypeStruct((NX * BLOCK, HD), jnp.float32)] * NX,
        in_specs=[SMEM] + [ANY] * 5,
        out_specs=[VMEM] * NX,
        scratch_shapes=[
            pltpu.VMEM((NY, NX, BLOCK, 512), jnp.float32),
            pltpu.VMEM((NY, NK, 512, 256), jnp.float32),
            pltpu.VMEM((NX, NX * BLOCK, HD), jnp.float32),
            pltpu.SemaphoreType.DMA((NY, NX + 1)),
        ],
        compiler_params=pltpu.CompilerParams(vmem_limit_bytes=LIMIT),
        cost_estimate=pl.CostEstimate(
            flops=6 * 256 * 2048 * 512, bytes_accessed=7 << 20, transcendentals=0
        ),
        name="project",
    )(where, rows, *moved, weights)


def attend_kernel(first, second, third, fourth, low, up, gathered, out, kv, scores, sem):
    tiles = gathered.shape[0]
    copies = [
        pltpu.make_async_copy(gathered.at[tile], kv.at[tile], sem.at[tile])
        for tile in range(tiles)
    ]
    for copy in copies:
        copy.start()
    width = NZ * BLOCK
    row = lax.broadcasted_iota(jnp.int32, (BLOCK, width), 0)
    col = lax.broadcasted_iota(jnp.int32, (BLOCK, width), 1)
    lower = row >= lax.rem(col, BLOCK)
    query = (first[...] + second[...]) + (third[...] + fourth[...])
    high, low_part = split(query * (math.log2(math.e) / math.sqrt(HD)))
    both = jnp.concatenate([high, low_part], axis=1)
    top = None
    for tile in range(tiles):
        copies[tile].wait()
        key_high, key_low = split(kv[tile, :, 0].reshape(width, HD))
        s = dot(both, jnp.concatenate([key_high, key_high], axis=1), MT)
        s = s + dot(high, key_low, MT)
        cols = slice(tile * width, (tile + 1) * width)
        bias = jnp.concatenate(
            [
                jnp.where(lower, low[b : b + 1, cols], up[b : b + 1, cols])
                for b in range(NX)
            ],
            axis=0,
        )
        s = s + bias
        scores[tile] = s
        top = s if top is None else jnp.maximum(top, s)
    top = jnp.max(top, axis=1, keepdims=True)
    total, summed = None, None
    for tile in range(tiles):
        weight = jnp.exp2(scores[tile] - top)
        weight_high, weight_low = split(weight)
        value_high, value_low = split(kv[tile, :, 1].reshape(width, HD))
        term = dot(weight_high, jnp.concatenate([value_high, value_low], axis=1), MM)
        term = term[:, :HD] + (term[:, HD:] + dot(weight_low, value_high, MM))
        total = weight if total is None else total + weight
        summed = term if summed is None else summed + term
    attended = summed / jnp.sum(total, axis=1, keepdims=True)
    for z in range(NZ):
        out[z] = attended


def attend(partial, low, up, gathered):
    rows = NX * BLOCK
    return pl.pallas_call(
        attend_kernel,
        out_shape=jax.ShapeDtypeStruct((NZ, rows, HD), jnp.float32),
        in_specs=[VMEM] * 6 + [ANY],
        out_specs=VMEM,
        scratch_shapes=[
            pltpu.VMEM((8, NZ, 2, BLOCK, HD), jnp.float32),
            pltpu.VMEM((8, rows, NZ * BLOCK), jnp.float32),
            pltpu.SemaphoreType.DMA((8,)),
        ],
        compiler_params=pltpu.CompilerParams(vmem_limit_bytes=LIMIT),
        cost_estimate=pl.CostEstimate(
            flops=12 * 256 * 4096 * HD, bytes_accessed=6 << 20, transcendentals=256 * 4096
        ),
        name="attend",
    )(*partial, low, up, gathered)


def mix_kernel(where, heads, weights, *refs):
    outs, (total_buf, buf, sem) = refs[:NX], refs[NX:]
    steps = NZ // 2
    copies = []
    for step in range(steps):
        copies.append(
            [
                pltpu.make_async_copy(
                    weights.at[part, pl.ds(2 * step, 2)], buf.at[step, part], sem.at[step, part]
                )
                for part in range(8)
            ]
        )
        for copy in copies[step]:
            copy.start()
    totals = [None, None]
    for step in range(steps):
        left = split(jnp.concatenate([heads[2 * step], heads[2 * step + 1]], axis=1))
        for copy in copies[step]:
            copy.wait()
        for core in range(NK):
            right = jnp.concatenate(
                [buf[step, :, z, core].reshape(HD, 512) for z in range(2)], axis=0
            )
            term = dot3(left, split(right), MM)
            totals[core] = term if totals[core] is None else totals[core] + term
    for core in range(NK):
        for x in range(NX):
            total_buf[x, core] = totals[core][x * BLOCK : (x + 1) * BLOCK]
    for shift in range(NX):
        outs[shift][...] = total_buf[lax.rem(where[0] + shift, NX)]


def mix(where, heads, weights):
    return pl.pallas_call(
        mix_kernel,
        out_shape=[jax.ShapeDtypeStruct((NK, BLOCK, 512), jnp.float32)] * NX,
        in_specs=[SMEM, VMEM, ANY],
        out_specs=[VMEM] * NX,
        scratch_shapes=[
            pltpu.VMEM((NX, NK, BLOCK, 512), jnp.float32),
            pltpu.VMEM((NZ // 2, 8, 2, NK, 16, 512), jnp.float32),
            pltpu.SemaphoreType.DMA((NZ // 2, 8)),
        ],
        compiler_params=pltpu.CompilerParams(vmem_limit_bytes=LIMIT),
        cost_estimate=pl.CostEstimate(
            flops=6 * 256 * 1024 * 1024, bytes_accessed=6 << 20, transcendentals=0
        ),
        name="mix",
    )(where, heads, weights)


def allowed_rows(
    head, key_block, query_block, vertical_blocks, vertical_count, slash_offsets, slash_count
):
    slots = jnp.arange(vertical_blocks.shape[1], dtype=jnp.int32)
    verticals = jnp.where(slots < vertical_count[head], vertical_blocks[head], -1)
    slashes = jnp.where(slots < slash_count[head], slash_offsets[head], -1)
    offset = query_block[:, None] - key_block[None, :]
    vert = jnp.any(key_block[:, None] == verticals[None, :], axis=1)[None, :]
    low_slash = jnp.any(offset[:, :, None] == slashes, axis=2)
    up_slash = jnp.any((offset - 1)[:, :, None] == slashes, axis=2)
    low = (offset >= 0) & (vert | low_slash)
    up = (offset >= 1) & (vert | up_slash)
    bias = jnp.where(jnp.stack([low, up]), 0.0, -jnp.inf)
    bias = jnp.repeat(bias, BLOCK, axis=2)
    return bias[0], bias[1]


CORES = [(0, 1), (1, 0)]


def along(axis, value, shift):
    count = lax.axis_size(axis)
    return lax.ppermute(value, axis, [(i, (i + shift) % count) for i in range(count)])


def shards(
    hidden_rows,
    query_weight,
    key_cache,
    value_cache,
    vertical_blocks,
    vertical_count,
    slash_offsets,
    slash_count,
    output_weight,
):
    x, y, z, k = (lax.axis_index(name) for name in ALL)
    where = jnp.stack([x, y, k]).astype(jnp.int32)
    weights = lax.all_gather(query_weight, ("y", "k"), axis=0)
    picked = pick(where, hidden_rows)
    hidden = [along("x", piece, shift) for shift, piece in enumerate(picked, 1)]
    behind, picked = lax.optimization_barrier((where, picked))
    near = lax.all_to_all(pick_keys(behind, key_cache, value_cache), "z", 0, 0)
    rows = output_weight.reshape(2, NY, NK, 16, 512)
    kept = lax.dynamic_index_in_dim(rows, k, 2, keepdims=False)
    given = lax.dynamic_index_in_dim(rows, 1 - k, 2, keepdims=False)
    taken = lax.ppermute(given, "k", CORES)
    rows = jnp.where(k == 0, jnp.stack([kept, taken]), jnp.stack([taken, kept]))
    rows, near, hidden = lax.optimization_barrier((rows, near, hidden))
    rows = lax.all_to_all(rows.reshape(NX * NY, 16, 512), ("x", "y"), 0, 0)
    kv = lax.all_gather(near, ("y", "k"), axis=0)
    partial = project(where, hidden_rows, hidden, weights)
    partial = [partial[0]] + [along("x", partial[s], s) for s in range(1, NX)]
    rows, partial = lax.optimization_barrier((rows, partial))
    rows = lax.all_to_all(rows.reshape(NZ, NK, 16, 512), "z", 0, 0)
    out_weight = lax.all_gather(rows, ("y", "k"), axis=0)
    key_block = jnp.arange(NY, dtype=jnp.int32)[:, None, None]
    key_block = key_block + 4 * jnp.arange(NK, dtype=jnp.int32)[None, :, None]
    key_block = key_block + 8 * jnp.arange(NZ, dtype=jnp.int32)[None, None, :]
    low, up = allowed_rows(
        4 * z + x,
        key_block.reshape(-1),
        32 + 8 * jnp.arange(NX, dtype=jnp.int32) + 2 * y + k,
        vertical_blocks,
        vertical_count,
        slash_offsets,
        slash_count,
    )
    heads = attend(partial, low, up, kv)
    heads = lax.all_to_all(heads, "z", 0, 0)
    mixed = mix(where, heads, out_weight)
    mixed = [mixed[0]] + [along("x", mixed[s], s) for s in range(1, NX)]
    mixed = (mixed[0] + mixed[1]) + (mixed[2] + mixed[3])
    own = lax.dynamic_index_in_dim(mixed, k, 0, keepdims=False)
    other = lax.dynamic_index_in_dim(mixed, 1 - k, 0, keepdims=False)
    other = lax.ppermute(other, "k", CORES)
    return jnp.concatenate([jnp.where(k == 0, own, other), jnp.where(k == 0, other, own)])


def solution(mesh):
    grid = Mesh(mesh.devices.reshape(NX, NY, NZ, NK), ALL)
    outer, ctx = ("x", "y"), ("z", "k")
    placed = (
        P(outer, None),
        P(outer, ctx),
        P(ctx, None),
        P(ctx, None),
        P(),
        P(),
        P(),
        P(),
        P(ctx, outer),
    )
    return jax.shard_map(
        shards, mesh=grid, in_specs=placed, out_specs=P(outer, ctx), check_vma=False
    )
```

```python
import math

import jax
import jax.numpy as jnp
from jax import lax
from jax.experimental import pallas as pl
from jax.experimental.pallas import tpu as pltpu
from jax.sharding import Mesh
from jax.sharding import PartitionSpec as P

HD = 128
BLOCK = 64
NX, NY, NZ, NK = 4, 4, 8, 2
ALL = ("x", "y", "z", "k")
VMEM = pl.BlockSpec(memory_space=pltpu.VMEM)
SMEM = pl.BlockSpec(memory_space=pltpu.SMEM)
ANY = pl.BlockSpec(memory_space=pl.ANY)
LIMIT = 60 << 20


def split(value):
    high = value.astype(jnp.bfloat16)
    low = (value - high.astype(jnp.float32)).astype(jnp.bfloat16)
    return high, low


def dot(left, right, dims):
    return lax.dot_general(left, right, dims, preferred_element_type=jnp.float32)


def dot3(left, right, dims):
    (lh, ll), (rh, rl) = left, right
    return dot(lh, rh, dims) + (dot(lh, rl, dims) + dot(ll, rh, dims))


MM = (((1,), (0,)), ((), ()))
MT = (((1,), (1,)), ((), ()))


def pick_kernel(where, rows, *refs):
    outs, sem = refs[:3], refs[3]
    x, k = where[0], where[2]
    copies = []
    for shift in range(1, NX):
        cols = pl.multiple_of(lax.rem(x + shift, NX) * 2048, 2048)
        part = rows.at[pl.ds(pl.multiple_of(k * BLOCK, BLOCK), BLOCK), pl.ds(cols, 2048)]
        copies.append(pltpu.make_async_copy(part, outs[shift - 1], sem.at[shift - 1]))
    for number, copy in enumerate(copies):
        copy.start(priority=number % 2)
    for copy in copies:
        copy.wait()


def pick(where, hidden_rows):
    return pl.pallas_call(
        pick_kernel,
        out_shape=[jax.ShapeDtypeStruct((BLOCK, 2048), jnp.float32)] * 3,
        in_specs=[SMEM, ANY],
        out_specs=[VMEM] * 3,
        scratch_shapes=[pltpu.SemaphoreType.DMA((3,))],
        compiler_params=pltpu.CompilerParams(vmem_limit_bytes=LIMIT),
        name="pick",
    )(where, hidden_rows)


def pick_keys_kernel(where, keys, values, out, sem):
    y = where[1]
    copies = []
    for to in range(NZ):
        for index, cache in enumerate((keys, values)):
            part = cache.at[
                pl.ds(pl.multiple_of(y * BLOCK, BLOCK), BLOCK), pl.ds((to // 2) * HD, HD)
            ]
            copies.append(pltpu.make_async_copy(part, out.at[to, index], sem.at[2 * to + index]))
    for number, copy in enumerate(copies):
        copy.start(priority=number % 2)
    for copy in copies:
        copy.wait()


def pick_keys(where, key_cache, value_cache):
    return pl.pallas_call(
        pick_keys_kernel,
        out_shape=jax.ShapeDtypeStruct((NZ, 2, BLOCK, HD), jnp.float32),
        in_specs=[SMEM, ANY, ANY],
        out_specs=VMEM,
        scratch_shapes=[pltpu.SemaphoreType.DMA((2 * NZ,))],
        compiler_params=pltpu.CompilerParams(vmem_limit_bytes=56 << 20),
        cost_estimate=pl.CostEstimate(flops=0, bytes_accessed=64 << 20, transcendentals=0),
        name="pick_keys",
    )(where, key_cache, value_cache)


def project_kernel(where, rows, first, second, third, weights, *refs):
    outs, (left_buf, right_buf, total_buf, sems) = refs[:NX], refs[NX:]
    x, k = where[0], where[2]
    copies = []
    for y in range(NY):
        own = rows.at[
            pl.ds(pl.multiple_of(k * BLOCK, BLOCK), BLOCK),
            pl.ds(pl.multiple_of(x * 2048 + y * 512, 512), 512),
        ]
        parts = [own] + [part.at[:, pl.ds(y * 512, 512)] for part in (first, second, third)]
        group = [
            pltpu.make_async_copy(
                part, left_buf.at[y, lax.rem(x + NX - shift, NX)], sems.at[y, shift]
            )
            for shift, part in enumerate(parts)
        ]
        group.append(
            pltpu.make_async_copy(weights.at[pl.ds(2 * y, 2)], right_buf.at[y], sems.at[y, NX])
        )
        for number, copy in enumerate(group):
            copy.start(priority=number % 2)
        copies.append(group)
    totals = [None, None]
    for y in range(NY):
        for copy in copies[y]:
            copy.wait()
        left = split(left_buf[y].reshape(NX * BLOCK, 512))
        for core in range(NK):
            term = dot3(left, split(right_buf[y, core]), MM)
            totals[core] = term if totals[core] is None else totals[core] + term
    for core in range(NK):
        for b in range(2):
            total_buf[2 * core + b] = totals[core][:, b * HD : (b + 1) * HD]
    for shift in range(NX):
        outs[shift][...] = total_buf[lax.rem(x + shift, NX)]


def project(where, rows, moved, weights):
    return pl.pallas_call(
        project_kernel,
        out_shape=[jax.ShapeDtypeStruct((NX * BLOCK, HD), jnp.float32)] * NX,
        in_specs=[SMEM] + [ANY] * 5,
        out_specs=[VMEM] * NX,
        scratch_shapes=[
            pltpu.VMEM((NY, NX, BLOCK, 512), jnp.float32),
            pltpu.VMEM((NY, NK, 512, 256), jnp.float32),
            pltpu.VMEM((NX, NX * BLOCK, HD), jnp.float32),
            pltpu.SemaphoreType.DMA((NY, NX + 1)),
        ],
        compiler_params=pltpu.CompilerParams(vmem_limit_bytes=LIMIT),
        cost_estimate=pl.CostEstimate(
            flops=6 * 256 * 2048 * 512, bytes_accessed=7 << 20, transcendentals=0
        ),
        name="project",
    )(where, rows, *moved, weights)


def attend_kernel(first, second, third, fourth, low, up, gathered, out, kv, scores, sem):
    tiles = gathered.shape[0]
    copies = [
        pltpu.make_async_copy(gathered.at[tile], kv.at[tile], sem.at[tile])
        for tile in range(tiles)
    ]
    for tile, copy in enumerate(copies):
        copy.start(priority=tile % 2)
    width = NZ * BLOCK
    row = lax.broadcasted_iota(jnp.int32, (BLOCK, width), 0)
    col = lax.broadcasted_iota(jnp.int32, (BLOCK, width), 1)
    lower = row >= lax.rem(col, BLOCK)
    query = (first[...] + second[...]) + (third[...] + fourth[...])
    high, low_part = split(query * (math.log2(math.e) / math.sqrt(HD)))
    both = jnp.concatenate([high, low_part], axis=1)
    top = None
    for tile in range(tiles):
        copies[tile].wait()
        key_high, key_low = split(kv[tile, :, 0].reshape(width, HD))
        s = dot(both, jnp.concatenate([key_high, key_high], axis=1), MT)
        s = s + dot(high, key_low, MT)
        cols = slice(tile * width, (tile + 1) * width)
        bias = jnp.concatenate(
            [
                jnp.where(lower, low[b : b + 1, cols], up[b : b + 1, cols])
                for b in range(NX)
            ],
            axis=0,
        )
        s = s + bias
        scores[tile] = s
        top = s if top is None else jnp.maximum(top, s)
    top = jnp.max(top, axis=1, keepdims=True)
    total, summed = None, None
    for tile in range(tiles):
        weight = jnp.exp2(scores[tile] - top)
        weight_high, weight_low = split(weight)
        value_high, value_low = split(kv[tile, :, 1].reshape(width, HD))
        term = dot(weight_high, jnp.concatenate([value_high, value_low], axis=1), MM)
        term = term[:, :HD] + (term[:, HD:] + dot(weight_low, value_high, MM))
        total = weight if total is None else total + weight
        summed = term if summed is None else summed + term
    attended = summed / jnp.sum(total, axis=1, keepdims=True)
    for z in range(NZ):
        out[z] = attended


def attend(partial, low, up, gathered):
    rows = NX * BLOCK
    return pl.pallas_call(
        attend_kernel,
        out_shape=jax.ShapeDtypeStruct((NZ, rows, HD), jnp.float32),
        in_specs=[VMEM] * 6 + [ANY],
        out_specs=VMEM,
        scratch_shapes=[
            pltpu.VMEM((8, NZ, 2, BLOCK, HD), jnp.float32),
            pltpu.VMEM((8, rows, NZ * BLOCK), jnp.float32),
            pltpu.SemaphoreType.DMA((8,)),
        ],
        compiler_params=pltpu.CompilerParams(vmem_limit_bytes=LIMIT),
        cost_estimate=pl.CostEstimate(
            flops=12 * 256 * 4096 * HD, bytes_accessed=6 << 20, transcendentals=256 * 4096
        ),
        name="attend",
    )(*partial, low, up, gathered)


def mix_kernel(where, heads, weights, *refs):
    outs, (total_buf, buf, sem) = refs[:NX], refs[NX:]
    steps = NZ // 2
    copies = []
    for step in range(steps):
        copies.append(
            [
                pltpu.make_async_copy(
                    weights.at[part, pl.ds(2 * step, 2)], buf.at[step, part], sem.at[step, part]
                )
                for part in range(8)
            ]
        )
        for number, copy in enumerate(copies[step]):
            copy.start(priority=number % 2)
    totals = [None, None]
    for step in range(steps):
        left = split(jnp.concatenate([heads[2 * step], heads[2 * step + 1]], axis=1))
        for copy in copies[step]:
            copy.wait()
        for core in range(NK):
            right = jnp.concatenate(
                [buf[step, :, z, core].reshape(HD, 512) for z in range(2)], axis=0
            )
            term = dot3(left, split(right), MM)
            totals[core] = term if totals[core] is None else totals[core] + term
    for core in range(NK):
        for x in range(NX):
            total_buf[x, core] = totals[core][x * BLOCK : (x + 1) * BLOCK]
    for shift in range(NX):
        outs[shift][...] = total_buf[lax.rem(where[0] + shift, NX)]


def mix(where, heads, weights):
    return pl.pallas_call(
        mix_kernel,
        out_shape=[jax.ShapeDtypeStruct((NK, BLOCK, 512), jnp.float32)] * NX,
        in_specs=[SMEM, VMEM, ANY],
        out_specs=[VMEM] * NX,
        scratch_shapes=[
            pltpu.VMEM((NX, NK, BLOCK, 512), jnp.float32),
            pltpu.VMEM((NZ // 2, 8, 2, NK, 16, 512), jnp.float32),
            pltpu.SemaphoreType.DMA((NZ // 2, 8)),
        ],
        compiler_params=pltpu.CompilerParams(vmem_limit_bytes=LIMIT),
        cost_estimate=pl.CostEstimate(
            flops=6 * 256 * 1024 * 1024, bytes_accessed=6 << 20, transcendentals=0
        ),
        name="mix",
    )(where, heads, weights)


def allowed_rows(
    head, key_block, query_block, vertical_blocks, vertical_count, slash_offsets, slash_count
):
    slots = jnp.arange(vertical_blocks.shape[1], dtype=jnp.int32)
    verticals = jnp.where(slots < vertical_count[head], vertical_blocks[head], -1)
    slashes = jnp.where(slots < slash_count[head], slash_offsets[head], -1)
    offset = query_block[:, None] - key_block[None, :]
    vert = jnp.any(key_block[:, None] == verticals[None, :], axis=1)[None, :]
    low_slash = jnp.any(offset[:, :, None] == slashes, axis=2)
    up_slash = jnp.any((offset - 1)[:, :, None] == slashes, axis=2)
    low = (offset >= 0) & (vert | low_slash)
    up = (offset >= 1) & (vert | up_slash)
    bias = jnp.where(jnp.stack([low, up]), 0.0, -jnp.inf)
    bias = jnp.repeat(bias, BLOCK, axis=2)
    return bias[0], bias[1]


CORES = [(0, 1), (1, 0)]


def along(axis, value, shift):
    count = lax.axis_size(axis)
    return lax.ppermute(value, axis, [(i, (i + shift) % count) for i in range(count)])


def shards(
    hidden_rows,
    query_weight,
    key_cache,
    value_cache,
    vertical_blocks,
    vertical_count,
    slash_offsets,
    slash_count,
    output_weight,
):
    x, y, z, k = (lax.axis_index(name) for name in ALL)
    where = jnp.stack([x, y, k]).astype(jnp.int32)
    weights = lax.all_gather(query_weight, ("y", "k"), axis=0)
    picked = pick(where, hidden_rows)
    hidden = [along("x", piece, shift) for shift, piece in enumerate(picked, 1)]
    behind, hidden[0] = lax.optimization_barrier((where, hidden[0]))
    near = lax.all_to_all(pick_keys(behind, key_cache, value_cache), "z", 0, 0)
    rows = output_weight.reshape(2, NY, NK, 16, 512)
    kept = lax.dynamic_index_in_dim(rows, k, 2, keepdims=False)
    given = lax.dynamic_index_in_dim(rows, 1 - k, 2, keepdims=False)
    taken = lax.ppermute(given, "k", CORES)
    rows = jnp.where(k == 0, jnp.stack([kept, taken]), jnp.stack([taken, kept]))
    rows, near, hidden = lax.optimization_barrier((rows, near, hidden))
    rows = lax.all_to_all(rows.reshape(NX * NY, 16, 512), ("x", "y"), 0, 0)
    kv = lax.all_gather(near, ("y", "k"), axis=0)
    key_block = jnp.arange(NY, dtype=jnp.int32)[:, None, None]
    key_block = key_block + 4 * jnp.arange(NK, dtype=jnp.int32)[None, :, None]
    key_block = key_block + 8 * jnp.arange(NZ, dtype=jnp.int32)[None, None, :]
    low, up = allowed_rows(
        4 * z + x,
        key_block.reshape(-1),
        32 + 8 * jnp.arange(NX, dtype=jnp.int32) + 2 * y + k,
        vertical_blocks,
        vertical_count,
        slash_offsets,
        slash_count,
    )
    partial = project(where, hidden_rows, hidden, weights)
    partial = [partial[0]] + [along("x", partial[s], s) for s in range(1, NX)]
    rows, partial, low, up = lax.optimization_barrier((rows, partial, low, up))
    rows = lax.all_to_all(rows.reshape(NZ, NK, 16, 512), "z", 0, 0)
    out_weight = lax.all_gather(rows, ("y", "k"), axis=0)
    heads = attend(partial, low, up, kv)
    heads = lax.all_to_all(heads, "z", 0, 0)
    mixed = mix(where, heads, out_weight)
    mixed = [mixed[0]] + [along("x", mixed[s], s) for s in range(1, NX)]
    mixed = (mixed[0] + mixed[1]) + (mixed[2] + mixed[3])
    own = lax.dynamic_index_in_dim(mixed, k, 0, keepdims=False)
    other = lax.dynamic_index_in_dim(mixed, 1 - k, 0, keepdims=False)
    other = lax.ppermute(other, "k", CORES)
    return jnp.concatenate([jnp.where(k == 0, own, other), jnp.where(k == 0, other, own)])


def solution(mesh):
    grid = Mesh(mesh.devices.reshape(NX, NY, NZ, NK), ALL)
    outer, ctx = ("x", "y"), ("z", "k")
    placed = (
        P(outer, None),
        P(outer, ctx),
        P(ctx, None),
        P(ctx, None),
        P(),
        P(),
        P(),
        P(),
        P(ctx, outer),
    )
    return jax.shard_map(
        shards, mesh=grid, in_specs=placed, out_specs=P(outer, ctx), check_vma=False
    )
```

```python
import math

import jax
import jax.numpy as jnp
from jax import lax
from jax.experimental import pallas as pl
from jax.experimental.pallas import tpu as pltpu
from jax.sharding import Mesh
from jax.sharding import PartitionSpec as P

HD = 128
BLOCK = 64
NX, NY, NZ, NK = 4, 4, 8, 2
ALL = ("x", "y", "z", "k")
VMEM = pl.BlockSpec(memory_space=pltpu.VMEM)
SMEM = pl.BlockSpec(memory_space=pltpu.SMEM)
ANY = pl.BlockSpec(memory_space=pl.ANY)
LIMIT = 60 << 20


def split(value):
    high = value.astype(jnp.bfloat16)
    low = (value - high.astype(jnp.float32)).astype(jnp.bfloat16)
    return high, low


def dot(left, right, dims):
    return lax.dot_general(left, right, dims, preferred_element_type=jnp.float32)


def dot3(left, right, dims):
    (lh, ll), (rh, rl) = left, right
    return dot(lh, rh, dims) + (dot(lh, rl, dims) + dot(ll, rh, dims))


MM = (((1,), (0,)), ((), ()))
MT = (((1,), (1,)), ((), ()))


def pick_kernel(where, rows, *refs):
    outs, sem = refs[:3], refs[3]
    x, k = where[0], where[2]
    copies = []
    for shift in range(1, NX):
        cols = pl.multiple_of(lax.rem(x + shift, NX) * 2048, 2048)
        part = rows.at[pl.ds(pl.multiple_of(k * BLOCK, BLOCK), BLOCK), pl.ds(cols, 2048)]
        copies.append(pltpu.make_async_copy(part, outs[shift - 1], sem.at[shift - 1]))
    for copy in copies:
        copy.start()
    for copy in copies:
        copy.wait()


def pick(where, hidden_rows):
    return pl.pallas_call(
        pick_kernel,
        out_shape=[jax.ShapeDtypeStruct((BLOCK, 2048), jnp.float32)] * 3,
        in_specs=[SMEM, ANY],
        out_specs=[VMEM] * 3,
        scratch_shapes=[pltpu.SemaphoreType.DMA((3,))],
        compiler_params=pltpu.CompilerParams(vmem_limit_bytes=LIMIT),
        name="pick",
    )(where, hidden_rows)


def pick_keys_kernel(where, keys, values, out, sem):
    y = where[1]
    copies = []
    for to in range(NZ):
        for index, cache in enumerate((keys, values)):
            part = cache.at[
                pl.ds(pl.multiple_of(y * BLOCK, BLOCK), BLOCK), pl.ds((to // 2) * HD, HD)
            ]
            copies.append(pltpu.make_async_copy(part, out.at[to, index], sem.at[2 * to + index]))
    for copy in copies:
        copy.start()
    for copy in copies:
        copy.wait()


def pick_keys(where, key_cache, value_cache):
    return pl.pallas_call(
        pick_keys_kernel,
        out_shape=jax.ShapeDtypeStruct((NZ, 2, BLOCK, HD), jnp.float32),
        in_specs=[SMEM, ANY, ANY],
        out_specs=VMEM,
        scratch_shapes=[pltpu.SemaphoreType.DMA((2 * NZ,))],
        compiler_params=pltpu.CompilerParams(vmem_limit_bytes=56 << 20),
        cost_estimate=pl.CostEstimate(flops=0, bytes_accessed=64 << 20, transcendentals=0),
        name="pick_keys",
    )(where, key_cache, value_cache)


def project_kernel(where, rows, first, second, third, weights, *refs):
    outs, (left_buf, right_buf, total_buf, sems) = refs[:NX], refs[NX:]
    x, k = where[0], where[2]
    copies = []
    for y in range(NY):
        own = rows.at[
            pl.ds(pl.multiple_of(k * BLOCK, BLOCK), BLOCK),
            pl.ds(pl.multiple_of(x * 2048 + y * 512, 512), 512),
        ]
        parts = [own] + [part.at[:, pl.ds(y * 512, 512)] for part in (first, second, third)]
        group = [
            pltpu.make_async_copy(
                part, left_buf.at[y, lax.rem(x + NX - shift, NX)], sems.at[y, shift]
            )
            for shift, part in enumerate(parts)
        ]
        group.append(
            pltpu.make_async_copy(weights.at[pl.ds(2 * y, 2)], right_buf.at[y], sems.at[y, NX])
        )
        for copy in group:
            copy.start()
        copies.append(group)
    totals = [None, None]
    for y in range(NY):
        for copy in copies[y]:
            copy.wait()
        left = split(left_buf[y].reshape(NX * BLOCK, 512))
        for core in range(NK):
            term = dot3(left, split(right_buf[y, core]), MM)
            totals[core] = term if totals[core] is None else totals[core] + term
    for core in range(NK):
        for b in range(2):
            total_buf[2 * core + b] = totals[core][:, b * HD : (b + 1) * HD]
    for shift in range(NX):
        outs[shift][...] = total_buf[lax.rem(x + shift, NX)]


def project(where, rows, moved, weights):
    return pl.pallas_call(
        project_kernel,
        out_shape=[jax.ShapeDtypeStruct((NX * BLOCK, HD), jnp.float32)] * NX,
        in_specs=[SMEM] + [ANY] * 5,
        out_specs=[VMEM] * NX,
        scratch_shapes=[
            pltpu.VMEM((NY, NX, BLOCK, 512), jnp.float32),
            pltpu.VMEM((NY, NK, 512, 256), jnp.float32),
            pltpu.VMEM((NX, NX * BLOCK, HD), jnp.float32),
            pltpu.SemaphoreType.DMA((NY, NX + 1)),
        ],
        compiler_params=pltpu.CompilerParams(vmem_limit_bytes=LIMIT),
        cost_estimate=pl.CostEstimate(
            flops=6 * 256 * 2048 * 512, bytes_accessed=7 << 20, transcendentals=0
        ),
        name="project",
    )(where, rows, *moved, weights)


def attend_kernel(first, second, third, fourth, low, up, gathered, out, kv, scores, sem):
    tiles = gathered.shape[0]
    copies = [
        pltpu.make_async_copy(gathered.at[tile], kv.at[tile], sem.at[tile])
        for tile in range(tiles)
    ]
    for copy in copies:
        copy.start()
    width = NZ * BLOCK
    row = lax.broadcasted_iota(jnp.int32, (BLOCK, width), 0)
    col = lax.broadcasted_iota(jnp.int32, (BLOCK, width), 1)
    lower = row >= lax.rem(col, BLOCK)
    query = (first[...] + second[...]) + (third[...] + fourth[...])
    high, low_part = split(query * (math.log2(math.e) / math.sqrt(HD)))
    both = jnp.concatenate([high, low_part], axis=1)
    top = None
    for tile in range(tiles):
        copies[tile].wait()
        key_high, key_low = split(kv[tile, :, 0].reshape(width, HD))
        s = dot(both, jnp.concatenate([key_high, key_high], axis=1), MT)
        s = s + dot(high, key_low, MT)
        cols = slice(tile * width, (tile + 1) * width)
        bias = jnp.concatenate(
            [
                jnp.where(lower, low[b : b + 1, cols], up[b : b + 1, cols])
                for b in range(NX)
            ],
            axis=0,
        )
        s = s + bias
        scores[tile] = s
        top = s if top is None else jnp.maximum(top, s)
    top = jnp.max(top, axis=1, keepdims=True)
    total, summed = None, None
    for tile in range(tiles):
        weight = jnp.exp2(scores[tile] - top)
        weight_high, weight_low = split(weight)
        value_high, value_low = split(kv[tile, :, 1].reshape(width, HD))
        term = dot(weight_high, jnp.concatenate([value_high, value_low], axis=1), MM)
        term = term[:, :HD] + (term[:, HD:] + dot(weight_low, value_high, MM))
        total = weight if total is None else total + weight
        summed = term if summed is None else summed + term
    attended = summed / jnp.sum(total, axis=1, keepdims=True)
    for z in range(NZ):
        out[z] = attended


def attend(partial, low, up, gathered):
    rows = NX * BLOCK
    return pl.pallas_call(
        attend_kernel,
        out_shape=jax.ShapeDtypeStruct((NZ, rows, HD), jnp.float32),
        in_specs=[VMEM] * 6 + [ANY],
        out_specs=VMEM,
        scratch_shapes=[
            pltpu.VMEM((8, NZ, 2, BLOCK, HD), jnp.float32),
            pltpu.VMEM((8, rows, NZ * BLOCK), jnp.float32),
            pltpu.SemaphoreType.DMA((8,)),
        ],
        compiler_params=pltpu.CompilerParams(vmem_limit_bytes=LIMIT),
        cost_estimate=pl.CostEstimate(
            flops=12 * 256 * 4096 * HD, bytes_accessed=6 << 20, transcendentals=256 * 4096
        ),
        name="attend",
    )(*partial, low, up, gathered)


def mix_kernel(where, heads, weights, *refs):
    outs, (total_buf, buf, sem) = refs[:NX], refs[NX:]
    steps = NZ // 2
    copies = []
    for step in range(steps):
        copies.append(
            [
                pltpu.make_async_copy(
                    weights.at[part, pl.ds(2 * step, 2)], buf.at[step, part], sem.at[step, part]
                )
                for part in range(8)
            ]
        )
        for copy in copies[step]:
            copy.start()
    totals = [None, None]
    for step in range(steps):
        left = split(jnp.concatenate([heads[2 * step], heads[2 * step + 1]], axis=1))
        for copy in copies[step]:
            copy.wait()
        for core in range(NK):
            right = jnp.concatenate(
                [buf[step, :, z, core].reshape(HD, 512) for z in range(2)], axis=0
            )
            term = dot3(left, split(right), MM)
            totals[core] = term if totals[core] is None else totals[core] + term
    for core in range(NK):
        for x in range(NX):
            total_buf[x, core] = totals[core][x * BLOCK : (x + 1) * BLOCK]
    for shift in range(NX):
        outs[shift][...] = total_buf[lax.rem(where[0] + shift, NX)]


def mix(where, heads, weights):
    return pl.pallas_call(
        mix_kernel,
        out_shape=[jax.ShapeDtypeStruct((NK, BLOCK, 512), jnp.float32)] * NX,
        in_specs=[SMEM, VMEM, ANY],
        out_specs=[VMEM] * NX,
        scratch_shapes=[
            pltpu.VMEM((NX, NK, BLOCK, 512), jnp.float32),
            pltpu.VMEM((NZ // 2, 8, 2, NK, 16, 512), jnp.float32),
            pltpu.SemaphoreType.DMA((NZ // 2, 8)),
        ],
        compiler_params=pltpu.CompilerParams(vmem_limit_bytes=LIMIT),
        cost_estimate=pl.CostEstimate(
            flops=6 * 256 * 1024 * 1024, bytes_accessed=6 << 20, transcendentals=0
        ),
        name="mix",
    )(where, heads, weights)


def allowed_rows(
    head, key_block, query_block, vertical_blocks, vertical_count, slash_offsets, slash_count
):
    slots = jnp.arange(vertical_blocks.shape[1], dtype=jnp.int32)
    verticals = jnp.where(slots < vertical_count[head], vertical_blocks[head], -1)
    slashes = jnp.where(slots < slash_count[head], slash_offsets[head], -1)
    offset = query_block[:, None] - key_block[None, :]
    vert = jnp.any(key_block[:, None] == verticals[None, :], axis=1)[None, :]
    low_slash = jnp.any(offset[:, :, None] == slashes, axis=2)
    up_slash = jnp.any((offset - 1)[:, :, None] == slashes, axis=2)
    low = (offset >= 0) & (vert | low_slash)
    up = (offset >= 1) & (vert | up_slash)
    bias = jnp.where(jnp.stack([low, up]), 0.0, -jnp.inf)
    bias = jnp.repeat(bias, BLOCK, axis=2)
    return bias[0], bias[1]


CORES = [(0, 1), (1, 0)]


def along(axis, value, shift):
    count = lax.axis_size(axis)
    return lax.ppermute(value, axis, [(i, (i + shift) % count) for i in range(count)])


def shards(
    hidden_rows,
    query_weight,
    key_cache,
    value_cache,
    vertical_blocks,
    vertical_count,
    slash_offsets,
    slash_count,
    output_weight,
):
    x, y, z, k = (lax.axis_index(name) for name in ALL)
    where = jnp.stack([x, y, k]).astype(jnp.int32)
    weights = lax.all_gather(query_weight, ("y", "k"), axis=0)
    picked = pick(where, hidden_rows)
    hidden = [along("x", piece, shift) for shift, piece in enumerate(picked, 1)]
    behind, picked = lax.optimization_barrier((where, picked))
    near = lax.all_to_all(pick_keys(behind, key_cache, value_cache), "z", 0, 0)
    rows = output_weight.reshape(2, NY, NK, 16, 512)
    kept = lax.dynamic_index_in_dim(rows, k, 2, keepdims=False)
    given = lax.dynamic_index_in_dim(rows, 1 - k, 2, keepdims=False)
    taken = lax.ppermute(given, "k", CORES)
    rows = jnp.where(k == 0, jnp.stack([kept, taken]), jnp.stack([taken, kept]))
    rows, near, hidden = lax.optimization_barrier((rows, near, hidden))
    rows = lax.all_to_all(rows.reshape(NX * NY, 16, 512), ("x", "y"), 0, 0)
    kv = lax.all_gather(near, ("y", "k"), axis=0)
    key_block = jnp.arange(NY, dtype=jnp.int32)[:, None, None]
    key_block = key_block + 4 * jnp.arange(NK, dtype=jnp.int32)[None, :, None]
    key_block = key_block + 8 * jnp.arange(NZ, dtype=jnp.int32)[None, None, :]
    low, up = allowed_rows(
        4 * z + x,
        key_block.reshape(-1),
        32 + 8 * jnp.arange(NX, dtype=jnp.int32) + 2 * y + k,
        vertical_blocks,
        vertical_count,
        slash_offsets,
        slash_count,
    )
    partial = project(where, hidden_rows, hidden, weights)
    rows, partial, low, up = lax.optimization_barrier((rows, partial, low, up))
    partial = [partial[0]] + [along("x", partial[s], s) for s in range(1, NX)]
    rows = lax.all_to_all(rows.reshape(NZ, NK, 16, 512), "z", 0, 0)
    out_weight = lax.all_gather(rows, ("y", "k"), axis=0)
    heads = attend(partial, low, up, kv)
    heads = lax.all_to_all(heads, "z", 0, 0)
    mixed = mix(where, heads, out_weight)
    mixed = [mixed[0]] + [along("x", mixed[s], s) for s in range(1, NX)]
    mixed = (mixed[0] + mixed[1]) + (mixed[2] + mixed[3])
    own = lax.dynamic_index_in_dim(mixed, k, 0, keepdims=False)
    other = lax.dynamic_index_in_dim(mixed, 1 - k, 0, keepdims=False)
    other = lax.ppermute(other, "k", CORES)
    return jnp.concatenate([jnp.where(k == 0, own, other), jnp.where(k == 0, other, own)])


def solution(mesh):
    grid = Mesh(mesh.devices.reshape(NX, NY, NZ, NK), ALL)
    outer, ctx = ("x", "y"), ("z", "k")
    placed = (
        P(outer, None),
        P(outer, ctx),
        P(ctx, None),
        P(ctx, None),
        P(),
        P(),
        P(),
        P(),
        P(ctx, outer),
    )
    return jax.shard_map(
        shards, mesh=grid, in_specs=placed, out_specs=P(outer, ctx), check_vma=False
    )
```

```python
import math

import jax
import jax.numpy as jnp
from jax import lax
from jax.experimental import pallas as pl
from jax.experimental.pallas import tpu as pltpu
from jax.sharding import Mesh
from jax.sharding import PartitionSpec as P

HD = 128
BLOCK = 64
NX, NY, NZ, NK = 4, 4, 8, 2
ALL = ("x", "y", "z", "k")
VMEM = pl.BlockSpec(memory_space=pltpu.VMEM)
SMEM = pl.BlockSpec(memory_space=pltpu.SMEM)
ANY = pl.BlockSpec(memory_space=pl.ANY)
LIMIT = 60 << 20


def split(value):
    high = value.astype(jnp.bfloat16)
    low = (value - high.astype(jnp.float32)).astype(jnp.bfloat16)
    return high, low


def dot(left, right, dims):
    return lax.dot_general(left, right, dims, preferred_element_type=jnp.float32)


def dot3(left, right, dims):
    (lh, ll), (rh, rl) = left, right
    return dot(lh, rh, dims) + (dot(lh, rl, dims) + dot(ll, rh, dims))


MM = (((1,), (0,)), ((), ()))
MT = (((1,), (1,)), ((), ()))


def pick_kernel(where, rows, *refs):
    outs, sem = refs[:3], refs[3]
    x, k = where[0], where[2]
    copies = []
    for shift in range(1, NX):
        cols = pl.multiple_of(lax.rem(x + shift, NX) * 2048, 2048)
        part = rows.at[pl.ds(pl.multiple_of(k * BLOCK, BLOCK), BLOCK), pl.ds(cols, 2048)]
        copies.append(pltpu.make_async_copy(part, outs[shift - 1], sem.at[shift - 1]))
    for copy in copies:
        copy.start()
    for copy in copies:
        copy.wait()


def pick(where, hidden_rows):
    return pl.pallas_call(
        pick_kernel,
        out_shape=[jax.ShapeDtypeStruct((BLOCK, 2048), jnp.float32)] * 3,
        in_specs=[SMEM, ANY],
        out_specs=[VMEM] * 3,
        scratch_shapes=[pltpu.SemaphoreType.DMA((3,))],
        compiler_params=pltpu.CompilerParams(vmem_limit_bytes=LIMIT),
        name="pick",
    )(where, hidden_rows)


def pick_keys_kernel(where, keys, values, out, sem):
    y = where[1]
    copies = []
    for to in range(NZ):
        for index, cache in enumerate((keys, values)):
            part = cache.at[
                pl.ds(pl.multiple_of(y * BLOCK, BLOCK), BLOCK), pl.ds((to // 2) * HD, HD)
            ]
            copies.append(pltpu.make_async_copy(part, out.at[to, index], sem.at[2 * to + index]))
    for copy in copies:
        copy.start()
    for copy in copies:
        copy.wait()


def pick_keys(where, key_cache, value_cache):
    return pl.pallas_call(
        pick_keys_kernel,
        out_shape=jax.ShapeDtypeStruct((NZ, 2, BLOCK, HD), jnp.float32),
        in_specs=[SMEM, ANY, ANY],
        out_specs=VMEM,
        scratch_shapes=[pltpu.SemaphoreType.DMA((2 * NZ,))],
        compiler_params=pltpu.CompilerParams(vmem_limit_bytes=56 << 20),
        cost_estimate=pl.CostEstimate(flops=0, bytes_accessed=64 << 20, transcendentals=0),
        name="pick_keys",
    )(where, key_cache, value_cache)


def project_kernel(where, rows, first, second, third, weights, *refs):
    outs, (left_buf, right_buf, total_buf, sems) = refs[:NX], refs[NX:]
    x, k = where[0], where[2]
    copies = []
    for y in range(NY):
        own = rows.at[
            pl.ds(pl.multiple_of(k * BLOCK, BLOCK), BLOCK),
            pl.ds(pl.multiple_of(x * 2048 + y * 512, 512), 512),
        ]
        parts = [own] + [part.at[:, pl.ds(y * 512, 512)] for part in (first, second, third)]
        group = [
            pltpu.make_async_copy(
                part, left_buf.at[y, lax.rem(x + NX - shift, NX)], sems.at[y, shift]
            )
            for shift, part in enumerate(parts)
        ]
        group.append(
            pltpu.make_async_copy(weights.at[pl.ds(2 * y, 2)], right_buf.at[y], sems.at[y, NX])
        )
        for copy in group:
            copy.start()
        copies.append(group)
    totals = [None, None]
    for y in range(NY):
        for copy in copies[y]:
            copy.wait()
        left = split(left_buf[y].reshape(NX * BLOCK, 512))
        for core in range(NK):
            term = dot3(left, split(right_buf[y, core]), MM)
            totals[core] = term if totals[core] is None else totals[core] + term
    for core in range(NK):
        for b in range(2):
            total_buf[2 * core + b] = totals[core][:, b * HD : (b + 1) * HD]
    for shift in range(NX):
        outs[shift][...] = total_buf[lax.rem(x + shift, NX)]


def project(where, rows, moved, weights):
    return pl.pallas_call(
        project_kernel,
        out_shape=[jax.ShapeDtypeStruct((NX * BLOCK, HD), jnp.float32)] * NX,
        in_specs=[SMEM] + [ANY] * 5,
        out_specs=[VMEM] * NX,
        scratch_shapes=[
            pltpu.VMEM((NY, NX, BLOCK, 512), jnp.float32),
            pltpu.VMEM((NY, NK, 512, 256), jnp.float32),
            pltpu.VMEM((NX, NX * BLOCK, HD), jnp.float32),
            pltpu.SemaphoreType.DMA((NY, NX + 1)),
        ],
        compiler_params=pltpu.CompilerParams(vmem_limit_bytes=LIMIT),
        cost_estimate=pl.CostEstimate(
            flops=6 * 256 * 2048 * 512, bytes_accessed=7 << 20, transcendentals=0
        ),
        name="project",
    )(where, rows, *moved, weights)


def attend_kernel(first, second, third, fourth, low, up, gathered, out, kv, scores, sem):
    tiles = gathered.shape[0]
    copies = [
        pltpu.make_async_copy(gathered.at[tile], kv.at[tile], sem.at[tile])
        for tile in range(tiles)
    ]
    for copy in copies:
        copy.start()
    width = NZ * BLOCK
    row = lax.broadcasted_iota(jnp.int32, (BLOCK, width), 0)
    col = lax.broadcasted_iota(jnp.int32, (BLOCK, width), 1)
    lower = row >= lax.rem(col, BLOCK)
    query = (first[...] + second[...]) + (third[...] + fourth[...])
    high, low_part = split(query * (math.log2(math.e) / math.sqrt(HD)))
    both = jnp.concatenate([high, low_part], axis=1)
    top = None
    for tile in range(tiles):
        copies[tile].wait()
        key_high, key_low = split(kv[tile, :, 0].reshape(width, HD))
        s = dot(both, jnp.concatenate([key_high, key_high], axis=1), MT)
        s = s + dot(high, key_low, MT)
        cols = slice(tile * width, (tile + 1) * width)
        bias = jnp.concatenate(
            [
                jnp.where(lower, low[b : b + 1, cols], up[b : b + 1, cols])
                for b in range(NX)
            ],
            axis=0,
        )
        s = s + bias
        scores[tile] = s
        top = s if top is None else jnp.maximum(top, s)
    top = jnp.max(top, axis=1, keepdims=True)
    total, summed = None, None
    for tile in range(tiles):
        weight = jnp.exp2(scores[tile] - top)
        weight_high, weight_low = split(weight)
        value_high, value_low = split(kv[tile, :, 1].reshape(width, HD))
        term = dot(weight_high, jnp.concatenate([value_high, value_low], axis=1), MM)
        term = term[:, :HD] + (term[:, HD:] + dot(weight_low, value_high, MM))
        total = weight if total is None else total + weight
        summed = term if summed is None else summed + term
    attended = summed / jnp.sum(total, axis=1, keepdims=True)
    for z in range(NZ):
        out[z] = attended


def attend(partial, low, up, gathered):
    rows = NX * BLOCK
    return pl.pallas_call(
        attend_kernel,
        out_shape=jax.ShapeDtypeStruct((NZ, rows, HD), jnp.float32),
        in_specs=[VMEM] * 6 + [ANY],
        out_specs=VMEM,
        scratch_shapes=[
            pltpu.VMEM((8, NZ, 2, BLOCK, HD), jnp.float32),
            pltpu.VMEM((8, rows, NZ * BLOCK), jnp.float32),
            pltpu.SemaphoreType.DMA((8,)),
        ],
        compiler_params=pltpu.CompilerParams(vmem_limit_bytes=LIMIT),
        cost_estimate=pl.CostEstimate(
            flops=12 * 256 * 4096 * HD, bytes_accessed=6 << 20, transcendentals=256 * 4096
        ),
        name="attend",
    )(*partial, low, up, gathered)


def mix_kernel(where, heads, weights, *refs):
    outs, total_buf = refs[:NX], refs[NX]
    totals = [None, None]
    for step in range(NZ // 2):
        left = split(jnp.concatenate([heads[2 * step], heads[2 * step + 1]], axis=1))
        for core in range(NK):
            right = jnp.concatenate(
                [weights[:, 2 * step + z, core].reshape(HD, 512) for z in range(2)], axis=0
            )
            term = dot3(left, split(right), MM)
            totals[core] = term if totals[core] is None else totals[core] + term
    for core in range(NK):
        for x in range(NX):
            total_buf[x, core] = totals[core][x * BLOCK : (x + 1) * BLOCK]
    for shift in range(NX):
        outs[shift][...] = total_buf[lax.rem(where[0] + shift, NX)]


def mix(where, heads, weights):
    return pl.pallas_call(
        mix_kernel,
        out_shape=[jax.ShapeDtypeStruct((NK, BLOCK, 512), jnp.float32)] * NX,
        in_specs=[SMEM, VMEM, VMEM],
        out_specs=[VMEM] * NX,
        scratch_shapes=[pltpu.VMEM((NX, NK, BLOCK, 512), jnp.float32)],
        compiler_params=pltpu.CompilerParams(vmem_limit_bytes=24 << 20),
        cost_estimate=pl.CostEstimate(
            flops=6 * 256 * 1024 * 1024, bytes_accessed=6 << 20, transcendentals=0
        ),
        name="mix",
    )(where, heads, weights)


def allowed_rows(
    head, key_block, query_block, vertical_blocks, vertical_count, slash_offsets, slash_count
):
    slots = jnp.arange(vertical_blocks.shape[1], dtype=jnp.int32)
    verticals = jnp.where(slots < vertical_count[head], vertical_blocks[head], -1)
    slashes = jnp.where(slots < slash_count[head], slash_offsets[head], -1)
    offset = query_block[:, None] - key_block[None, :]
    vert = jnp.any(key_block[:, None] == verticals[None, :], axis=1)[None, :]
    low_slash = jnp.any(offset[:, :, None] == slashes, axis=2)
    up_slash = jnp.any((offset - 1)[:, :, None] == slashes, axis=2)
    low = (offset >= 0) & (vert | low_slash)
    up = (offset >= 1) & (vert | up_slash)
    bias = jnp.where(jnp.stack([low, up]), 0.0, -jnp.inf)
    bias = jnp.repeat(bias, BLOCK, axis=2)
    return bias[0], bias[1]


CORES = [(0, 1), (1, 0)]


def along(axis, value, shift):
    count = lax.axis_size(axis)
    return lax.ppermute(value, axis, [(i, (i + shift) % count) for i in range(count)])


def shards(
    hidden_rows,
    query_weight,
    key_cache,
    value_cache,
    vertical_blocks,
    vertical_count,
    slash_offsets,
    slash_count,
    output_weight,
):
    x, y, z, k = (lax.axis_index(name) for name in ALL)
    where = jnp.stack([x, y, k]).astype(jnp.int32)
    weights = lax.all_gather(query_weight, ("y", "k"), axis=0)
    picked = pick(where, hidden_rows)
    hidden = [along("x", piece, shift) for shift, piece in enumerate(picked, 1)]
    behind, picked = lax.optimization_barrier((where, picked))
    near = lax.all_to_all(pick_keys(behind, key_cache, value_cache), "z", 0, 0)
    rows = output_weight.reshape(2, NY, NK, 16, 512)
    kept = lax.dynamic_index_in_dim(rows, k, 2, keepdims=False)
    given = lax.dynamic_index_in_dim(rows, 1 - k, 2, keepdims=False)
    taken = lax.ppermute(given, "k", CORES)
    rows = jnp.where(k == 0, jnp.stack([kept, taken]), jnp.stack([taken, kept]))
    rows, near, hidden = lax.optimization_barrier((rows, near, hidden))
    rows = lax.all_to_all(rows.reshape(NX * NY, 16, 512), ("x", "y"), 0, 0)
    kv = lax.all_gather(near, ("y", "k"), axis=0)
    key_block = jnp.arange(NY, dtype=jnp.int32)[:, None, None]
    key_block = key_block + 4 * jnp.arange(NK, dtype=jnp.int32)[None, :, None]
    key_block = key_block + 8 * jnp.arange(NZ, dtype=jnp.int32)[None, None, :]
    low, up = allowed_rows(
        4 * z + x,
        key_block.reshape(-1),
        32 + 8 * jnp.arange(NX, dtype=jnp.int32) + 2 * y + k,
        vertical_blocks,
        vertical_count,
        slash_offsets,
        slash_count,
    )
    partial = project(where, hidden_rows, hidden, weights)
    partial = [partial[0]] + [along("x", partial[s], s) for s in range(1, NX)]
    rows, partial, low, up = lax.optimization_barrier((rows, partial, low, up))
    rows = lax.all_to_all(rows.reshape(NZ, NK, 16, 512), "z", 0, 0)
    out_weight = lax.all_gather(rows, ("y", "k"), axis=0)
    heads = attend(partial, low, up, kv)
    heads = lax.all_to_all(heads, "z", 0, 0)
    mixed = mix(where, heads, out_weight)
    mixed = [mixed[0]] + [along("x", mixed[s], s) for s in range(1, NX)]
    mixed = (mixed[0] + mixed[1]) + (mixed[2] + mixed[3])
    own = lax.dynamic_index_in_dim(mixed, k, 0, keepdims=False)
    other = lax.dynamic_index_in_dim(mixed, 1 - k, 0, keepdims=False)
    other = lax.ppermute(other, "k", CORES)
    return jnp.concatenate([jnp.where(k == 0, own, other), jnp.where(k == 0, other, own)])


def solution(mesh):
    grid = Mesh(mesh.devices.reshape(NX, NY, NZ, NK), ALL)
    outer, ctx = ("x", "y"), ("z", "k")
    placed = (
        P(outer, None),
        P(outer, ctx),
        P(ctx, None),
        P(ctx, None),
        P(),
        P(),
        P(),
        P(),
        P(ctx, outer),
    )
    return jax.shard_map(
        shards, mesh=grid, in_specs=placed, out_specs=P(outer, ctx), check_vma=False
    )
```

```python
import math

import jax
import jax.numpy as jnp
from jax import lax
from jax.experimental import pallas as pl
from jax.experimental.pallas import tpu as pltpu
from jax.sharding import Mesh
from jax.sharding import PartitionSpec as P

HD = 128
BLOCK = 64
NX, NY, NZ, NK = 4, 4, 8, 2
ALL = ("x", "y", "z", "k")
VMEM = pl.BlockSpec(memory_space=pltpu.VMEM)
SMEM = pl.BlockSpec(memory_space=pltpu.SMEM)
ANY = pl.BlockSpec(memory_space=pl.ANY)
LIMIT = 60 << 20


def split(value):
    high = value.astype(jnp.bfloat16)
    low = (value - high.astype(jnp.float32)).astype(jnp.bfloat16)
    return high, low


def dot(left, right, dims):
    return lax.dot_general(left, right, dims, preferred_element_type=jnp.float32)


def dot3(left, right, dims):
    (lh, ll), (rh, rl) = left, right
    return dot(lh, rh, dims) + (dot(lh, rl, dims) + dot(ll, rh, dims))


MM = (((1,), (0,)), ((), ()))
MT = (((1,), (1,)), ((), ()))


def pick_kernel(where, rows, *refs):
    outs, sem = refs[:3], refs[3]
    x, k = where[0], where[2]
    copies = []
    for shift in range(1, NX):
        cols = pl.multiple_of(lax.rem(x + shift, NX) * 2048, 2048)
        part = rows.at[pl.ds(pl.multiple_of(k * BLOCK, BLOCK), BLOCK), pl.ds(cols, 2048)]
        copies.append(pltpu.make_async_copy(part, outs[shift - 1], sem.at[shift - 1]))
    for copy in copies:
        copy.start()
    for copy in copies:
        copy.wait()


def pick(where, hidden_rows):
    return pl.pallas_call(
        pick_kernel,
        out_shape=[jax.ShapeDtypeStruct((BLOCK, 2048), jnp.float32)] * 3,
        in_specs=[SMEM, ANY],
        out_specs=[VMEM] * 3,
        scratch_shapes=[pltpu.SemaphoreType.DMA((3,))],
        compiler_params=pltpu.CompilerParams(vmem_limit_bytes=LIMIT),
        name="pick",
    )(where, hidden_rows)


def pick_keys_kernel(where, keys, values, *refs):
    outs, sem = refs[:NZ], refs[NZ]
    y, z = where[1], where[3]
    copies = []
    for shift in range(NZ):
        head = lax.rem(z + shift, NZ) // 2
        for index, cache in enumerate((keys, values)):
            part = cache.at[
                pl.ds(pl.multiple_of(y * BLOCK, BLOCK), BLOCK),
                pl.ds(pl.multiple_of(head * HD, HD), HD),
            ]
            copies.append(
                pltpu.make_async_copy(part, outs[shift].at[index], sem.at[2 * shift + index])
            )
    for copy in copies:
        copy.start()
    for copy in copies:
        copy.wait()


def pick_keys(where, key_cache, value_cache):
    return pl.pallas_call(
        pick_keys_kernel,
        out_shape=[jax.ShapeDtypeStruct((2, BLOCK, HD), jnp.float32)] * NZ,
        in_specs=[SMEM, ANY, ANY],
        out_specs=[VMEM] * NZ,
        scratch_shapes=[pltpu.SemaphoreType.DMA((2 * NZ,))],
        compiler_params=pltpu.CompilerParams(vmem_limit_bytes=56 << 20),
        cost_estimate=pl.CostEstimate(flops=0, bytes_accessed=64 << 20, transcendentals=0),
        name="pick_keys",
    )(where, key_cache, value_cache)


def project_kernel(where, rows, first, second, third, weights, *refs):
    outs, (left_buf, right_buf, total_buf, sems) = refs[:NX], refs[NX:]
    x, k = where[0], where[2]
    copies = []
    for y in range(NY):
        own = rows.at[
            pl.ds(pl.multiple_of(k * BLOCK, BLOCK), BLOCK),
            pl.ds(pl.multiple_of(x * 2048 + y * 512, 512), 512),
        ]
        parts = [own] + [part.at[:, pl.ds(y * 512, 512)] for part in (first, second, third)]
        group = [
            pltpu.make_async_copy(
                part, left_buf.at[y, lax.rem(x + NX - shift, NX)], sems.at[y, shift]
            )
            for shift, part in enumerate(parts)
        ]
        group.append(
            pltpu.make_async_copy(weights.at[pl.ds(2 * y, 2)], right_buf.at[y], sems.at[y, NX])
        )
        for copy in group:
            copy.start()
        copies.append(group)
    totals = [None, None]
    for y in range(NY):
        for copy in copies[y]:
            copy.wait()
        left = split(left_buf[y].reshape(NX * BLOCK, 512))
        for core in range(NK):
            term = dot3(left, split(right_buf[y, core]), MM)
            totals[core] = term if totals[core] is None else totals[core] + term
    for core in range(NK):
        for b in range(2):
            total_buf[2 * core + b] = totals[core][:, b * HD : (b + 1) * HD]
    for shift in range(NX):
        outs[shift][...] = total_buf[lax.rem(x + shift, NX)]


def project(where, rows, moved, weights):
    return pl.pallas_call(
        project_kernel,
        out_shape=[jax.ShapeDtypeStruct((NX * BLOCK, HD), jnp.float32)] * NX,
        in_specs=[SMEM] + [ANY] * 5,
        out_specs=[VMEM] * NX,
        scratch_shapes=[
            pltpu.VMEM((NY, NX, BLOCK, 512), jnp.float32),
            pltpu.VMEM((NY, NK, 512, 256), jnp.float32),
            pltpu.VMEM((NX, NX * BLOCK, HD), jnp.float32),
            pltpu.SemaphoreType.DMA((NY, NX + 1)),
        ],
        compiler_params=pltpu.CompilerParams(vmem_limit_bytes=LIMIT),
        cost_estimate=pl.CostEstimate(
            flops=6 * 256 * 2048 * 512, bytes_accessed=7 << 20, transcendentals=0
        ),
        name="project",
    )(where, rows, *moved, weights)


def attend_kernel(first, second, third, fourth, low, up, gathered, out, kv, scores, sem):
    tiles = gathered.shape[0]
    copies = [
        pltpu.make_async_copy(gathered.at[tile], kv.at[tile], sem.at[tile])
        for tile in range(tiles)
    ]
    for copy in copies:
        copy.start()
    width = NZ * BLOCK
    row = lax.broadcasted_iota(jnp.int32, (BLOCK, width), 0)
    col = lax.broadcasted_iota(jnp.int32, (BLOCK, width), 1)
    lower = row >= lax.rem(col, BLOCK)
    query = (first[...] + second[...]) + (third[...] + fourth[...])
    high, low_part = split(query * (math.log2(math.e) / math.sqrt(HD)))
    both = jnp.concatenate([high, low_part], axis=1)
    top = None
    for tile in range(tiles):
        copies[tile].wait()
        key_high, key_low = split(kv[tile, :, 0].reshape(width, HD))
        s = dot(both, jnp.concatenate([key_high, key_high], axis=1), MT)
        s = s + dot(high, key_low, MT)
        cols = slice(tile * width, (tile + 1) * width)
        bias = jnp.concatenate(
            [
                jnp.where(lower, low[b : b + 1, cols], up[b : b + 1, cols])
                for b in range(NX)
            ],
            axis=0,
        )
        s = s + bias
        scores[tile] = s
        top = s if top is None else jnp.maximum(top, s)
    top = jnp.max(top, axis=1, keepdims=True)
    total, summed = None, None
    for tile in range(tiles):
        weight = jnp.exp2(scores[tile] - top)
        weight_high, weight_low = split(weight)
        value_high, value_low = split(kv[tile, :, 1].reshape(width, HD))
        term = dot(weight_high, jnp.concatenate([value_high, value_low], axis=1), MM)
        term = term[:, :HD] + (term[:, HD:] + dot(weight_low, value_high, MM))
        total = weight if total is None else total + weight
        summed = term if summed is None else summed + term
    attended = summed / jnp.sum(total, axis=1, keepdims=True)
    for z in range(NZ):
        out[z] = attended


def attend(partial, low, up, gathered):
    rows = NX * BLOCK
    return pl.pallas_call(
        attend_kernel,
        out_shape=jax.ShapeDtypeStruct((NZ, rows, HD), jnp.float32),
        in_specs=[VMEM] * 6 + [ANY],
        out_specs=VMEM,
        scratch_shapes=[
            pltpu.VMEM((8, NZ, 2, BLOCK, HD), jnp.float32),
            pltpu.VMEM((8, rows, NZ * BLOCK), jnp.float32),
            pltpu.SemaphoreType.DMA((8,)),
        ],
        compiler_params=pltpu.CompilerParams(vmem_limit_bytes=LIMIT),
        cost_estimate=pl.CostEstimate(
            flops=12 * 256 * 4096 * HD, bytes_accessed=6 << 20, transcendentals=256 * 4096
        ),
        name="attend",
    )(*partial, low, up, gathered)


def mix_kernel(where, heads, weights, *refs):
    outs, total_buf = refs[:NX], refs[NX]
    totals = [None, None]
    for step in range(NZ // 2):
        left = split(jnp.concatenate([heads[2 * step], heads[2 * step + 1]], axis=1))
        for core in range(NK):
            right = jnp.concatenate(
                [weights[:, 2 * step + z, core].reshape(HD, 512) for z in range(2)], axis=0
            )
            term = dot3(left, split(right), MM)
            totals[core] = term if totals[core] is None else totals[core] + term
    for core in range(NK):
        for x in range(NX):
            total_buf[x, core] = totals[core][x * BLOCK : (x + 1) * BLOCK]
    for shift in range(NX):
        outs[shift][...] = total_buf[lax.rem(where[0] + shift, NX)]


def mix(where, heads, weights):
    return pl.pallas_call(
        mix_kernel,
        out_shape=[jax.ShapeDtypeStruct((NK, BLOCK, 512), jnp.float32)] * NX,
        in_specs=[SMEM, VMEM, VMEM],
        out_specs=[VMEM] * NX,
        scratch_shapes=[pltpu.VMEM((NX, NK, BLOCK, 512), jnp.float32)],
        compiler_params=pltpu.CompilerParams(vmem_limit_bytes=24 << 20),
        cost_estimate=pl.CostEstimate(
            flops=6 * 256 * 1024 * 1024, bytes_accessed=6 << 20, transcendentals=0
        ),
        name="mix",
    )(where, heads, weights)


def allowed_rows(
    head, key_block, query_block, vertical_blocks, vertical_count, slash_offsets, slash_count
):
    slots = jnp.arange(vertical_blocks.shape[1], dtype=jnp.int32)
    verticals = jnp.where(slots < vertical_count[head], vertical_blocks[head], -1)
    slashes = jnp.where(slots < slash_count[head], slash_offsets[head], -1)
    offset = query_block[:, None] - key_block[None, :]
    vert = jnp.any(key_block[:, None] == verticals[None, :], axis=1)[None, :]
    low_slash = jnp.any(offset[:, :, None] == slashes, axis=2)
    up_slash = jnp.any((offset - 1)[:, :, None] == slashes, axis=2)
    low = (offset >= 0) & (vert | low_slash)
    up = (offset >= 1) & (vert | up_slash)
    bias = jnp.where(jnp.stack([low, up]), 0.0, -jnp.inf)
    bias = jnp.repeat(bias, BLOCK, axis=2)
    return bias[0], bias[1]


CORES = [(0, 1), (1, 0)]


def along(axis, value, shift):
    count = lax.axis_size(axis)
    return lax.ppermute(value, axis, [(i, (i + shift) % count) for i in range(count)])


def shards(
    hidden_rows,
    query_weight,
    key_cache,
    value_cache,
    vertical_blocks,
    vertical_count,
    slash_offsets,
    slash_count,
    output_weight,
):
    x, y, z, k = (lax.axis_index(name) for name in ALL)
    where = jnp.stack([x, y, k, z]).astype(jnp.int32)
    weights = lax.all_gather(query_weight, ("y", "k"), axis=0)
    picked = pick(where, hidden_rows)
    hidden = [along("x", piece, shift) for shift, piece in enumerate(picked, 1)]
    behind, picked = lax.optimization_barrier((where, picked))
    near = pick_keys(behind, key_cache, value_cache)
    near = jnp.stack([near[0]] + [along("z", near[s], s) for s in range(1, NZ)])
    rows = output_weight.reshape(2, NY, NK, 16, 512)
    kept = lax.dynamic_index_in_dim(rows, k, 2, keepdims=False)
    given = lax.dynamic_index_in_dim(rows, 1 - k, 2, keepdims=False)
    taken = lax.ppermute(given, "k", CORES)
    rows = jnp.where(k == 0, jnp.stack([kept, taken]), jnp.stack([taken, kept]))
    rows, near, hidden = lax.optimization_barrier((rows, near, hidden))
    rows = lax.all_to_all(rows.reshape(NX * NY, 16, 512), ("x", "y"), 0, 0)
    kv = lax.all_gather(near, ("y", "k"), axis=0)
    key_block = jnp.arange(NY, dtype=jnp.int32)[:, None, None]
    key_block = key_block + 4 * jnp.arange(NK, dtype=jnp.int32)[None, :, None]
    key_block = key_block + 8 * ((z - jnp.arange(NZ, dtype=jnp.int32))[None, None, :] % NZ)
    low, up = allowed_rows(
        4 * z + x,
        key_block.reshape(-1),
        32 + 8 * jnp.arange(NX, dtype=jnp.int32) + 2 * y + k,
        vertical_blocks,
        vertical_count,
        slash_offsets,
        slash_count,
    )
    partial = project(where, hidden_rows, hidden, weights)
    partial = [partial[0]] + [along("x", partial[s], s) for s in range(1, NX)]
    rows, partial, low, up = lax.optimization_barrier((rows, partial, low, up))
    rows = lax.all_to_all(rows.reshape(NZ, NK, 16, 512), "z", 0, 0)
    out_weight = lax.all_gather(rows, ("y", "k"), axis=0)
    heads = attend(partial, low, up, kv)
    heads = lax.all_to_all(heads, "z", 0, 0)
    mixed = mix(where, heads, out_weight)
    mixed = [mixed[0]] + [along("x", mixed[s], s) for s in range(1, NX)]
    mixed = (mixed[0] + mixed[1]) + (mixed[2] + mixed[3])
    own = lax.dynamic_index_in_dim(mixed, k, 0, keepdims=False)
    other = lax.dynamic_index_in_dim(mixed, 1 - k, 0, keepdims=False)
    other = lax.ppermute(other, "k", CORES)
    return jnp.concatenate([jnp.where(k == 0, own, other), jnp.where(k == 0, other, own)])


def solution(mesh):
    grid = Mesh(mesh.devices.reshape(NX, NY, NZ, NK), ALL)
    outer, ctx = ("x", "y"), ("z", "k")
    placed = (
        P(outer, None),
        P(outer, ctx),
        P(ctx, None),
        P(ctx, None),
        P(),
        P(),
        P(),
        P(),
        P(ctx, outer),
    )
    return jax.shard_map(
        shards, mesh=grid, in_specs=placed, out_specs=P(outer, ctx), check_vma=False
    )
```

```python
import math

import jax
import jax.numpy as jnp
from jax import lax
from jax.experimental import pallas as pl
from jax.experimental.pallas import tpu as pltpu
from jax.sharding import Mesh
from jax.sharding import PartitionSpec as P

HD = 128
BLOCK = 64
NX, NY, NZ, NK = 4, 4, 8, 2
ALL = ("x", "y", "z", "k")
VMEM = pl.BlockSpec(memory_space=pltpu.VMEM)
SMEM = pl.BlockSpec(memory_space=pltpu.SMEM)
ANY = pl.BlockSpec(memory_space=pl.ANY)
LIMIT = 60 << 20


def split(value):
    high = value.astype(jnp.bfloat16)
    low = (value - high.astype(jnp.float32)).astype(jnp.bfloat16)
    return high, low


def dot(left, right, dims):
    return lax.dot_general(left, right, dims, preferred_element_type=jnp.float32)


def dot3(left, right, dims):
    (lh, ll), (rh, rl) = left, right
    return dot(lh, rh, dims) + (dot(lh, rl, dims) + dot(ll, rh, dims))


MM = (((1,), (0,)), ((), ()))
MT = (((1,), (1,)), ((), ()))


def pick_kernel(where, rows, *refs):
    outs, sem = refs[:3], refs[3]
    x, k = where[0], where[2]
    copies = []
    for shift in range(1, NX):
        cols = pl.multiple_of(lax.rem(x + shift, NX) * 2048, 2048)
        part = rows.at[pl.ds(pl.multiple_of(k * BLOCK, BLOCK), BLOCK), pl.ds(cols, 2048)]
        copies.append(pltpu.make_async_copy(part, outs[shift - 1], sem.at[shift - 1]))
    for copy in copies:
        copy.start()
    for copy in copies:
        copy.wait()


def pick(where, hidden_rows):
    return pl.pallas_call(
        pick_kernel,
        out_shape=[jax.ShapeDtypeStruct((BLOCK, 2048), jnp.float32)] * 3,
        in_specs=[SMEM, ANY],
        out_specs=[VMEM] * 3,
        scratch_shapes=[pltpu.SemaphoreType.DMA((3,))],
        compiler_params=pltpu.CompilerParams(vmem_limit_bytes=LIMIT),
        name="pick",
    )(where, hidden_rows)


def pick_keys_kernel(where, keys, values, *refs):
    outs, sem = refs[: NZ // 2], refs[NZ // 2]
    y, z = where[1], where[3]
    copies = []
    for turn in range(NZ // 2):
        head = lax.rem(z + 2 * turn, NZ) // 2
        for index, cache in enumerate((keys, values)):
            part = cache.at[
                pl.ds(pl.multiple_of(y * BLOCK, BLOCK), BLOCK),
                pl.ds(pl.multiple_of(head * HD, HD), HD),
            ]
            copies.append(
                pltpu.make_async_copy(part, outs[turn].at[index], sem.at[2 * turn + index])
            )
    for copy in copies:
        copy.start()
    for copy in copies:
        copy.wait()


def pick_keys(where, key_cache, value_cache):
    return pl.pallas_call(
        pick_keys_kernel,
        out_shape=[jax.ShapeDtypeStruct((2, BLOCK, HD), jnp.float32)] * (NZ // 2),
        in_specs=[SMEM, ANY, ANY],
        out_specs=[VMEM] * (NZ // 2),
        scratch_shapes=[pltpu.SemaphoreType.DMA((NZ,))],
        compiler_params=pltpu.CompilerParams(vmem_limit_bytes=56 << 20),
        cost_estimate=pl.CostEstimate(flops=0, bytes_accessed=64 << 20, transcendentals=0),
        name="pick_keys",
    )(where, key_cache, value_cache)


def project_kernel(where, rows, first, second, third, weights, *refs):
    outs, (left_buf, right_buf, total_buf, sems) = refs[:NX], refs[NX:]
    x, k = where[0], where[2]
    copies = []
    for y in range(NY):
        own = rows.at[
            pl.ds(pl.multiple_of(k * BLOCK, BLOCK), BLOCK),
            pl.ds(pl.multiple_of(x * 2048 + y * 512, 512), 512),
        ]
        parts = [own] + [part.at[:, pl.ds(y * 512, 512)] for part in (first, second, third)]
        group = [
            pltpu.make_async_copy(
                part, left_buf.at[y, lax.rem(x + NX - shift, NX)], sems.at[y, shift]
            )
            for shift, part in enumerate(parts)
        ]
        group.append(
            pltpu.make_async_copy(weights.at[pl.ds(2 * y, 2)], right_buf.at[y], sems.at[y, NX])
        )
        for copy in group:
            copy.start()
        copies.append(group)
    totals = [None, None]
    for y in range(NY):
        for copy in copies[y]:
            copy.wait()
        left = split(left_buf[y].reshape(NX * BLOCK, 512))
        for core in range(NK):
            term = dot3(left, split(right_buf[y, core]), MM)
            totals[core] = term if totals[core] is None else totals[core] + term
    for core in range(NK):
        for b in range(2):
            total_buf[2 * core + b] = totals[core][:, b * HD : (b + 1) * HD]
    for shift in range(NX):
        outs[shift][...] = total_buf[lax.rem(x + shift, NX)]


def project(where, rows, moved, weights):
    return pl.pallas_call(
        project_kernel,
        out_shape=[jax.ShapeDtypeStruct((NX * BLOCK, HD), jnp.float32)] * NX,
        in_specs=[SMEM] + [ANY] * 5,
        out_specs=[VMEM] * NX,
        scratch_shapes=[
            pltpu.VMEM((NY, NX, BLOCK, 512), jnp.float32),
            pltpu.VMEM((NY, NK, 512, 256), jnp.float32),
            pltpu.VMEM((NX, NX * BLOCK, HD), jnp.float32),
            pltpu.SemaphoreType.DMA((NY, NX + 1)),
        ],
        compiler_params=pltpu.CompilerParams(vmem_limit_bytes=LIMIT),
        cost_estimate=pl.CostEstimate(
            flops=6 * 256 * 2048 * 512, bytes_accessed=7 << 20, transcendentals=0
        ),
        name="project",
    )(where, rows, *moved, weights)


def attend_kernel(first, second, third, fourth, low, up, gathered, out, kv, scores, sem):
    tiles = gathered.shape[0]
    copies = [
        pltpu.make_async_copy(gathered.at[tile], kv.at[tile], sem.at[tile])
        for tile in range(tiles)
    ]
    for copy in copies:
        copy.start()
    width = NZ * BLOCK
    row = lax.broadcasted_iota(jnp.int32, (BLOCK, width), 0)
    col = lax.broadcasted_iota(jnp.int32, (BLOCK, width), 1)
    lower = row >= lax.rem(col, BLOCK)
    query = (first[...] + second[...]) + (third[...] + fourth[...])
    high, low_part = split(query * (math.log2(math.e) / math.sqrt(HD)))
    both = jnp.concatenate([high, low_part], axis=1)
    top = None
    for tile in range(tiles):
        copies[tile].wait()
        key_high, key_low = split(kv[tile, :, 0].reshape(width, HD))
        s = dot(both, jnp.concatenate([key_high, key_high], axis=1), MT)
        s = s + dot(high, key_low, MT)
        cols = slice(tile * width, (tile + 1) * width)
        bias = jnp.concatenate(
            [
                jnp.where(lower, low[b : b + 1, cols], up[b : b + 1, cols])
                for b in range(NX)
            ],
            axis=0,
        )
        s = s + bias
        scores[tile] = s
        top = s if top is None else jnp.maximum(top, s)
    top = jnp.max(top, axis=1, keepdims=True)
    total, summed = None, None
    for tile in range(tiles):
        weight = jnp.exp2(scores[tile] - top)
        weight_high, weight_low = split(weight)
        value_high, value_low = split(kv[tile, :, 1].reshape(width, HD))
        term = dot(weight_high, jnp.concatenate([value_high, value_low], axis=1), MM)
        term = term[:, :HD] + (term[:, HD:] + dot(weight_low, value_high, MM))
        total = weight if total is None else total + weight
        summed = term if summed is None else summed + term
    attended = summed / jnp.sum(total, axis=1, keepdims=True)
    for z in range(NZ):
        out[z] = attended


def attend(partial, low, up, gathered):
    rows = NX * BLOCK
    return pl.pallas_call(
        attend_kernel,
        out_shape=jax.ShapeDtypeStruct((NZ, rows, HD), jnp.float32),
        in_specs=[VMEM] * 6 + [ANY],
        out_specs=VMEM,
        scratch_shapes=[
            pltpu.VMEM((8, NZ, 2, BLOCK, HD), jnp.float32),
            pltpu.VMEM((8, rows, NZ * BLOCK), jnp.float32),
            pltpu.SemaphoreType.DMA((8,)),
        ],
        compiler_params=pltpu.CompilerParams(vmem_limit_bytes=LIMIT),
        cost_estimate=pl.CostEstimate(
            flops=12 * 256 * 4096 * HD, bytes_accessed=6 << 20, transcendentals=256 * 4096
        ),
        name="attend",
    )(*partial, low, up, gathered)


def mix_kernel(where, heads, weights, *refs):
    outs, total_buf = refs[:NX], refs[NX]
    totals = [None, None]
    for step in range(NZ // 2):
        left = split(jnp.concatenate([heads[2 * step], heads[2 * step + 1]], axis=1))
        for core in range(NK):
            right = jnp.concatenate(
                [weights[:, 2 * step + z, core].reshape(HD, 512) for z in range(2)], axis=0
            )
            term = dot3(left, split(right), MM)
            totals[core] = term if totals[core] is None else totals[core] + term
    for core in range(NK):
        for x in range(NX):
            total_buf[x, core] = totals[core][x * BLOCK : (x + 1) * BLOCK]
    for shift in range(NX):
        outs[shift][...] = total_buf[lax.rem(where[0] + shift, NX)]


def mix(where, heads, weights):
    return pl.pallas_call(
        mix_kernel,
        out_shape=[jax.ShapeDtypeStruct((NK, BLOCK, 512), jnp.float32)] * NX,
        in_specs=[SMEM, VMEM, VMEM],
        out_specs=[VMEM] * NX,
        scratch_shapes=[pltpu.VMEM((NX, NK, BLOCK, 512), jnp.float32)],
        compiler_params=pltpu.CompilerParams(vmem_limit_bytes=24 << 20),
        cost_estimate=pl.CostEstimate(
            flops=6 * 256 * 1024 * 1024, bytes_accessed=6 << 20, transcendentals=0
        ),
        name="mix",
    )(where, heads, weights)


def allowed_rows(
    head, key_block, query_block, vertical_blocks, vertical_count, slash_offsets, slash_count
):
    slots = jnp.arange(vertical_blocks.shape[1], dtype=jnp.int32)
    verticals = jnp.where(slots < vertical_count[head], vertical_blocks[head], -1)
    slashes = jnp.where(slots < slash_count[head], slash_offsets[head], -1)
    offset = query_block[:, None] - key_block[None, :]
    vert = jnp.any(key_block[:, None] == verticals[None, :], axis=1)[None, :]
    low_slash = jnp.any(offset[:, :, None] == slashes, axis=2)
    up_slash = jnp.any((offset - 1)[:, :, None] == slashes, axis=2)
    low = (offset >= 0) & (vert | low_slash)
    up = (offset >= 1) & (vert | up_slash)
    bias = jnp.where(jnp.stack([low, up]), 0.0, -jnp.inf)
    bias = jnp.repeat(bias, BLOCK, axis=2)
    return bias[0], bias[1]


CORES = [(0, 1), (1, 0)]


def along(axis, value, shift):
    count = lax.axis_size(axis)
    return lax.ppermute(value, axis, [(i, (i + shift) % count) for i in range(count)])


def shards(
    hidden_rows,
    query_weight,
    key_cache,
    value_cache,
    vertical_blocks,
    vertical_count,
    slash_offsets,
    slash_count,
    output_weight,
):
    x, y, z, k = (lax.axis_index(name) for name in ALL)
    where = jnp.stack([x, y, k, z]).astype(jnp.int32)
    weights = lax.all_gather(query_weight, ("y", "k"), axis=0)
    picked = pick(where, hidden_rows)
    hidden = [along("x", piece, shift) for shift, piece in enumerate(picked, 1)]
    behind, picked = lax.optimization_barrier((where, picked))
    near = pick_keys(behind, key_cache, value_cache)
    near = jnp.stack([near[0]] + [along("z", near[t], 2 * t) for t in range(1, NZ // 2)])
    near = jnp.concatenate([near, lax.ppermute(near, "z", [(i, i ^ 1) for i in range(NZ)])])
    rows = output_weight.reshape(2, NY, NK, 16, 512)
    kept = lax.dynamic_index_in_dim(rows, k, 2, keepdims=False)
    given = lax.dynamic_index_in_dim(rows, 1 - k, 2, keepdims=False)
    taken = lax.ppermute(given, "k", CORES)
    rows = jnp.where(k == 0, jnp.stack([kept, taken]), jnp.stack([taken, kept]))
    rows, near, hidden = lax.optimization_barrier((rows, near, hidden))
    rows = lax.all_to_all(rows.reshape(NX * NY, 16, 512), ("x", "y"), 0, 0)
    kv = lax.all_gather(near, ("y", "k"), axis=0)
    key_block = jnp.arange(NY, dtype=jnp.int32)[:, None, None]
    key_block = key_block + 4 * jnp.arange(NK, dtype=jnp.int32)[None, :, None]
    turns = 2 * jnp.arange(NZ // 2, dtype=jnp.int32)
    along_z = jnp.concatenate([z - turns, (z ^ 1) - turns]) % NZ
    key_block = key_block + 8 * along_z[None, None, :]
    low, up = allowed_rows(
        4 * z + x,
        key_block.reshape(-1),
        32 + 8 * jnp.arange(NX, dtype=jnp.int32) + 2 * y + k,
        vertical_blocks,
        vertical_count,
        slash_offsets,
        slash_count,
    )
    partial = project(where, hidden_rows, hidden, weights)
    partial = [partial[0]] + [along("x", partial[s], s) for s in range(1, NX)]
    rows, partial, low, up = lax.optimization_barrier((rows, partial, low, up))
    rows = lax.all_to_all(rows.reshape(NZ, NK, 16, 512), "z", 0, 0)
    out_weight = lax.all_gather(rows, ("y", "k"), axis=0)
    heads = attend(partial, low, up, kv)
    heads = lax.all_to_all(heads, "z", 0, 0)
    mixed = mix(where, heads, out_weight)
    mixed = [mixed[0]] + [along("x", mixed[s], s) for s in range(1, NX)]
    mixed = (mixed[0] + mixed[1]) + (mixed[2] + mixed[3])
    own = lax.dynamic_index_in_dim(mixed, k, 0, keepdims=False)
    other = lax.dynamic_index_in_dim(mixed, 1 - k, 0, keepdims=False)
    other = lax.ppermute(other, "k", CORES)
    return jnp.concatenate([jnp.where(k == 0, own, other), jnp.where(k == 0, other, own)])


def solution(mesh):
    grid = Mesh(mesh.devices.reshape(NX, NY, NZ, NK), ALL)
    outer, ctx = ("x", "y"), ("z", "k")
    placed = (
        P(outer, None),
        P(outer, ctx),
        P(ctx, None),
        P(ctx, None),
        P(),
        P(),
        P(),
        P(),
        P(ctx, outer),
    )
    return jax.shard_map(
        shards, mesh=grid, in_specs=placed, out_specs=P(outer, ctx), check_vma=False
    )
```

```python
import math

import jax
import jax.numpy as jnp
from jax import lax
from jax.experimental import pallas as pl
from jax.experimental.pallas import tpu as pltpu
from jax.sharding import Mesh
from jax.sharding import PartitionSpec as P

HD = 128
BLOCK = 64
NX, NY, NZ, NK = 4, 4, 8, 2
ALL = ("x", "y", "z", "k")
VMEM = pl.BlockSpec(memory_space=pltpu.VMEM)
SMEM = pl.BlockSpec(memory_space=pltpu.SMEM)
ANY = pl.BlockSpec(memory_space=pl.ANY)
LIMIT = 60 << 20


def split(value):
    high = value.astype(jnp.bfloat16)
    low = (value - high.astype(jnp.float32)).astype(jnp.bfloat16)
    return high, low


def dot(left, right, dims):
    return lax.dot_general(left, right, dims, preferred_element_type=jnp.float32)


def dot3(left, right, dims):
    (lh, ll), (rh, rl) = left, right
    return dot(lh, rh, dims) + (dot(lh, rl, dims) + dot(ll, rh, dims))


MM = (((1,), (0,)), ((), ()))
MT = (((1,), (1,)), ((), ()))


def pick_kernel(where, rows, *refs):
    outs, sem = refs[:3], refs[3]
    x, k = where[0], where[2]
    copies = []
    for shift in range(1, NX):
        cols = pl.multiple_of(lax.rem(x + shift, NX) * 2048, 2048)
        part = rows.at[pl.ds(pl.multiple_of(k * BLOCK, BLOCK), BLOCK), pl.ds(cols, 2048)]
        copies.append(pltpu.make_async_copy(part, outs[shift - 1], sem.at[shift - 1]))
    for copy in copies:
        copy.start()
    for copy in copies:
        copy.wait()


def pick(where, hidden_rows):
    return pl.pallas_call(
        pick_kernel,
        out_shape=[jax.ShapeDtypeStruct((BLOCK, 2048), jnp.float32)] * 3,
        in_specs=[SMEM, ANY],
        out_specs=[VMEM] * 3,
        scratch_shapes=[pltpu.SemaphoreType.DMA((3,))],
        compiler_params=pltpu.CompilerParams(vmem_limit_bytes=LIMIT),
        name="pick",
    )(where, hidden_rows)


def pick_keys_kernel(where, keys, values, *refs):
    outs, sem = refs[: NZ // 2], refs[NZ // 2]
    y, z = where[1], where[3]
    copies = []
    for turn in range(NZ // 2):
        head = lax.rem(z + 2 * turn, NZ) // 2
        for index, cache in enumerate((keys, values)):
            part = cache.at[
                pl.ds(pl.multiple_of(y * BLOCK, BLOCK), BLOCK),
                pl.ds(pl.multiple_of(head * HD, HD), HD),
            ]
            copies.append(
                pltpu.make_async_copy(part, outs[turn].at[index], sem.at[2 * turn + index])
            )
    for copy in copies:
        copy.start()
    for copy in copies:
        copy.wait()


def pick_keys(where, key_cache, value_cache):
    return pl.pallas_call(
        pick_keys_kernel,
        out_shape=[jax.ShapeDtypeStruct((2, BLOCK, HD), jnp.float32)] * (NZ // 2),
        in_specs=[SMEM, ANY, ANY],
        out_specs=[VMEM] * (NZ // 2),
        scratch_shapes=[pltpu.SemaphoreType.DMA((NZ,))],
        compiler_params=pltpu.CompilerParams(vmem_limit_bytes=56 << 20),
        cost_estimate=pl.CostEstimate(flops=0, bytes_accessed=64 << 20, transcendentals=0),
        name="pick_keys",
    )(where, key_cache, value_cache)


def project_kernel(where, rows, first, second, third, weights, *refs):
    outs, (left_buf, right_buf, total_buf, sems) = refs[:NX], refs[NX:]
    x, k = where[0], where[2]
    copies = []
    for y in range(NY):
        own = rows.at[
            pl.ds(pl.multiple_of(k * BLOCK, BLOCK), BLOCK),
            pl.ds(pl.multiple_of(x * 2048 + y * 512, 512), 512),
        ]
        parts = [own] + [part.at[:, pl.ds(y * 512, 512)] for part in (first, second, third)]
        group = [
            pltpu.make_async_copy(
                part, left_buf.at[y, lax.rem(x + NX - shift, NX)], sems.at[y, shift]
            )
            for shift, part in enumerate(parts)
        ]
        group.append(
            pltpu.make_async_copy(weights.at[pl.ds(2 * y, 2)], right_buf.at[y], sems.at[y, NX])
        )
        for copy in group:
            copy.start()
        copies.append(group)
    totals = [None, None]
    for y in range(NY):
        for copy in copies[y]:
            copy.wait()
        left = split(left_buf[y].reshape(NX * BLOCK, 512))
        for core in range(NK):
            term = dot3(left, split(right_buf[y, core]), MM)
            totals[core] = term if totals[core] is None else totals[core] + term
    for core in range(NK):
        for b in range(2):
            total_buf[2 * core + b] = totals[core][:, b * HD : (b + 1) * HD]
    for shift in range(NX):
        outs[shift][...] = total_buf[lax.rem(x + shift, NX)]


def project(where, rows, moved, weights):
    return pl.pallas_call(
        project_kernel,
        out_shape=[jax.ShapeDtypeStruct((NX * BLOCK, HD), jnp.float32)] * NX,
        in_specs=[SMEM] + [ANY] * 5,
        out_specs=[VMEM] * NX,
        scratch_shapes=[
            pltpu.VMEM((NY, NX, BLOCK, 512), jnp.float32),
            pltpu.VMEM((NY, NK, 512, 256), jnp.float32),
            pltpu.VMEM((NX, NX * BLOCK, HD), jnp.float32),
            pltpu.SemaphoreType.DMA((NY, NX + 1)),
        ],
        compiler_params=pltpu.CompilerParams(vmem_limit_bytes=LIMIT),
        cost_estimate=pl.CostEstimate(
            flops=6 * 256 * 2048 * 512, bytes_accessed=7 << 20, transcendentals=0
        ),
        name="project",
    )(where, rows, *moved, weights)


def attend_kernel(first, second, third, fourth, low, up, gathered, out, kv, scores, sem):
    tiles = gathered.shape[0]
    copies = [
        pltpu.make_async_copy(gathered.at[tile], kv.at[tile], sem.at[tile])
        for tile in range(tiles)
    ]
    for copy in copies:
        copy.start()
    width = NZ * BLOCK
    row = lax.broadcasted_iota(jnp.int32, (BLOCK, width), 0)
    col = lax.broadcasted_iota(jnp.int32, (BLOCK, width), 1)
    lower = row >= lax.rem(col, BLOCK)
    query = (first[...] + second[...]) + (third[...] + fourth[...])
    high, low_part = split(query * (math.log2(math.e) / math.sqrt(HD)))
    both = jnp.concatenate([high, low_part], axis=1)
    top = None
    for tile in range(tiles):
        copies[tile].wait()
        key_high, key_low = split(kv[tile, :, 0].reshape(width, HD))
        s = dot(both, jnp.concatenate([key_high, key_high], axis=1), MT)
        s = s + dot(high, key_low, MT)
        cols = slice(tile * width, (tile + 1) * width)
        bias = jnp.concatenate(
            [
                jnp.where(lower, low[b : b + 1, cols], up[b : b + 1, cols])
                for b in range(NX)
            ],
            axis=0,
        )
        s = s + bias
        scores[tile] = s
        top = s if top is None else jnp.maximum(top, s)
    top = jnp.max(top, axis=1, keepdims=True)
    total, summed = None, None
    for tile in range(tiles):
        weight = jnp.exp2(scores[tile] - top)
        weight_high, weight_low = split(weight)
        value_high, value_low = split(kv[tile, :, 1].reshape(width, HD))
        term = dot(weight_high, jnp.concatenate([value_high, value_low], axis=1), MM)
        term = term[:, :HD] + (term[:, HD:] + dot(weight_low, value_high, MM))
        total = weight if total is None else total + weight
        summed = term if summed is None else summed + term
    out[...] = summed / jnp.sum(total, axis=1, keepdims=True)


def attend(partial, low, up, gathered):
    rows = NX * BLOCK
    return pl.pallas_call(
        attend_kernel,
        out_shape=jax.ShapeDtypeStruct((rows, HD), jnp.float32),
        in_specs=[VMEM] * 6 + [ANY],
        out_specs=VMEM,
        scratch_shapes=[
            pltpu.VMEM((8, NZ, 2, BLOCK, HD), jnp.float32),
            pltpu.VMEM((8, rows, NZ * BLOCK), jnp.float32),
            pltpu.SemaphoreType.DMA((8,)),
        ],
        compiler_params=pltpu.CompilerParams(vmem_limit_bytes=LIMIT),
        cost_estimate=pl.CostEstimate(
            flops=12 * 256 * 4096 * HD, bytes_accessed=6 << 20, transcendentals=256 * 4096
        ),
        name="attend",
    )(*partial, low, up, gathered)


OFFSETS = (0, -1, 1, -2, 2, -3, 3, 4)


def mix_kernel(where, *refs):
    heads, weights, outs, total_buf = refs[:9], refs[9], refs[10 : 10 + NX], refs[10 + NX]
    blocks = [head[...] for head in heads[:7]]
    blocks.append(jnp.concatenate([heads[7][...], heads[8][...]], axis=0))
    places = [lax.rem(where[3] + offset + NZ, NZ) for offset in OFFSETS]
    totals = [None, None]
    for step in range(NZ // 2):
        left = split(jnp.concatenate(blocks[2 * step : 2 * step + 2], axis=1))
        for core in range(NK):
            right = jnp.concatenate(
                [
                    weights[:, spot, core].reshape(HD, 512)
                    for spot in places[2 * step : 2 * step + 2]
                ],
                axis=0,
            )
            term = dot3(left, split(right), MM)
            totals[core] = term if totals[core] is None else totals[core] + term
    for core in range(NK):
        for x in range(NX):
            total_buf[x, core] = totals[core][x * BLOCK : (x + 1) * BLOCK]
    for shift in range(NX):
        outs[shift][...] = total_buf[lax.rem(where[0] + shift, NX)]


def mix(where, heads, weights):
    return pl.pallas_call(
        mix_kernel,
        out_shape=[jax.ShapeDtypeStruct((NK, BLOCK, 512), jnp.float32)] * NX,
        in_specs=[SMEM] + [VMEM] * 10,
        out_specs=[VMEM] * NX,
        scratch_shapes=[pltpu.VMEM((NX, NK, BLOCK, 512), jnp.float32)],
        compiler_params=pltpu.CompilerParams(vmem_limit_bytes=24 << 20),
        cost_estimate=pl.CostEstimate(
            flops=6 * 256 * 1024 * 1024, bytes_accessed=6 << 20, transcendentals=0
        ),
        name="mix",
    )(where, *heads, weights)


def allowed_rows(
    head, key_block, query_block, vertical_blocks, vertical_count, slash_offsets, slash_count
):
    slots = jnp.arange(vertical_blocks.shape[1], dtype=jnp.int32)
    verticals = jnp.where(slots < vertical_count[head], vertical_blocks[head], -1)
    slashes = jnp.where(slots < slash_count[head], slash_offsets[head], -1)
    offset = query_block[:, None] - key_block[None, :]
    vert = jnp.any(key_block[:, None] == verticals[None, :], axis=1)[None, :]
    low_slash = jnp.any(offset[:, :, None] == slashes, axis=2)
    up_slash = jnp.any((offset - 1)[:, :, None] == slashes, axis=2)
    low = (offset >= 0) & (vert | low_slash)
    up = (offset >= 1) & (vert | up_slash)
    bias = jnp.where(jnp.stack([low, up]), 0.0, -jnp.inf)
    bias = jnp.repeat(bias, BLOCK, axis=2)
    return bias[0], bias[1]


CORES = [(0, 1), (1, 0)]


def along(axis, value, shift):
    count = lax.axis_size(axis)
    return lax.ppermute(value, axis, [(i, (i + shift) % count) for i in range(count)])


def shards(
    hidden_rows,
    query_weight,
    key_cache,
    value_cache,
    vertical_blocks,
    vertical_count,
    slash_offsets,
    slash_count,
    output_weight,
):
    x, y, z, k = (lax.axis_index(name) for name in ALL)
    where = jnp.stack([x, y, k, z]).astype(jnp.int32)
    weights = lax.all_gather(query_weight, ("y", "k"), axis=0)
    picked = pick(where, hidden_rows)
    hidden = [along("x", piece, shift) for shift, piece in enumerate(picked, 1)]
    behind, picked = lax.optimization_barrier((where, picked))
    near = pick_keys(behind, key_cache, value_cache)
    near = jnp.stack([near[0]] + [along("z", near[t], 2 * t) for t in range(1, NZ // 2)])
    near = jnp.concatenate([near, lax.ppermute(near, "z", [(i, i ^ 1) for i in range(NZ)])])
    rows = output_weight.reshape(2, NY, NK, 16, 512)
    kept = lax.dynamic_index_in_dim(rows, k, 2, keepdims=False)
    given = lax.dynamic_index_in_dim(rows, 1 - k, 2, keepdims=False)
    taken = lax.ppermute(given, "k", CORES)
    rows = jnp.where(k == 0, jnp.stack([kept, taken]), jnp.stack([taken, kept]))
    rows, near, hidden = lax.optimization_barrier((rows, near, hidden))
    rows = lax.all_to_all(rows.reshape(NX * NY, 16, 512), ("x", "y"), 0, 0)
    kv = lax.all_gather(near, ("y", "k"), axis=0)
    key_block = jnp.arange(NY, dtype=jnp.int32)[:, None, None]
    key_block = key_block + 4 * jnp.arange(NK, dtype=jnp.int32)[None, :, None]
    turns = 2 * jnp.arange(NZ // 2, dtype=jnp.int32)
    along_z = jnp.concatenate([z - turns, (z ^ 1) - turns]) % NZ
    key_block = key_block + 8 * along_z[None, None, :]
    low, up = allowed_rows(
        4 * z + x,
        key_block.reshape(-1),
        32 + 8 * jnp.arange(NX, dtype=jnp.int32) + 2 * y + k,
        vertical_blocks,
        vertical_count,
        slash_offsets,
        slash_count,
    )
    partial = project(where, hidden_rows, hidden, weights)
    partial = [partial[0]] + [along("x", partial[s], s) for s in range(1, NX)]
    rows, partial, low, up = lax.optimization_barrier((rows, partial, low, up))
    rows = lax.all_to_all(rows.reshape(NZ, NK, 16, 512), "z", 0, 0)
    out_weight = lax.all_gather(rows, ("y", "k"), axis=0)
    own = attend(partial, low, up, kv)
    near_up, near_down = along("z", own, 1), along("z", own, -1)
    far_up, far_down = along("z", own, 2), along("z", own, -2)
    heads = [own, near_up, near_down, far_up, far_down]
    heads += [along("z", far_up, 1), along("z", far_down, -1)]
    heads += [along("z", far_up[:128], 2), along("z", far_down[128:], -2)]
    mixed = mix(where, heads, out_weight)
    mixed = [mixed[0]] + [along("x", mixed[s], s) for s in range(1, NX)]
    first, second = (
        sum(lax.dynamic_index_in_dim(part, core, 0, keepdims=False) for part in mixed)
        for core in (1 - k, k)
    )
    other = lax.ppermute(first, "k", CORES)
    return jnp.concatenate(
        [jnp.where(k == 0, second, other), jnp.where(k == 0, other, second)]
    )


def solution(mesh):
    grid = Mesh(mesh.devices.reshape(NX, NY, NZ, NK), ALL)
    outer, ctx = ("x", "y"), ("z", "k")
    placed = (
        P(outer, None),
        P(outer, ctx),
        P(ctx, None),
        P(ctx, None),
        P(),
        P(),
        P(),
        P(),
        P(ctx, outer),
    )
    return jax.shard_map(
        shards, mesh=grid, in_specs=placed, out_specs=P(outer, ctx), check_vma=False
    )
```

```python
import math

import jax
import jax.numpy as jnp
from jax import lax
from jax.experimental import pallas as pl
from jax.experimental.pallas import tpu as pltpu
from jax.sharding import Mesh
from jax.sharding import PartitionSpec as P

HD = 128
BLOCK = 64
NX, NY, NZ, NK = 4, 4, 8, 2
ALL = ("x", "y", "z", "k")
VMEM = pl.BlockSpec(memory_space=pltpu.VMEM)
SMEM = pl.BlockSpec(memory_space=pltpu.SMEM)
ANY = pl.BlockSpec(memory_space=pl.ANY)
LIMIT = 60 << 20


def split(value):
    high = value.astype(jnp.bfloat16)
    low = (value - high.astype(jnp.float32)).astype(jnp.bfloat16)
    return high, low


def dot(left, right, dims):
    return lax.dot_general(left, right, dims, preferred_element_type=jnp.float32)


def dot3(left, right, dims):
    (lh, ll), (rh, rl) = left, right
    return dot(lh, rh, dims) + (dot(lh, rl, dims) + dot(ll, rh, dims))


MM = (((1,), (0,)), ((), ()))
MT = (((1,), (1,)), ((), ()))


def pick_kernel(where, rows, *refs):
    outs, sem = refs[:3], refs[3]
    x, k = where[0], where[2]
    copies = []
    for shift in range(1, NX):
        cols = pl.multiple_of(lax.rem(x + shift, NX) * 2048, 2048)
        part = rows.at[pl.ds(pl.multiple_of(k * BLOCK, BLOCK), BLOCK), pl.ds(cols, 2048)]
        copies.append(pltpu.make_async_copy(part, outs[shift - 1], sem.at[shift - 1]))
    for copy in copies:
        copy.start()
    for copy in copies:
        copy.wait()


def pick(where, hidden_rows):
    return pl.pallas_call(
        pick_kernel,
        out_shape=[jax.ShapeDtypeStruct((BLOCK, 2048), jnp.float32)] * 3,
        in_specs=[SMEM, ANY],
        out_specs=[VMEM] * 3,
        scratch_shapes=[pltpu.SemaphoreType.DMA((3,))],
        compiler_params=pltpu.CompilerParams(vmem_limit_bytes=LIMIT),
        name="pick",
    )(where, hidden_rows)


def pick_keys_kernel(where, keys, values, *refs):
    outs, sem = refs[: NZ // 2], refs[NZ // 2]
    y, z = where[1], where[3]
    copies = []
    for turn in range(NZ // 2):
        head = lax.rem(z + 2 * turn, NZ) // 2
        for index, cache in enumerate((keys, values)):
            part = cache.at[
                pl.ds(pl.multiple_of(y * BLOCK, BLOCK), BLOCK),
                pl.ds(pl.multiple_of(head * HD, HD), HD),
            ]
            copies.append(
                pltpu.make_async_copy(part, outs[turn].at[index], sem.at[2 * turn + index])
            )
    for copy in copies:
        copy.start()
    for copy in copies:
        copy.wait()


def pick_keys(where, key_cache, value_cache):
    return pl.pallas_call(
        pick_keys_kernel,
        out_shape=[jax.ShapeDtypeStruct((2, BLOCK, HD), jnp.float32)] * (NZ // 2),
        in_specs=[SMEM, ANY, ANY],
        out_specs=[VMEM] * (NZ // 2),
        scratch_shapes=[pltpu.SemaphoreType.DMA((NZ,))],
        compiler_params=pltpu.CompilerParams(vmem_limit_bytes=56 << 20),
        cost_estimate=pl.CostEstimate(flops=0, bytes_accessed=64 << 20, transcendentals=0),
        name="pick_keys",
    )(where, key_cache, value_cache)


def project_kernel(where, rows, first, second, third, weights, *refs):
    outs, (left_buf, right_buf, total_buf, sems) = refs[:NX], refs[NX:]
    x, k = where[0], where[2]
    copies = []
    for y in range(NY):
        own = rows.at[
            pl.ds(pl.multiple_of(k * BLOCK, BLOCK), BLOCK),
            pl.ds(pl.multiple_of(x * 2048 + y * 512, 512), 512),
        ]
        parts = [own] + [part.at[:, pl.ds(y * 512, 512)] for part in (first, second, third)]
        group = [
            pltpu.make_async_copy(
                part, left_buf.at[y, lax.rem(x + NX - shift, NX)], sems.at[y, shift]
            )
            for shift, part in enumerate(parts)
        ]
        group.append(
            pltpu.make_async_copy(weights.at[pl.ds(2 * y, 2)], right_buf.at[y], sems.at[y, NX])
        )
        for copy in group:
            copy.start()
        copies.append(group)
    totals = [None, None]
    for y in range(NY):
        for copy in copies[y]:
            copy.wait()
        left = split(left_buf[y].reshape(NX * BLOCK, 512))
        for core in range(NK):
            term = dot3(left, split(right_buf[y, core]), MM)
            totals[core] = term if totals[core] is None else totals[core] + term
    for core in range(NK):
        for b in range(2):
            total_buf[2 * core + b] = totals[core][:, b * HD : (b + 1) * HD]
    for shift in range(NX):
        outs[shift][...] = total_buf[lax.rem(x + shift, NX)]


def project(where, rows, moved, weights):
    return pl.pallas_call(
        project_kernel,
        out_shape=[jax.ShapeDtypeStruct((NX * BLOCK, HD), jnp.float32)] * NX,
        in_specs=[SMEM] + [ANY] * 5,
        out_specs=[VMEM] * NX,
        scratch_shapes=[
            pltpu.VMEM((NY, NX, BLOCK, 512), jnp.float32),
            pltpu.VMEM((NY, NK, 512, 256), jnp.float32),
            pltpu.VMEM((NX, NX * BLOCK, HD), jnp.float32),
            pltpu.SemaphoreType.DMA((NY, NX + 1)),
        ],
        compiler_params=pltpu.CompilerParams(vmem_limit_bytes=LIMIT),
        cost_estimate=pl.CostEstimate(
            flops=6 * 256 * 2048 * 512, bytes_accessed=7 << 20, transcendentals=0
        ),
        name="project",
    )(where, rows, *moved, weights)


def attend_kernel(first, second, third, fourth, low, up, gathered, out, kv, scores, sem):
    tiles = gathered.shape[0]
    copies = [
        pltpu.make_async_copy(gathered.at[tile], kv.at[tile], sem.at[tile])
        for tile in range(tiles)
    ]
    for copy in copies:
        copy.start()
    width = NZ * BLOCK
    row = lax.broadcasted_iota(jnp.int32, (BLOCK, width), 0)
    col = lax.broadcasted_iota(jnp.int32, (BLOCK, width), 1)
    lower = row >= lax.rem(col, BLOCK)
    query = (first[...] + second[...]) + (third[...] + fourth[...])
    high, low_part = split(query * (math.log2(math.e) / math.sqrt(HD)))
    both = jnp.concatenate([high, low_part], axis=1)
    top = None
    for tile in range(tiles):
        copies[tile].wait()
        key_high, key_low = split(kv[tile, :, 0].reshape(width, HD))
        s = dot(both, jnp.concatenate([key_high, key_high], axis=1), MT)
        s = s + dot(high, key_low, MT)
        cols = slice(tile * width, (tile + 1) * width)
        bias = jnp.concatenate(
            [
                jnp.where(lower, low[b : b + 1, cols], up[b : b + 1, cols])
                for b in range(NX)
            ],
            axis=0,
        )
        s = s + bias
        scores[tile] = s
        top = s if top is None else jnp.maximum(top, s)
    top = jnp.max(top, axis=1, keepdims=True)
    total, summed = None, None
    for tile in range(tiles):
        weight = jnp.exp2(scores[tile] - top)
        weight_high, weight_low = split(weight)
        value_high, value_low = split(kv[tile, :, 1].reshape(width, HD))
        term = dot(weight_high, jnp.concatenate([value_high, value_low], axis=1), MM)
        term = term[:, :HD] + (term[:, HD:] + dot(weight_low, value_high, MM))
        total = weight if total is None else total + weight
        summed = term if summed is None else summed + term
    out[...] = summed / jnp.sum(total, axis=1, keepdims=True)


def attend(partial, low, up, gathered):
    rows = NX * BLOCK
    return pl.pallas_call(
        attend_kernel,
        out_shape=jax.ShapeDtypeStruct((rows, HD), jnp.float32),
        in_specs=[VMEM] * 6 + [ANY],
        out_specs=VMEM,
        scratch_shapes=[
            pltpu.VMEM((8, NZ, 2, BLOCK, HD), jnp.float32),
            pltpu.VMEM((8, rows, NZ * BLOCK), jnp.float32),
            pltpu.SemaphoreType.DMA((8,)),
        ],
        compiler_params=pltpu.CompilerParams(vmem_limit_bytes=40 << 20),
        cost_estimate=pl.CostEstimate(
            flops=12 * 256 * 4096 * HD, bytes_accessed=6 << 20, transcendentals=256 * 4096
        ),
        name="attend",
    )(*partial, low, up, gathered)


OFFSETS = (0, -1, 1, -2, 2, -3, 3, 4)


def mix_kernel(where, *refs):
    heads, weights, outs = refs[:9], refs[9], refs[10 : 10 + NX]
    total_buf, buf, sems = refs[10 + NX :]
    places = [lax.rem(where[3] + offset + NZ, NZ) for offset in OFFSETS]
    copies = [
        [
            pltpu.make_async_copy(
                weights.at[part, spot], buf.at[index, :, pl.ds(16 * part, 16)], sems.at[index, part]
            )
            for part in range(8)
        ]
        for index, spot in enumerate(places)
    ]
    for group in copies:
        for copy in group:
            copy.start()
    blocks = [head[...] for head in heads[:7]]
    blocks.append(jnp.concatenate([heads[7][...], heads[8][...]], axis=0))
    totals = [None, None]
    for step in range(NZ // 2):
        pair = (2 * step, 2 * step + 1)
        left = split(jnp.concatenate([blocks[index] for index in pair], axis=1))
        for index in pair:
            for copy in copies[index]:
                copy.wait()
        for core in range(NK):
            right = jnp.concatenate([buf[index, core] for index in pair], axis=0)
            term = dot3(left, split(right), MM)
            totals[core] = term if totals[core] is None else totals[core] + term
    for core in range(NK):
        for x in range(NX):
            total_buf[x, core] = totals[core][x * BLOCK : (x + 1) * BLOCK]
    for shift in range(NX):
        outs[shift][...] = total_buf[lax.rem(where[0] + shift, NX)]


def mix(where, heads, weights):
    return pl.pallas_call(
        mix_kernel,
        out_shape=[jax.ShapeDtypeStruct((NK, BLOCK, 512), jnp.float32)] * NX,
        in_specs=[SMEM] + [VMEM] * 9 + [ANY],
        out_specs=[VMEM] * NX,
        scratch_shapes=[
            pltpu.VMEM((NX, NK, BLOCK, 512), jnp.float32),
            pltpu.VMEM((NZ, NK, HD, 512), jnp.float32),
            pltpu.SemaphoreType.DMA((NZ, 8)),
        ],
        compiler_params=pltpu.CompilerParams(vmem_limit_bytes=48 << 20),
        cost_estimate=pl.CostEstimate(
            flops=6 * 256 * 1024 * 1024, bytes_accessed=6 << 20, transcendentals=0
        ),
        name="mix",
    )(where, *heads, weights)


def allowed_rows(
    head, key_block, query_block, vertical_blocks, vertical_count, slash_offsets, slash_count
):
    slots = jnp.arange(vertical_blocks.shape[1], dtype=jnp.int32)
    verticals = jnp.where(slots < vertical_count[head], vertical_blocks[head], -1)
    slashes = jnp.where(slots < slash_count[head], slash_offsets[head], -1)
    offset = query_block[:, None] - key_block[None, :]
    vert = jnp.any(key_block[:, None] == verticals[None, :], axis=1)[None, :]
    low_slash = jnp.any(offset[:, :, None] == slashes, axis=2)
    up_slash = jnp.any((offset - 1)[:, :, None] == slashes, axis=2)
    low = (offset >= 0) & (vert | low_slash)
    up = (offset >= 1) & (vert | up_slash)
    bias = jnp.where(jnp.stack([low, up]), 0.0, -jnp.inf)
    bias = jnp.repeat(bias, BLOCK, axis=2)
    return bias[0], bias[1]


CORES = [(0, 1), (1, 0)]


def along(axis, value, shift):
    count = lax.axis_size(axis)
    return lax.ppermute(value, axis, [(i, (i + shift) % count) for i in range(count)])


def shards(
    hidden_rows,
    query_weight,
    key_cache,
    value_cache,
    vertical_blocks,
    vertical_count,
    slash_offsets,
    slash_count,
    output_weight,
):
    x, y, z, k = (lax.axis_index(name) for name in ALL)
    where = jnp.stack([x, y, k, z]).astype(jnp.int32)
    weights = lax.all_gather(query_weight, ("y", "k"), axis=0)
    picked = pick(where, hidden_rows)
    hidden = [along("x", piece, shift) for shift, piece in enumerate(picked, 1)]
    behind, picked = lax.optimization_barrier((where, picked))
    near = pick_keys(behind, key_cache, value_cache)
    near = jnp.stack([near[0]] + [along("z", near[t], 2 * t) for t in range(1, NZ // 2)])
    near = jnp.concatenate([near, lax.ppermute(near, "z", [(i, i ^ 1) for i in range(NZ)])])
    rows = output_weight.reshape(2, NY, NK, 16, 512)
    kept = lax.dynamic_index_in_dim(rows, k, 2, keepdims=False)
    given = lax.dynamic_index_in_dim(rows, 1 - k, 2, keepdims=False)
    taken = lax.ppermute(given, "k", CORES)
    rows = jnp.where(k == 0, jnp.stack([kept, taken]), jnp.stack([taken, kept]))
    rows, near, hidden = lax.optimization_barrier((rows, near, hidden))
    rows = lax.all_to_all(rows.reshape(NX * NY, 16, 512), ("x", "y"), 0, 0)
    kv = lax.all_gather(near, ("y", "k"), axis=0)
    key_block = jnp.arange(NY, dtype=jnp.int32)[:, None, None]
    key_block = key_block + 4 * jnp.arange(NK, dtype=jnp.int32)[None, :, None]
    turns = 2 * jnp.arange(NZ // 2, dtype=jnp.int32)
    along_z = jnp.concatenate([z - turns, (z ^ 1) - turns]) % NZ
    key_block = key_block + 8 * along_z[None, None, :]
    low, up = allowed_rows(
        4 * z + x,
        key_block.reshape(-1),
        32 + 8 * jnp.arange(NX, dtype=jnp.int32) + 2 * y + k,
        vertical_blocks,
        vertical_count,
        slash_offsets,
        slash_count,
    )
    partial = project(where, hidden_rows, hidden, weights)
    partial = [partial[0]] + [along("x", partial[s], s) for s in range(1, NX)]
    rows, partial, low, up = lax.optimization_barrier((rows, partial, low, up))
    rows = lax.all_to_all(rows.reshape(NZ, NK, 16, 512), "z", 0, 0)
    out_weight = lax.all_gather(rows, ("y", "k"), axis=0)
    own = attend(partial, low, up, kv)
    near_up, near_down = along("z", own, 1), along("z", own, -1)
    far_up, far_down = along("z", own, 2), along("z", own, -2)
    heads = [own, near_up, near_down, far_up, far_down]
    heads += [along("z", far_up, 1), along("z", far_down, -1)]
    heads += [along("z", far_up[:128], 2), along("z", far_down[128:], -2)]
    mixed = mix(where, heads, out_weight)
    mixed = [mixed[0]] + [along("x", mixed[s], s) for s in range(1, NX)]
    first, second = (
        sum(lax.dynamic_index_in_dim(part, core, 0, keepdims=False) for part in mixed)
        for core in (1 - k, k)
    )
    other = lax.ppermute(first, "k", CORES)
    return jnp.concatenate(
        [jnp.where(k == 0, second, other), jnp.where(k == 0, other, second)]
    )


def solution(mesh):
    grid = Mesh(mesh.devices.reshape(NX, NY, NZ, NK), ALL)
    outer, ctx = ("x", "y"), ("z", "k")
    placed = (
        P(outer, None),
        P(outer, ctx),
        P(ctx, None),
        P(ctx, None),
        P(),
        P(),
        P(),
        P(),
        P(ctx, outer),
    )
    return jax.shard_map(
        shards, mesh=grid, in_specs=placed, out_specs=P(outer, ctx), check_vma=False
    )
```

```python
import math

import jax
import jax.numpy as jnp
from jax import lax
from jax.experimental import pallas as pl
from jax.experimental.pallas import tpu as pltpu
from jax.sharding import Mesh
from jax.sharding import PartitionSpec as P

HD = 128
BLOCK = 64
NX, NY, NZ, NK = 4, 4, 8, 2
ALL = ("x", "y", "z", "k")
VMEM = pl.BlockSpec(memory_space=pltpu.VMEM)
SMEM = pl.BlockSpec(memory_space=pltpu.SMEM)
ANY = pl.BlockSpec(memory_space=pl.ANY)
LIMIT = 60 << 20


def split(value):
    high = value.astype(jnp.bfloat16)
    low = (value - high.astype(jnp.float32)).astype(jnp.bfloat16)
    return high, low


def dot(left, right, dims):
    return lax.dot_general(left, right, dims, preferred_element_type=jnp.float32)


def dot3(left, right, dims):
    (lh, ll), (rh, rl) = left, right
    return dot(lh, rh, dims) + (dot(lh, rl, dims) + dot(ll, rh, dims))


MM = (((1,), (0,)), ((), ()))
MT = (((1,), (1,)), ((), ()))


def pick_kernel(where, rows, *refs):
    outs, sem = refs[:3], refs[3]
    x, k = where[0], where[2]
    copies = []
    for shift in range(1, NX):
        cols = pl.multiple_of(lax.rem(x + shift, NX) * 2048, 2048)
        part = rows.at[pl.ds(pl.multiple_of(k * BLOCK, BLOCK), BLOCK), pl.ds(cols, 2048)]
        copies.append(pltpu.make_async_copy(part, outs[shift - 1], sem.at[shift - 1]))
    for copy in copies:
        copy.start()
    for copy in copies:
        copy.wait()


def pick(where, hidden_rows):
    return pl.pallas_call(
        pick_kernel,
        out_shape=[jax.ShapeDtypeStruct((BLOCK, 2048), jnp.float32)] * 3,
        in_specs=[SMEM, ANY],
        out_specs=[VMEM] * 3,
        scratch_shapes=[pltpu.SemaphoreType.DMA((3,))],
        compiler_params=pltpu.CompilerParams(vmem_limit_bytes=LIMIT),
        name="pick",
    )(where, hidden_rows)


def pick_keys_kernel(where, keys, values, *refs):
    outs, sem = refs[: NZ // 2], refs[NZ // 2]
    y, z = where[1], where[3]
    copies = []
    for turn in range(NZ // 2):
        head = lax.rem(z + 2 * turn, NZ) // 2
        for index, cache in enumerate((keys, values)):
            part = cache.at[
                pl.ds(pl.multiple_of(y * BLOCK, BLOCK), BLOCK),
                pl.ds(pl.multiple_of(head * HD, HD), HD),
            ]
            copies.append(
                pltpu.make_async_copy(part, outs[turn].at[index], sem.at[2 * turn + index])
            )
    for copy in copies:
        copy.start()
    for copy in copies:
        copy.wait()


def pick_keys(where, key_cache, value_cache):
    return pl.pallas_call(
        pick_keys_kernel,
        out_shape=[jax.ShapeDtypeStruct((2, BLOCK, HD), jnp.float32)] * (NZ // 2),
        in_specs=[SMEM, ANY, ANY],
        out_specs=[VMEM] * (NZ // 2),
        scratch_shapes=[pltpu.SemaphoreType.DMA((NZ,))],
        compiler_params=pltpu.CompilerParams(vmem_limit_bytes=56 << 20),
        cost_estimate=pl.CostEstimate(flops=0, bytes_accessed=64 << 20, transcendentals=0),
        name="pick_keys",
    )(where, key_cache, value_cache)


def project_kernel(where, rows, first, second, third, weights, *refs):
    outs, (left_buf, right_buf, total_buf, sems) = refs[:NX], refs[NX:]
    x, k = where[0], where[2]
    copies = []
    for y in range(NY):
        own = rows.at[
            pl.ds(pl.multiple_of(k * BLOCK, BLOCK), BLOCK),
            pl.ds(pl.multiple_of(x * 2048 + y * 512, 512), 512),
        ]
        parts = [own] + [part.at[:, pl.ds(y * 512, 512)] for part in (first, second, third)]
        group = [
            pltpu.make_async_copy(
                part, left_buf.at[y, lax.rem(x + NX - shift, NX)], sems.at[y, shift]
            )
            for shift, part in enumerate(parts)
        ]
        group.append(
            pltpu.make_async_copy(weights.at[pl.ds(2 * y, 2)], right_buf.at[y], sems.at[y, NX])
        )
        for copy in group:
            copy.start()
        copies.append(group)
    totals = [None, None]
    for y in range(NY):
        for copy in copies[y]:
            copy.wait()
        left = split(left_buf[y].reshape(NX * BLOCK, 512))
        for core in range(NK):
            term = dot3(left, split(right_buf[y, core]), MM)
            totals[core] = term if totals[core] is None else totals[core] + term
    for core in range(NK):
        for b in range(2):
            total_buf[2 * core + b] = totals[core][:, b * HD : (b + 1) * HD]
    for shift in range(NX):
        outs[shift][...] = total_buf[lax.rem(x + shift, NX)]


def project(where, rows, moved, weights):
    return pl.pallas_call(
        project_kernel,
        out_shape=[jax.ShapeDtypeStruct((NX * BLOCK, HD), jnp.float32)] * NX,
        in_specs=[SMEM] + [ANY] * 5,
        out_specs=[VMEM] * NX,
        scratch_shapes=[
            pltpu.VMEM((NY, NX, BLOCK, 512), jnp.float32),
            pltpu.VMEM((NY, NK, 512, 256), jnp.float32),
            pltpu.VMEM((NX, NX * BLOCK, HD), jnp.float32),
            pltpu.SemaphoreType.DMA((NY, NX + 1)),
        ],
        compiler_params=pltpu.CompilerParams(vmem_limit_bytes=48 << 20),
        cost_estimate=pl.CostEstimate(
            flops=6 * 256 * 2048 * 512, bytes_accessed=7 << 20, transcendentals=0
        ),
        name="project",
    )(where, rows, *moved, weights)


def attend_kernel(first, second, third, fourth, low, up, gathered, out, kv, scores, sem):
    tiles = gathered.shape[0]
    copies = [
        pltpu.make_async_copy(gathered.at[tile], kv.at[tile], sem.at[tile])
        for tile in range(tiles)
    ]
    for copy in copies:
        copy.start()
    width = NZ * BLOCK
    row = lax.broadcasted_iota(jnp.int32, (BLOCK, width), 0)
    col = lax.broadcasted_iota(jnp.int32, (BLOCK, width), 1)
    lower = row >= lax.rem(col, BLOCK)
    query = (first[...] + second[...]) + (third[...] + fourth[...])
    high, low_part = split(query * (math.log2(math.e) / math.sqrt(HD)))
    both = jnp.concatenate([high, low_part], axis=1)
    top = None
    for tile in range(tiles):
        copies[tile].wait()
        key_high, key_low = split(kv[tile, :, 0].reshape(width, HD))
        s = dot(both, jnp.concatenate([key_high, key_high], axis=1), MT)
        s = s + dot(high, key_low, MT)
        cols = slice(tile * width, (tile + 1) * width)
        bias = jnp.concatenate(
            [
                jnp.where(lower, low[b : b + 1, cols], up[b : b + 1, cols])
                for b in range(NX)
            ],
            axis=0,
        )
        s = s + bias
        scores[tile] = s
        top = s if top is None else jnp.maximum(top, s)
    top = jnp.max(top, axis=1, keepdims=True)
    total, summed = None, None
    for tile in range(tiles):
        weight = jnp.exp2(scores[tile] - top)
        weight_high, weight_low = split(weight)
        value_high, value_low = split(kv[tile, :, 1].reshape(width, HD))
        term = dot(weight_high, jnp.concatenate([value_high, value_low], axis=1), MM)
        term = term[:, :HD] + (term[:, HD:] + dot(weight_low, value_high, MM))
        total = weight if total is None else total + weight
        summed = term if summed is None else summed + term
    out[...] = summed / jnp.sum(total, axis=1, keepdims=True)


def attend(partial, low, up, gathered):
    rows = NX * BLOCK
    return pl.pallas_call(
        attend_kernel,
        out_shape=jax.ShapeDtypeStruct((rows, HD), jnp.float32),
        in_specs=[VMEM] * 6 + [ANY],
        out_specs=VMEM,
        scratch_shapes=[
            pltpu.VMEM((8, NZ, 2, BLOCK, HD), jnp.float32),
            pltpu.VMEM((8, rows, NZ * BLOCK), jnp.float32),
            pltpu.SemaphoreType.DMA((8,)),
        ],
        compiler_params=pltpu.CompilerParams(vmem_limit_bytes=40 << 20),
        cost_estimate=pl.CostEstimate(
            flops=12 * 256 * 4096 * HD, bytes_accessed=6 << 20, transcendentals=256 * 4096
        ),
        name="attend",
    )(*partial, low, up, gathered)


OFFSETS = (0, -1, 1, -2, 2, -3, 3, 4)


def mix_kernel(where, *refs):
    heads, weights, outs = refs[:9], refs[9], refs[10 : 10 + NX]
    total_buf, buf, sems = refs[10 + NX :]
    places = [lax.rem(where[3] + offset + NZ, NZ) for offset in OFFSETS]
    copies = [
        [
            pltpu.make_async_copy(
                weights.at[part, spot], buf.at[index, :, pl.ds(16 * part, 16)], sems.at[index, part]
            )
            for part in range(8)
        ]
        for index, spot in enumerate(places)
    ]
    for group in copies:
        for copy in group:
            copy.start()
    blocks = [head[...] for head in heads[:7]]
    blocks.append(jnp.concatenate([heads[7][...], heads[8][...]], axis=0))
    totals = [None, None]
    for step in range(NZ // 2):
        pair = (2 * step, 2 * step + 1)
        left = split(jnp.concatenate([blocks[index] for index in pair], axis=1))
        for index in pair:
            for copy in copies[index]:
                copy.wait()
        for core in range(NK):
            right = jnp.concatenate([buf[index, core] for index in pair], axis=0)
            term = dot3(left, split(right), MM)
            totals[core] = term if totals[core] is None else totals[core] + term
    for core in range(NK):
        for x in range(NX):
            total_buf[x, core] = totals[core][x * BLOCK : (x + 1) * BLOCK]
    for shift in range(NX):
        outs[shift][...] = total_buf[lax.rem(where[0] + shift, NX)]


def mix(where, heads, weights):
    return pl.pallas_call(
        mix_kernel,
        out_shape=[jax.ShapeDtypeStruct((NK, BLOCK, 512), jnp.float32)] * NX,
        in_specs=[SMEM] + [VMEM] * 9 + [ANY],
        out_specs=[VMEM] * NX,
        scratch_shapes=[
            pltpu.VMEM((NX, NK, BLOCK, 512), jnp.float32),
            pltpu.VMEM((NZ, NK, HD, 512), jnp.float32),
            pltpu.SemaphoreType.DMA((NZ, 8)),
        ],
        compiler_params=pltpu.CompilerParams(vmem_limit_bytes=48 << 20),
        cost_estimate=pl.CostEstimate(
            flops=6 * 256 * 1024 * 1024, bytes_accessed=6 << 20, transcendentals=0
        ),
        name="mix",
    )(where, *heads, weights)


def allowed_rows(
    head, key_block, query_block, vertical_blocks, vertical_count, slash_offsets, slash_count
):
    slots = jnp.arange(vertical_blocks.shape[1], dtype=jnp.int32)
    verticals = jnp.where(slots < vertical_count[head], vertical_blocks[head], -1)
    slashes = jnp.where(slots < slash_count[head], slash_offsets[head], -1)
    offset = query_block[:, None] - key_block[None, :]
    vert = jnp.any(key_block[:, None] == verticals[None, :], axis=1)[None, :]
    low_slash = jnp.any(offset[:, :, None] == slashes, axis=2)
    up_slash = jnp.any((offset - 1)[:, :, None] == slashes, axis=2)
    low = (offset >= 0) & (vert | low_slash)
    up = (offset >= 1) & (vert | up_slash)
    bias = jnp.where(jnp.stack([low, up]), 0.0, -jnp.inf)
    bias = jnp.repeat(bias, BLOCK, axis=2)
    return bias[0], bias[1]


CORES = [(0, 1), (1, 0)]


def along(axis, value, shift):
    count = lax.axis_size(axis)
    return lax.ppermute(value, axis, [(i, (i + shift) % count) for i in range(count)])


def shards(
    hidden_rows,
    query_weight,
    key_cache,
    value_cache,
    vertical_blocks,
    vertical_count,
    slash_offsets,
    slash_count,
    output_weight,
):
    x, y, z, k = (lax.axis_index(name) for name in ALL)
    where = jnp.stack([x, y, k, z]).astype(jnp.int32)
    weights = lax.all_gather(query_weight, ("y", "k"), axis=0)
    picked = pick(where, hidden_rows)
    hidden = [along("x", piece, shift) for shift, piece in enumerate(picked, 1)]
    behind, picked = lax.optimization_barrier((where, picked))
    near = pick_keys(behind, key_cache, value_cache)
    near = jnp.stack([near[0]] + [along("z", near[t], 2 * t) for t in range(1, NZ // 2)])
    near = jnp.concatenate([near, lax.ppermute(near, "z", [(i, i ^ 1) for i in range(NZ)])])
    rows = output_weight.reshape(2, NY, NK, 16, 512)
    kept = lax.dynamic_index_in_dim(rows, k, 2, keepdims=False)
    given = lax.dynamic_index_in_dim(rows, 1 - k, 2, keepdims=False)
    taken = lax.ppermute(given, "k", CORES)
    rows = jnp.where(k == 0, jnp.stack([kept, taken]), jnp.stack([taken, kept]))
    rows, near, hidden = lax.optimization_barrier((rows, near, hidden))
    rows = lax.all_to_all(rows.reshape(NX * NY, 16, 512), ("x", "y"), 0, 0)
    kv = lax.all_gather(near, ("y", "k"), axis=0)
    key_block = jnp.arange(NY, dtype=jnp.int32)[:, None, None]
    key_block = key_block + 4 * jnp.arange(NK, dtype=jnp.int32)[None, :, None]
    turns = 2 * jnp.arange(NZ // 2, dtype=jnp.int32)
    along_z = jnp.concatenate([z - turns, (z ^ 1) - turns]) % NZ
    key_block = key_block + 8 * along_z[None, None, :]
    low, up = allowed_rows(
        4 * z + x,
        key_block.reshape(-1),
        32 + 8 * jnp.arange(NX, dtype=jnp.int32) + 2 * y + k,
        vertical_blocks,
        vertical_count,
        slash_offsets,
        slash_count,
    )
    partial = project(where, hidden_rows, hidden, weights)
    partial = [partial[0]] + [along("x", partial[s], s) for s in range(1, NX)]
    rows, partial = lax.optimization_barrier((rows, partial))
    rows = lax.all_to_all(rows.reshape(NZ, NK, 16, 512), "z", 0, 0)
    out_weight = lax.all_gather(rows, ("y", "k"), axis=0)
    own = attend(partial, low, up, kv)
    near_up, near_down = along("z", own, 1), along("z", own, -1)
    far_up, far_down = along("z", own, 2), along("z", own, -2)
    heads = [own, near_up, near_down, far_up, far_down]
    heads += [along("z", far_up, 1), along("z", far_down, -1)]
    heads += [along("z", far_up[:128], 2), along("z", far_down[128:], -2)]
    mixed = mix(where, heads, out_weight)
    mixed = [mixed[0]] + [along("x", mixed[s], s) for s in range(1, NX)]
    first, second = (
        sum(lax.dynamic_index_in_dim(part, core, 0, keepdims=False) for part in mixed)
        for core in (1 - k, k)
    )
    other = lax.ppermute(first, "k", CORES)
    return jnp.concatenate(
        [jnp.where(k == 0, second, other), jnp.where(k == 0, other, second)]
    )


def solution(mesh):
    grid = Mesh(mesh.devices.reshape(NX, NY, NZ, NK), ALL)
    outer, ctx = ("x", "y"), ("z", "k")
    placed = (
        P(outer, None),
        P(outer, ctx),
        P(ctx, None),
        P(ctx, None),
        P(),
        P(),
        P(),
        P(),
        P(ctx, outer),
    )
    return jax.shard_map(
        shards, mesh=grid, in_specs=placed, out_specs=P(outer, ctx), check_vma=False
    )
```

```python
import math

import jax
import jax.numpy as jnp
from jax import lax
from jax.experimental import pallas as pl
from jax.experimental.pallas import tpu as pltpu
from jax.sharding import Mesh
from jax.sharding import PartitionSpec as P

HD = 128
BLOCK = 64
NX, NY, NZ, NK = 4, 4, 8, 2
ALL = ("x", "y", "z", "k")
VMEM = pl.BlockSpec(memory_space=pltpu.VMEM)
SMEM = pl.BlockSpec(memory_space=pltpu.SMEM)
ANY = pl.BlockSpec(memory_space=pl.ANY)
LIMIT = 60 << 20


def split(value):
    high = value.astype(jnp.bfloat16)
    low = (value - high.astype(jnp.float32)).astype(jnp.bfloat16)
    return high, low


def dot(left, right, dims):
    return lax.dot_general(left, right, dims, preferred_element_type=jnp.float32)


def dot3(left, right, dims):
    (lh, ll), (rh, rl) = left, right
    return dot(lh, rh, dims) + (dot(lh, rl, dims) + dot(ll, rh, dims))


MM = (((1,), (0,)), ((), ()))
MT = (((1,), (1,)), ((), ()))


def pick_kernel(where, rows, *refs):
    outs, sem = refs[:3], refs[3]
    x, k = where[0], where[2]
    copies = []
    for shift in range(1, NX):
        cols = pl.multiple_of(lax.rem(x + shift, NX) * 2048, 2048)
        part = rows.at[pl.ds(pl.multiple_of(k * BLOCK, BLOCK), BLOCK), pl.ds(cols, 2048)]
        copies.append(pltpu.make_async_copy(part, outs[shift - 1], sem.at[shift - 1]))
    for copy in copies:
        copy.start()
    for copy in copies:
        copy.wait()


def pick(where, hidden_rows):
    return pl.pallas_call(
        pick_kernel,
        out_shape=[jax.ShapeDtypeStruct((BLOCK, 2048), jnp.float32)] * 3,
        in_specs=[SMEM, ANY],
        out_specs=[VMEM] * 3,
        scratch_shapes=[pltpu.SemaphoreType.DMA((3,))],
        compiler_params=pltpu.CompilerParams(vmem_limit_bytes=LIMIT),
        name="pick",
    )(where, hidden_rows)


def pick_keys_kernel(where, keys, values, *refs):
    outs, sem = refs[: NZ // 2], refs[NZ // 2]
    y, z = where[1], where[3]
    copies = []
    for turn in range(NZ // 2):
        head = lax.rem(z + 2 * turn, NZ) // 2
        for index, cache in enumerate((keys, values)):
            part = cache.at[
                pl.ds(pl.multiple_of(y * BLOCK, BLOCK), BLOCK),
                pl.ds(pl.multiple_of(head * HD, HD), HD),
            ]
            copies.append(
                pltpu.make_async_copy(part, outs[turn].at[index], sem.at[2 * turn + index])
            )
    for copy in copies:
        copy.start()
    for copy in copies:
        copy.wait()


def pick_keys(where, key_cache, value_cache):
    return pl.pallas_call(
        pick_keys_kernel,
        out_shape=[jax.ShapeDtypeStruct((2, BLOCK, HD), jnp.float32)] * (NZ // 2),
        in_specs=[SMEM, ANY, ANY],
        out_specs=[VMEM] * (NZ // 2),
        scratch_shapes=[pltpu.SemaphoreType.DMA((NZ,))],
        compiler_params=pltpu.CompilerParams(vmem_limit_bytes=56 << 20),
        cost_estimate=pl.CostEstimate(flops=0, bytes_accessed=64 << 20, transcendentals=0),
        name="pick_keys",
    )(where, key_cache, value_cache)


def project_kernel(where, rows, first, second, third, weights, *refs):
    outs, (left_buf, right_buf, total_buf, sems) = refs[:NX], refs[NX:]
    x, k = where[0], where[2]
    copies = []
    for y in range(NY):
        own = rows.at[
            pl.ds(pl.multiple_of(k * BLOCK, BLOCK), BLOCK),
            pl.ds(pl.multiple_of(x * 2048 + y * 512, 512), 512),
        ]
        parts = [own] + [part.at[:, pl.ds(y * 512, 512)] for part in (first, second, third)]
        group = [
            pltpu.make_async_copy(
                part, left_buf.at[y, lax.rem(x + NX - shift, NX)], sems.at[y, shift]
            )
            for shift, part in enumerate(parts)
        ]
        group.append(
            pltpu.make_async_copy(weights.at[pl.ds(2 * y, 2)], right_buf.at[y], sems.at[y, NX])
        )
        for copy in group:
            copy.start()
        copies.append(group)
    totals = [None, None]
    for y in range(NY):
        for copy in copies[y]:
            copy.wait()
        left = split(left_buf[y].reshape(NX * BLOCK, 512))
        for core in range(NK):
            term = dot3(left, split(right_buf[y, core]), MM)
            totals[core] = term if totals[core] is None else totals[core] + term
    for core in range(NK):
        for b in range(2):
            total_buf[2 * core + b] = totals[core][:, b * HD : (b + 1) * HD]
    for shift in range(NX):
        outs[shift][...] = total_buf[lax.rem(x + shift, NX)]


def project(where, rows, moved, weights):
    return pl.pallas_call(
        project_kernel,
        out_shape=[jax.ShapeDtypeStruct((NX * BLOCK, HD), jnp.float32)] * NX,
        in_specs=[SMEM] + [ANY] * 5,
        out_specs=[VMEM] * NX,
        scratch_shapes=[
            pltpu.VMEM((NY, NX, BLOCK, 512), jnp.float32),
            pltpu.VMEM((NY, NK, 512, 256), jnp.float32),
            pltpu.VMEM((NX, NX * BLOCK, HD), jnp.float32),
            pltpu.SemaphoreType.DMA((NY, NX + 1)),
        ],
        compiler_params=pltpu.CompilerParams(vmem_limit_bytes=48 << 20),
        cost_estimate=pl.CostEstimate(
            flops=6 * 256 * 2048 * 512, bytes_accessed=7 << 20, transcendentals=0
        ),
        name="project",
    )(where, rows, *moved, weights)


def attend_kernel(first, second, third, fourth, low, up, gathered, out, kv, scores, sem):
    tiles = gathered.shape[0]
    copies = [
        pltpu.make_async_copy(gathered.at[tile], kv.at[tile], sem.at[tile])
        for tile in range(tiles)
    ]
    for copy in copies:
        copy.start()
    width = NZ * BLOCK
    row = lax.broadcasted_iota(jnp.int32, (BLOCK, width), 0)
    col = lax.broadcasted_iota(jnp.int32, (BLOCK, width), 1)
    lower = row >= lax.rem(col, BLOCK)
    query = (first[...] + second[...]) + (third[...] + fourth[...])
    high, low_part = split(query * (math.log2(math.e) / math.sqrt(HD)))
    both = jnp.concatenate([high, low_part], axis=1)
    top = None
    for tile in range(tiles):
        copies[tile].wait()
        key_high, key_low = split(kv[tile, :, 0].reshape(width, HD))
        s = dot(both, jnp.concatenate([key_high, key_high], axis=1), MT)
        s = s + dot(high, key_low, MT)
        cols = slice(tile * width, (tile + 1) * width)
        bias = jnp.concatenate(
            [
                jnp.where(lower, low[b : b + 1, cols], up[b : b + 1, cols])
                for b in range(NX)
            ],
            axis=0,
        )
        s = s + bias
        scores[tile] = s
        top = s if top is None else jnp.maximum(top, s)
    top = jnp.max(top, axis=1, keepdims=True)
    total, summed = None, None
    for tile in range(tiles):
        weight = jnp.exp2(scores[tile] - top)
        weight_high, weight_low = split(weight)
        value_high, value_low = split(kv[tile, :, 1].reshape(width, HD))
        term = dot(weight_high, jnp.concatenate([value_high, value_low], axis=1), MM)
        term = term[:, :HD] + (term[:, HD:] + dot(weight_low, value_high, MM))
        total = weight if total is None else total + weight
        summed = term if summed is None else summed + term
    out[...] = summed / jnp.sum(total, axis=1, keepdims=True)


def attend(partial, low, up, gathered):
    rows = NX * BLOCK
    return pl.pallas_call(
        attend_kernel,
        out_shape=jax.ShapeDtypeStruct((rows, HD), jnp.float32),
        in_specs=[VMEM] * 6 + [ANY],
        out_specs=VMEM,
        scratch_shapes=[
            pltpu.VMEM((8, NZ, 2, BLOCK, HD), jnp.float32),
            pltpu.VMEM((8, rows, NZ * BLOCK), jnp.float32),
            pltpu.SemaphoreType.DMA((8,)),
        ],
        compiler_params=pltpu.CompilerParams(vmem_limit_bytes=40 << 20),
        cost_estimate=pl.CostEstimate(
            flops=12 * 256 * 4096 * HD, bytes_accessed=6 << 20, transcendentals=256 * 4096
        ),
        name="attend",
    )(*partial, low, up, gathered)


OFFSETS = (0, -1, 1, -2, 2, -3, 3, 4)


def mix_kernel(where, *refs):
    own, other, weights, outs = refs[:9], refs[9:18], refs[18], refs[19 : 19 + NX]
    total_buf, buf, sems = refs[19 + NX :]
    places = [lax.rem(where[3] + offset + NZ, NZ) for offset in OFFSETS]
    copies = [
        [
            pltpu.make_async_copy(
                weights.at[y, pl.ds(2 * spot, 2)], buf.at[index, y], sems.at[index, y]
            )
            for y in range(NY)
        ]
        for index, spot in enumerate(places)
    ]
    for group in copies:
        for copy in group:
            copy.start()
    blocks = [
        [head[...] for head in heads[:7]]
        + [jnp.concatenate([heads[7][...], heads[8][...]], axis=0)]
        for heads in (own, other)
    ]
    totals = [None, None]
    for step in range(NZ // 2):
        pair = (2 * step, 2 * step + 1)
        for index in pair:
            for copy in copies[index]:
                copy.wait()
        right = split(jnp.concatenate([buf[index].reshape(HD, 512) for index in pair], axis=0))
        for side in range(2):
            left = split(jnp.concatenate([blocks[side][index] for index in pair], axis=1))
            term = dot3(left, right, MM)
            totals[side] = term if totals[side] is None else totals[side] + term
    for side in range(2):
        core = where[2] if side == 0 else 1 - where[2]
        for x in range(NX):
            total_buf[x, core] = totals[side][x * BLOCK : (x + 1) * BLOCK]
    for shift in range(NX):
        outs[shift][...] = total_buf[lax.rem(where[0] + shift, NX)]


def mix(where, own, other, weights):
    return pl.pallas_call(
        mix_kernel,
        out_shape=[jax.ShapeDtypeStruct((NK, BLOCK, 512), jnp.float32)] * NX,
        in_specs=[SMEM] + [VMEM] * 18 + [ANY],
        out_specs=[VMEM] * NX,
        scratch_shapes=[
            pltpu.VMEM((NX, NK, BLOCK, 512), jnp.float32),
            pltpu.VMEM((NZ, NY, 2, 16, 512), jnp.float32),
            pltpu.SemaphoreType.DMA((NZ, NY)),
        ],
        compiler_params=pltpu.CompilerParams(vmem_limit_bytes=50 << 20),
        cost_estimate=pl.CostEstimate(
            flops=6 * 256 * 1024 * 1024, bytes_accessed=6 << 20, transcendentals=0
        ),
        name="mix",
    )(where, *own, *other, weights)


def allowed_rows(
    head, key_block, query_block, vertical_blocks, vertical_count, slash_offsets, slash_count
):
    slots = jnp.arange(vertical_blocks.shape[1], dtype=jnp.int32)
    verticals = jnp.where(slots < vertical_count[head], vertical_blocks[head], -1)
    slashes = jnp.where(slots < slash_count[head], slash_offsets[head], -1)
    offset = query_block[:, None] - key_block[None, :]
    vert = jnp.any(key_block[:, None] == verticals[None, :], axis=1)[None, :]
    low_slash = jnp.any(offset[:, :, None] == slashes, axis=2)
    up_slash = jnp.any((offset - 1)[:, :, None] == slashes, axis=2)
    low = (offset >= 0) & (vert | low_slash)
    up = (offset >= 1) & (vert | up_slash)
    bias = jnp.where(jnp.stack([low, up]), 0.0, -jnp.inf)
    bias = jnp.repeat(bias, BLOCK, axis=2)
    return bias[0], bias[1]


CORES = [(0, 1), (1, 0)]


def along(axis, value, shift):
    count = lax.axis_size(axis)
    return lax.ppermute(value, axis, [(i, (i + shift) % count) for i in range(count)])


def shards(
    hidden_rows,
    query_weight,
    key_cache,
    value_cache,
    vertical_blocks,
    vertical_count,
    slash_offsets,
    slash_count,
    output_weight,
):
    x, y, z, k = (lax.axis_index(name) for name in ALL)
    where = jnp.stack([x, y, k, z]).astype(jnp.int32)
    weights = lax.all_gather(query_weight, ("y", "k"), axis=0)
    picked = pick(where, hidden_rows)
    hidden = [along("x", piece, shift) for shift, piece in enumerate(picked, 1)]
    behind, picked = lax.optimization_barrier((where, picked))
    near = pick_keys(behind, key_cache, value_cache)
    near = jnp.stack([near[0]] + [along("z", near[t], 2 * t) for t in range(1, NZ // 2)])
    near = jnp.concatenate([near, lax.ppermute(near, "z", [(i, i ^ 1) for i in range(NZ)])])
    rows = output_weight.reshape(2, NY, NK, 16, 512)
    kept = lax.dynamic_index_in_dim(rows, k, 2, keepdims=False)
    given = lax.dynamic_index_in_dim(rows, 1 - k, 2, keepdims=False)
    taken = lax.ppermute(given, "k", CORES)
    rows = jnp.where(k == 0, jnp.stack([kept, taken]), jnp.stack([taken, kept]))
    rows, near, hidden = lax.optimization_barrier((rows, near, hidden))
    rows = lax.all_to_all(rows.reshape(NX * NY, 16, 512), ("x", "y"), 0, 0)
    kv = lax.all_gather(near, ("y", "k"), axis=0)
    key_block = jnp.arange(NY, dtype=jnp.int32)[:, None, None]
    key_block = key_block + 4 * jnp.arange(NK, dtype=jnp.int32)[None, :, None]
    turns = 2 * jnp.arange(NZ // 2, dtype=jnp.int32)
    along_z = jnp.concatenate([z - turns, (z ^ 1) - turns]) % NZ
    key_block = key_block + 8 * along_z[None, None, :]
    low, up = allowed_rows(
        4 * z + x,
        key_block.reshape(-1),
        32 + 8 * jnp.arange(NX, dtype=jnp.int32) + 2 * y + k,
        vertical_blocks,
        vertical_count,
        slash_offsets,
        slash_count,
    )
    partial = project(where, hidden_rows, hidden, weights)
    partial = [partial[0]] + [along("x", partial[s], s) for s in range(1, NX)]
    rows, partial = lax.optimization_barrier((rows, partial))
    rows = lax.all_to_all(rows, ("z", "k"), 0, 0)
    out_weight = lax.all_gather(rows, "y", axis=0)
    own = attend(partial, low, up, kv)
    near_up, near_down = along("z", own, 1), along("z", own, -1)
    far_up, far_down = along("z", own, 2), along("z", own, -2)
    heads = [own, near_up, near_down, far_up, far_down]
    heads += [along("z", far_up, 1), along("z", far_down, -1)]
    heads += [along("z", far_up[:128], 2), along("z", far_down[128:], -2)]
    swapped = [lax.ppermute(head, "k", CORES) for head in heads]
    mixed = mix(where, heads, swapped, out_weight)
    mixed = [mixed[0]] + [along("x", mixed[s], s) for s in range(1, NX)]
    return ((mixed[0] + mixed[1]) + (mixed[2] + mixed[3])).reshape(NK * BLOCK, 512)


def solution(mesh):
    grid = Mesh(mesh.devices.reshape(NX, NY, NZ, NK), ALL)
    outer, ctx = ("x", "y"), ("z", "k")
    placed = (
        P(outer, None),
        P(outer, ctx),
        P(ctx, None),
        P(ctx, None),
        P(),
        P(),
        P(),
        P(),
        P(ctx, outer),
    )
    return jax.shard_map(
        shards, mesh=grid, in_specs=placed, out_specs=P(outer, ctx), check_vma=False
    )
```

```python
import math

import jax
import jax.numpy as jnp
from jax import lax
from jax.experimental import pallas as pl
from jax.experimental.pallas import tpu as pltpu
from jax.sharding import Mesh
from jax.sharding import PartitionSpec as P

HD = 128
BLOCK = 64
NX, NY, NZ, NK = 4, 4, 8, 2
ALL = ("x", "y", "z", "k")
VMEM = pl.BlockSpec(memory_space=pltpu.VMEM)
SMEM = pl.BlockSpec(memory_space=pltpu.SMEM)
ANY = pl.BlockSpec(memory_space=pl.ANY)
LIMIT = 60 << 20


def split(value):
    high = value.astype(jnp.bfloat16)
    low = (value - high.astype(jnp.float32)).astype(jnp.bfloat16)
    return high, low


def dot(left, right, dims):
    return lax.dot_general(left, right, dims, preferred_element_type=jnp.float32)


def dot3(left, right, dims):
    (lh, ll), (rh, rl) = left, right
    return dot(lh, rh, dims) + (dot(lh, rl, dims) + dot(ll, rh, dims))


MM = (((1,), (0,)), ((), ()))
MT = (((1,), (1,)), ((), ()))


def pick_kernel(where, rows, *refs):
    outs, sem = refs[:3], refs[3]
    x, k = where[0], where[2]
    copies = []
    for shift in range(1, NX):
        cols = pl.multiple_of(lax.rem(x + shift, NX) * 2048, 2048)
        part = rows.at[pl.ds(pl.multiple_of(k * BLOCK, BLOCK), BLOCK), pl.ds(cols, 2048)]
        copies.append(pltpu.make_async_copy(part, outs[shift - 1], sem.at[shift - 1]))
    for copy in copies:
        copy.start()
    for copy in copies:
        copy.wait()


def pick(where, hidden_rows):
    return pl.pallas_call(
        pick_kernel,
        out_shape=[jax.ShapeDtypeStruct((BLOCK, 2048), jnp.float32)] * 3,
        in_specs=[SMEM, ANY],
        out_specs=[VMEM] * 3,
        scratch_shapes=[pltpu.SemaphoreType.DMA((3,))],
        compiler_params=pltpu.CompilerParams(vmem_limit_bytes=LIMIT),
        name="pick",
    )(where, hidden_rows)


def pick_keys_kernel(where, keys, values, *refs):
    outs, sem = refs[: NZ // 2], refs[NZ // 2]
    y, z = where[1], where[3]
    copies = []
    for turn in range(NZ // 2):
        head = lax.rem(z + 2 * turn, NZ) // 2
        for index, cache in enumerate((keys, values)):
            part = cache.at[
                pl.ds(pl.multiple_of(y * BLOCK, BLOCK), BLOCK),
                pl.ds(pl.multiple_of(head * HD, HD), HD),
            ]
            copies.append(
                pltpu.make_async_copy(part, outs[turn].at[index], sem.at[2 * turn + index])
            )
    for copy in copies:
        copy.start()
    for copy in copies:
        copy.wait()


def pick_keys(where, key_cache, value_cache):
    return pl.pallas_call(
        pick_keys_kernel,
        out_shape=[jax.ShapeDtypeStruct((2, BLOCK, HD), jnp.float32)] * (NZ // 2),
        in_specs=[SMEM, ANY, ANY],
        out_specs=[VMEM] * (NZ // 2),
        scratch_shapes=[pltpu.SemaphoreType.DMA((NZ,))],
        compiler_params=pltpu.CompilerParams(vmem_limit_bytes=56 << 20),
        cost_estimate=pl.CostEstimate(flops=0, bytes_accessed=64 << 20, transcendentals=0),
        name="pick_keys",
    )(where, key_cache, value_cache)


def project_kernel(where, rows, first, second, third, weights, *refs):
    outs, (left_buf, right_buf, total_buf, sems) = refs[:NX], refs[NX:]
    x, k = where[0], where[2]
    copies = []
    for y in range(NY):
        own = rows.at[
            pl.ds(pl.multiple_of(k * BLOCK, BLOCK), BLOCK),
            pl.ds(pl.multiple_of(x * 2048 + y * 512, 512), 512),
        ]
        parts = [own] + [part.at[:, pl.ds(y * 512, 512)] for part in (first, second, third)]
        group = [
            pltpu.make_async_copy(
                part, left_buf.at[y, lax.rem(x + NX - shift, NX)], sems.at[y, shift]
            )
            for shift, part in enumerate(parts)
        ]
        group.append(
            pltpu.make_async_copy(weights.at[pl.ds(2 * y, 2)], right_buf.at[y], sems.at[y, NX])
        )
        for copy in group:
            copy.start()
        copies.append(group)
    totals = [None, None]
    for y in range(NY):
        for copy in copies[y]:
            copy.wait()
        left = split(left_buf[y].reshape(NX * BLOCK, 512))
        for core in range(NK):
            term = dot3(left, split(right_buf[y, core]), MM)
            totals[core] = term if totals[core] is None else totals[core] + term
    for core in range(NK):
        for b in range(2):
            total_buf[2 * core + b] = totals[core][:, b * HD : (b + 1) * HD]
    for shift in range(NX):
        outs[shift][...] = total_buf[lax.rem(x + shift, NX)]


def project(where, rows, moved, weights):
    return pl.pallas_call(
        project_kernel,
        out_shape=[jax.ShapeDtypeStruct((NX * BLOCK, HD), jnp.float32)] * NX,
        in_specs=[SMEM] + [ANY] * 5,
        out_specs=[VMEM] * NX,
        scratch_shapes=[
            pltpu.VMEM((NY, NX, BLOCK, 512), jnp.float32),
            pltpu.VMEM((NY, NK, 512, 256), jnp.float32),
            pltpu.VMEM((NX, NX * BLOCK, HD), jnp.float32),
            pltpu.SemaphoreType.DMA((NY, NX + 1)),
        ],
        compiler_params=pltpu.CompilerParams(vmem_limit_bytes=48 << 20),
        cost_estimate=pl.CostEstimate(
            flops=6 * 256 * 2048 * 512, bytes_accessed=7 << 20, transcendentals=0
        ),
        name="project",
    )(where, rows, *moved, weights)


def attend_kernel(first, second, third, fourth, low, up, gathered, out, kv, scores, sem):
    tiles = gathered.shape[0]
    copies = [
        pltpu.make_async_copy(gathered.at[tile], kv.at[tile], sem.at[tile])
        for tile in range(tiles)
    ]
    for copy in copies:
        copy.start()
    width = NZ * BLOCK
    row = lax.broadcasted_iota(jnp.int32, (BLOCK, width), 0)
    col = lax.broadcasted_iota(jnp.int32, (BLOCK, width), 1)
    lower = row >= lax.rem(col, BLOCK)
    query = (first[...] + second[...]) + (third[...] + fourth[...])
    high, low_part = split(query * (math.log2(math.e) / math.sqrt(HD)))
    both = jnp.concatenate([high, low_part], axis=1)
    top = None
    for tile in range(tiles):
        copies[tile].wait()
        key_high, key_low = split(kv[tile, :, 0].reshape(width, HD))
        s = dot(both, jnp.concatenate([key_high, key_high], axis=1), MT)
        s = s + dot(high, key_low, MT)
        cols = slice(tile * width, (tile + 1) * width)
        bias = jnp.concatenate(
            [
                jnp.where(lower, low[b : b + 1, cols], up[b : b + 1, cols])
                for b in range(NX)
            ],
            axis=0,
        )
        s = s + bias
        scores[tile] = s
        top = s if top is None else jnp.maximum(top, s)
    top = jnp.max(top, axis=1, keepdims=True)
    total, summed = None, None
    for tile in range(tiles):
        weight = jnp.exp2(scores[tile] - top)
        weight_high, weight_low = split(weight)
        value_high, value_low = split(kv[tile, :, 1].reshape(width, HD))
        term = dot(weight_high, jnp.concatenate([value_high, value_low], axis=1), MM)
        term = term[:, :HD] + (term[:, HD:] + dot(weight_low, value_high, MM))
        total = weight if total is None else total + weight
        summed = term if summed is None else summed + term
    out[...] = summed / jnp.sum(total, axis=1, keepdims=True)


def attend(partial, low, up, gathered):
    rows = NX * BLOCK
    return pl.pallas_call(
        attend_kernel,
        out_shape=jax.ShapeDtypeStruct((rows, HD), jnp.float32),
        in_specs=[VMEM] * 6 + [ANY],
        out_specs=VMEM,
        scratch_shapes=[
            pltpu.VMEM((8, NZ, 2, BLOCK, HD), jnp.float32),
            pltpu.VMEM((8, rows, NZ * BLOCK), jnp.float32),
            pltpu.SemaphoreType.DMA((8,)),
        ],
        compiler_params=pltpu.CompilerParams(vmem_limit_bytes=50 << 20),
        cost_estimate=pl.CostEstimate(
            flops=12 * 256 * 4096 * HD, bytes_accessed=6 << 20, transcendentals=256 * 4096
        ),
        name="attend",
    )(*partial, low, up, gathered)


OFFSETS = (0, -1, 1, -2, 2, -3, 3, 4)


def mix_kernel(where, *refs):
    own, other, weights, outs = refs[:9], refs[9:18], refs[18], refs[19 : 19 + NX]
    total_buf, buf, sems = refs[19 + NX :]
    places = [lax.rem(where[3] + offset + NZ, NZ) for offset in OFFSETS]
    copies = [
        [
            pltpu.make_async_copy(
                weights.at[y, pl.ds(2 * spot, 2)], buf.at[index, y], sems.at[index, y]
            )
            for y in range(NY)
        ]
        for index, spot in enumerate(places)
    ]
    for group in copies:
        for copy in group:
            copy.start()
    blocks = [
        [head[...] for head in heads[:7]]
        + [jnp.concatenate([heads[7][...], heads[8][...]], axis=0)]
        for heads in (own, other)
    ]
    totals = [None, None]
    for step in range(NZ // 2):
        pair = (2 * step, 2 * step + 1)
        for index in pair:
            for copy in copies[index]:
                copy.wait()
        right = split(jnp.concatenate([buf[index].reshape(HD, 512) for index in pair], axis=0))
        for side in range(2):
            left = split(jnp.concatenate([blocks[side][index] for index in pair], axis=1))
            term = dot3(left, right, MM)
            totals[side] = term if totals[side] is None else totals[side] + term
    for side in range(2):
        core = where[2] if side == 0 else 1 - where[2]
        for x in range(NX):
            total_buf[x, core] = totals[side][x * BLOCK : (x + 1) * BLOCK]
    for shift in range(NX):
        outs[shift][...] = total_buf[lax.rem(where[0] + shift, NX)]


def mix(where, own, other, weights):
    return pl.pallas_call(
        mix_kernel,
        out_shape=[jax.ShapeDtypeStruct((NK, BLOCK, 512), jnp.float32)] * NX,
        in_specs=[SMEM] + [VMEM] * 18 + [ANY],
        out_specs=[VMEM] * NX,
        scratch_shapes=[
            pltpu.VMEM((NX, NK, BLOCK, 512), jnp.float32),
            pltpu.VMEM((NZ, NY, 2, 16, 512), jnp.float32),
            pltpu.SemaphoreType.DMA((NZ, NY)),
        ],
        compiler_params=pltpu.CompilerParams(vmem_limit_bytes=50 << 20),
        cost_estimate=pl.CostEstimate(
            flops=6 * 256 * 1024 * 1024, bytes_accessed=6 << 20, transcendentals=0
        ),
        name="mix",
    )(where, *own, *other, weights)


def allowed_rows(
    head, key_block, query_block, vertical_blocks, vertical_count, slash_offsets, slash_count
):
    slots = jnp.arange(vertical_blocks.shape[1], dtype=jnp.int32)
    verticals = jnp.where(slots < vertical_count[head], vertical_blocks[head], -1)
    slashes = jnp.where(slots < slash_count[head], slash_offsets[head], -1)
    offset = query_block[:, None] - key_block[None, :]
    vert = jnp.any(key_block[:, None] == verticals[None, :], axis=1)[None, :]
    low_slash = jnp.any(offset[:, :, None] == slashes, axis=2)
    up_slash = jnp.any((offset - 1)[:, :, None] == slashes, axis=2)
    low = (offset >= 0) & (vert | low_slash)
    up = (offset >= 1) & (vert | up_slash)
    bias = jnp.where(jnp.stack([low, up]), 0.0, -jnp.inf)
    bias = jnp.repeat(bias, BLOCK, axis=2)
    return bias[0], bias[1]


CORES = [(0, 1), (1, 0)]


def along(axis, value, shift):
    count = lax.axis_size(axis)
    return lax.ppermute(value, axis, [(i, (i + shift) % count) for i in range(count)])


def shards(
    hidden_rows,
    query_weight,
    key_cache,
    value_cache,
    vertical_blocks,
    vertical_count,
    slash_offsets,
    slash_count,
    output_weight,
):
    x, y, z, k = (lax.axis_index(name) for name in ALL)
    where = jnp.stack([x, y, k, z]).astype(jnp.int32)
    weights = lax.all_gather(query_weight, ("y", "k"), axis=0)
    picked = pick(where, hidden_rows)
    hidden = [along("x", piece, shift) for shift, piece in enumerate(picked, 1)]
    behind, picked = lax.optimization_barrier((where, picked))
    near = pick_keys(behind, key_cache, value_cache)
    near = jnp.stack([near[0]] + [along("z", near[t], 2 * t) for t in range(1, NZ // 2)])
    near = jnp.concatenate([near, lax.ppermute(near, "z", [(i, i ^ 1) for i in range(NZ)])])
    rows = output_weight.reshape(2, NY, NK, 16, 512)
    kept = lax.dynamic_index_in_dim(rows, k, 2, keepdims=False)
    given = lax.dynamic_index_in_dim(rows, 1 - k, 2, keepdims=False)
    taken = lax.ppermute(given, "k", CORES)
    rows = jnp.where(k == 0, jnp.stack([kept, taken]), jnp.stack([taken, kept]))
    key_block = jnp.arange(NY, dtype=jnp.int32)[:, None, None]
    key_block = key_block + 4 * jnp.arange(NK, dtype=jnp.int32)[None, :, None]
    turns = 2 * jnp.arange(NZ // 2, dtype=jnp.int32)
    along_z = jnp.concatenate([z - turns, (z ^ 1) - turns]) % NZ
    key_block = key_block + 8 * along_z[None, None, :]
    low, up = allowed_rows(
        4 * z + x,
        key_block.reshape(-1),
        32 + 8 * jnp.arange(NX, dtype=jnp.int32) + 2 * y + k,
        vertical_blocks,
        vertical_count,
        slash_offsets,
        slash_count,
    )
    rows, near, hidden, low, up = lax.optimization_barrier((rows, near, hidden, low, up))
    rows = lax.all_to_all(rows.reshape(NX * NY, 16, 512), ("x", "y"), 0, 0)
    kv = lax.all_gather(near, ("y", "k"), axis=0)
    partial = project(where, hidden_rows, hidden, weights)
    partial = [partial[0]] + [along("x", partial[s], s) for s in range(1, NX)]
    rows, partial = lax.optimization_barrier((rows, partial))
    rows = lax.all_to_all(rows, ("z", "k"), 0, 0)
    out_weight = lax.all_gather(rows, "y", axis=0)
    own = attend(partial, low, up, kv)
    near_up, near_down = along("z", own, 1), along("z", own, -1)
    far_up, far_down = along("z", own, 2), along("z", own, -2)
    heads = [own, near_up, near_down, far_up, far_down]
    heads += [along("z", far_up, 1), along("z", far_down, -1)]
    heads += [along("z", far_up[:128], 2), along("z", far_down[128:], -2)]
    swapped = [lax.ppermute(head, "k", CORES) for head in heads]
    mixed = mix(where, heads, swapped, out_weight)
    mixed = [mixed[0]] + [along("x", mixed[s], s) for s in range(1, NX)]
    return ((mixed[0] + mixed[1]) + (mixed[2] + mixed[3])).reshape(NK * BLOCK, 512)


def solution(mesh):
    grid = Mesh(mesh.devices.reshape(NX, NY, NZ, NK), ALL)
    outer, ctx = ("x", "y"), ("z", "k")
    placed = (
        P(outer, None),
        P(outer, ctx),
        P(ctx, None),
        P(ctx, None),
        P(),
        P(),
        P(),
        P(),
        P(ctx, outer),
    )
    return jax.shard_map(
        shards, mesh=grid, in_specs=placed, out_specs=P(outer, ctx), check_vma=False
    )
```

```python
import math

import jax
import jax.numpy as jnp
from jax import lax
from jax.experimental import pallas as pl
from jax.experimental.pallas import tpu as pltpu
from jax.sharding import Mesh
from jax.sharding import PartitionSpec as P

HD = 128
BLOCK = 64
NX, NY, NZ, NK = 4, 4, 8, 2
ALL = ("x", "y", "z", "k")
VMEM = pl.BlockSpec(memory_space=pltpu.VMEM)
SMEM = pl.BlockSpec(memory_space=pltpu.SMEM)
ANY = pl.BlockSpec(memory_space=pl.ANY)
LIMIT = 60 << 20


def split(value):
    high = value.astype(jnp.bfloat16)
    low = (value - high.astype(jnp.float32)).astype(jnp.bfloat16)
    return high, low


def dot(left, right, dims):
    return lax.dot_general(left, right, dims, preferred_element_type=jnp.float32)


def dot3(left, right, dims):
    (lh, ll), (rh, rl) = left, right
    return dot(lh, rh, dims) + (dot(lh, rl, dims) + dot(ll, rh, dims))


MM = (((1,), (0,)), ((), ()))
MT = (((1,), (1,)), ((), ()))


def pick_kernel(where, rows, *refs):
    outs, sem = refs[:3], refs[3]
    x, k = where[0], where[2]
    copies = []
    for shift in range(1, NX):
        cols = pl.multiple_of(lax.rem(x + shift, NX) * 2048, 2048)
        part = rows.at[pl.ds(pl.multiple_of(k * BLOCK, BLOCK), BLOCK), pl.ds(cols, 2048)]
        copies.append(pltpu.make_async_copy(part, outs[shift - 1], sem.at[shift - 1]))
    for copy in copies:
        copy.start()
    for copy in copies:
        copy.wait()


def pick(where, hidden_rows):
    return pl.pallas_call(
        pick_kernel,
        out_shape=[jax.ShapeDtypeStruct((BLOCK, 2048), jnp.float32)] * 3,
        in_specs=[SMEM, ANY],
        out_specs=[VMEM] * 3,
        scratch_shapes=[pltpu.SemaphoreType.DMA((3,))],
        compiler_params=pltpu.CompilerParams(vmem_limit_bytes=LIMIT),
        name="pick",
    )(where, hidden_rows)


def pick_keys_kernel(where, keys, values, *refs):
    outs, sem = refs[: NZ // 2], refs[NZ // 2]
    y, z = where[1], where[3]
    copies = []
    for turn in range(NZ // 2):
        head = lax.rem(z + 2 * turn, NZ) // 2
        for index, cache in enumerate((keys, values)):
            part = cache.at[
                pl.ds(pl.multiple_of(y * BLOCK, BLOCK), BLOCK),
                pl.ds(pl.multiple_of(head * HD, HD), HD),
            ]
            copies.append(
                pltpu.make_async_copy(part, outs[turn].at[index], sem.at[2 * turn + index])
            )
    for copy in copies:
        copy.start()
    for copy in copies:
        copy.wait()


def pick_keys(where, key_cache, value_cache):
    return pl.pallas_call(
        pick_keys_kernel,
        out_shape=[jax.ShapeDtypeStruct((2, BLOCK, HD), jnp.float32)] * (NZ // 2),
        in_specs=[SMEM, ANY, ANY],
        out_specs=[VMEM] * (NZ // 2),
        scratch_shapes=[pltpu.SemaphoreType.DMA((NZ,))],
        compiler_params=pltpu.CompilerParams(vmem_limit_bytes=56 << 20),
        cost_estimate=pl.CostEstimate(flops=0, bytes_accessed=64 << 20, transcendentals=0),
        name="pick_keys",
    )(where, key_cache, value_cache)


def project_kernel(where, rows, first, second, third, weights, *refs):
    outs, (left_buf, right_buf, total_buf, sems) = refs[:NX], refs[NX:]
    x, k = where[0], where[2]
    copies = []
    for y in range(NY):
        own = rows.at[
            pl.ds(pl.multiple_of(k * BLOCK, BLOCK), BLOCK),
            pl.ds(pl.multiple_of(x * 2048 + y * 512, 512), 512),
        ]
        parts = [own] + [part.at[:, pl.ds(y * 512, 512)] for part in (first, second, third)]
        group = [
            pltpu.make_async_copy(
                part, left_buf.at[y, lax.rem(x + NX - shift, NX)], sems.at[y, shift]
            )
            for shift, part in enumerate(parts)
        ]
        group.append(
            pltpu.make_async_copy(weights.at[pl.ds(2 * y, 2)], right_buf.at[y], sems.at[y, NX])
        )
        for copy in group:
            copy.start()
        copies.append(group)
    totals = [None, None]
    for y in range(NY):
        for copy in copies[y]:
            copy.wait()
        left = split(left_buf[y].reshape(NX * BLOCK, 512))
        for core in range(NK):
            term = dot3(left, split(right_buf[y, core]), MM)
            totals[core] = term if totals[core] is None else totals[core] + term
    for core in range(NK):
        for b in range(2):
            total_buf[2 * core + b] = totals[core][:, b * HD : (b + 1) * HD]
    for shift in range(NX):
        outs[shift][...] = total_buf[lax.rem(x + shift, NX)]


def project(where, rows, moved, weights):
    return pl.pallas_call(
        project_kernel,
        out_shape=[jax.ShapeDtypeStruct((NX * BLOCK, HD), jnp.float32)] * NX,
        in_specs=[SMEM] + [ANY] * 5,
        out_specs=[VMEM] * NX,
        scratch_shapes=[
            pltpu.VMEM((NY, NX, BLOCK, 512), jnp.float32),
            pltpu.VMEM((NY, NK, 512, 256), jnp.float32),
            pltpu.VMEM((NX, NX * BLOCK, HD), jnp.float32),
            pltpu.SemaphoreType.DMA((NY, NX + 1)),
        ],
        compiler_params=pltpu.CompilerParams(vmem_limit_bytes=48 << 20),
        cost_estimate=pl.CostEstimate(
            flops=6 * 256 * 2048 * 512, bytes_accessed=7 << 20, transcendentals=0
        ),
        name="project",
    )(where, rows, *moved, weights)


def attend_kernel(first, second, third, fourth, low, up, gathered, out, kv, scores, sem):
    tiles = gathered.shape[0]
    copies = [
        pltpu.make_async_copy(gathered.at[tile], kv.at[tile], sem.at[tile])
        for tile in range(tiles)
    ]
    for copy in copies:
        copy.start()
    width = NZ * BLOCK
    row = lax.broadcasted_iota(jnp.int32, (BLOCK, width), 0)
    col = lax.broadcasted_iota(jnp.int32, (BLOCK, width), 1)
    lower = row >= lax.rem(col, BLOCK)
    query = (first[...] + second[...]) + (third[...] + fourth[...])
    high, low_part = split(query * (math.log2(math.e) / math.sqrt(HD)))
    both = jnp.concatenate([high, low_part], axis=1)
    top = None
    for tile in range(tiles):
        copies[tile].wait()
        key_high, key_low = split(kv[tile, :, 0].reshape(width, HD))
        s = dot(both, jnp.concatenate([key_high, key_high], axis=1), MT)
        s = s + dot(high, key_low, MT)
        cols = slice(tile * width, (tile + 1) * width)
        bias = jnp.concatenate(
            [
                jnp.where(lower, low[b : b + 1, cols], up[b : b + 1, cols])
                for b in range(NX)
            ],
            axis=0,
        )
        s = s + bias
        scores[tile] = s
        top = s if top is None else jnp.maximum(top, s)
    top = jnp.max(top, axis=1, keepdims=True)
    total, summed = None, None
    for tile in range(tiles):
        weight = jnp.exp2(scores[tile] - top)
        weight_high, weight_low = split(weight)
        value_high, value_low = split(kv[tile, :, 1].reshape(width, HD))
        term = dot(weight_high, jnp.concatenate([value_high, value_low], axis=1), MM)
        term = term[:, :HD] + (term[:, HD:] + dot(weight_low, value_high, MM))
        total = weight if total is None else total + weight
        summed = term if summed is None else summed + term
    out[...] = summed / jnp.sum(total, axis=1, keepdims=True)


def attend(partial, low, up, gathered):
    rows = NX * BLOCK
    return pl.pallas_call(
        attend_kernel,
        out_shape=jax.ShapeDtypeStruct((rows, HD), jnp.float32),
        in_specs=[VMEM] * 6 + [ANY],
        out_specs=VMEM,
        scratch_shapes=[
            pltpu.VMEM((8, NZ, 2, BLOCK, HD), jnp.float32),
            pltpu.VMEM((8, rows, NZ * BLOCK), jnp.float32),
            pltpu.SemaphoreType.DMA((8,)),
        ],
        compiler_params=pltpu.CompilerParams(vmem_limit_bytes=50 << 20),
        cost_estimate=pl.CostEstimate(
            flops=12 * 256 * 4096 * HD, bytes_accessed=6 << 20, transcendentals=256 * 4096
        ),
        name="attend",
    )(*partial, low, up, gathered)


OFFSETS = (0, -1, 1, -2, 2, -3, 3, 4)


def mix_kernel(where, *refs):
    own, other, weights, outs = refs[:9], refs[9:18], refs[18], refs[19 : 19 + NX]
    total_buf, buf, sems = refs[19 + NX :]
    places = [lax.rem(where[3] + offset + NZ, NZ) for offset in OFFSETS]
    copies = [
        [
            pltpu.make_async_copy(
                weights.at[y, pl.ds(2 * spot, 2)], buf.at[index, y], sems.at[index, y]
            )
            for y in range(NY)
        ]
        for index, spot in enumerate(places)
    ]
    for group in copies:
        for copy in group:
            copy.start()
    blocks = [
        [head[...] for head in heads[:7]]
        + [jnp.concatenate([heads[7][...], heads[8][...]], axis=0)]
        for heads in (own, other)
    ]
    totals = [None, None]
    for step in range(NZ // 2):
        pair = (2 * step, 2 * step + 1)
        for index in pair:
            for copy in copies[index]:
                copy.wait()
        right = split(jnp.concatenate([buf[index].reshape(HD, 512) for index in pair], axis=0))
        for side in range(2):
            left = split(jnp.concatenate([blocks[side][index] for index in pair], axis=1))
            term = dot3(left, right, MM)
            totals[side] = term if totals[side] is None else totals[side] + term
    for side in range(2):
        core = where[2] if side == 0 else 1 - where[2]
        for x in range(NX):
            total_buf[x, core] = totals[side][x * BLOCK : (x + 1) * BLOCK]
    for shift in range(NX):
        outs[shift][...] = total_buf[lax.rem(where[0] + shift, NX)]


def mix(where, own, other, weights):
    return pl.pallas_call(
        mix_kernel,
        out_shape=[jax.ShapeDtypeStruct((NK, BLOCK, 512), jnp.float32)] * NX,
        in_specs=[SMEM] + [VMEM] * 18 + [ANY],
        out_specs=[VMEM] * NX,
        scratch_shapes=[
            pltpu.VMEM((NX, NK, BLOCK, 512), jnp.float32),
            pltpu.VMEM((NZ, NY, 2, 16, 512), jnp.float32),
            pltpu.SemaphoreType.DMA((NZ, NY)),
        ],
        compiler_params=pltpu.CompilerParams(vmem_limit_bytes=50 << 20),
        cost_estimate=pl.CostEstimate(
            flops=6 * 256 * 1024 * 1024, bytes_accessed=6 << 20, transcendentals=0
        ),
        name="mix",
    )(where, *own, *other, weights)


def allowed_rows(
    head, key_block, query_block, vertical_blocks, vertical_count, slash_offsets, slash_count
):
    slots = jnp.arange(vertical_blocks.shape[1], dtype=jnp.int32)
    verticals = jnp.where(slots < vertical_count[head], vertical_blocks[head], -1)
    slashes = jnp.where(slots < slash_count[head], slash_offsets[head], -1)
    offset = query_block[:, None] - key_block[None, :]
    vert = jnp.any(key_block[:, None] == verticals[None, :], axis=1)[None, :]
    low_slash = jnp.any(offset[:, :, None] == slashes, axis=2)
    up_slash = jnp.any((offset - 1)[:, :, None] == slashes, axis=2)
    low = (offset >= 0) & (vert | low_slash)
    up = (offset >= 1) & (vert | up_slash)
    bias = jnp.where(jnp.stack([low, up]), 0.0, -jnp.inf)
    bias = jnp.repeat(bias, BLOCK, axis=2)
    return bias[0], bias[1]


CORES = [(0, 1), (1, 0)]


def along(axis, value, shift):
    count = lax.axis_size(axis)
    return lax.ppermute(value, axis, [(i, (i + shift) % count) for i in range(count)])


def shards(
    hidden_rows,
    query_weight,
    key_cache,
    value_cache,
    vertical_blocks,
    vertical_count,
    slash_offsets,
    slash_count,
    output_weight,
):
    x, y, z, k = (lax.axis_index(name) for name in ALL)
    where = jnp.stack([x, y, k, z]).astype(jnp.int32)
    weights = lax.all_gather(query_weight, ("y", "k"), axis=0)
    picked = pick(where, hidden_rows)
    hidden = [along("x", piece, shift) for shift, piece in enumerate(picked, 1)]
    behind, picked = lax.optimization_barrier((where, picked))
    near = pick_keys(behind, key_cache, value_cache)
    near = jnp.stack([near[0]] + [along("z", near[t], 2 * t) for t in range(1, NZ // 2)])
    near = jnp.concatenate([near, lax.ppermute(near, "z", [(i, i ^ 1) for i in range(NZ)])])
    rows = output_weight.reshape(2, NY, NK, 16, 512)
    kept = lax.dynamic_index_in_dim(rows, k, 2, keepdims=False)
    given = lax.dynamic_index_in_dim(rows, 1 - k, 2, keepdims=False)
    taken = lax.ppermute(given, "k", CORES)
    rows = jnp.where(k == 0, jnp.stack([kept, taken]), jnp.stack([taken, kept]))
    key_block = jnp.arange(NY, dtype=jnp.int32)[:, None, None]
    key_block = key_block + 4 * jnp.arange(NK, dtype=jnp.int32)[None, :, None]
    turns = 2 * jnp.arange(NZ // 2, dtype=jnp.int32)
    along_z = jnp.concatenate([z - turns, (z ^ 1) - turns]) % NZ
    key_block = key_block + 8 * along_z[None, None, :]
    low, up = allowed_rows(
        4 * z + x,
        key_block.reshape(-1),
        32 + 8 * jnp.arange(NX, dtype=jnp.int32) + 2 * y + k,
        vertical_blocks,
        vertical_count,
        slash_offsets,
        slash_count,
    )
    rows, near, hidden, low, up = lax.optimization_barrier((rows, near, hidden, low, up))
    rows = lax.all_to_all(rows.reshape(NX * NY, 16, 512), ("x", "y"), 0, 0)
    kv = lax.all_gather(near, ("y", "k"), axis=0)
    partial = project(where, hidden_rows, hidden, weights)
    partial = [partial[0]] + [along("x", partial[s], s) for s in range(1, NX)]
    rows, partial = lax.optimization_barrier((rows, partial))
    rows = lax.all_to_all(rows.reshape(NZ, NK, 16, 512), "z", 0, 0)
    kept = lax.dynamic_index_in_dim(rows, k, 1, keepdims=False)
    taken = lax.ppermute(lax.dynamic_index_in_dim(rows, 1 - k, 1, keepdims=False), "k", CORES)
    rows = jnp.where(k == 0, jnp.stack([kept, taken], 1), jnp.stack([taken, kept], 1))
    rows = rows.reshape(NZ * NK, 16, 512)
    out_weight = lax.all_gather(rows, "y", axis=0)
    own = attend(partial, low, up, kv)
    near_up, near_down = along("z", own, 1), along("z", own, -1)
    far_up, far_down = along("z", own, 2), along("z", own, -2)
    heads = [own, near_up, near_down, far_up, far_down]
    heads += [along("z", far_up, 1), along("z", far_down, -1)]
    heads += [along("z", far_up[:128], 2), along("z", far_down[128:], -2)]
    swapped = [lax.ppermute(head, "k", CORES) for head in heads]
    mixed = mix(where, heads, swapped, out_weight)
    mixed = [mixed[0]] + [along("x", mixed[s], s) for s in range(1, NX)]
    return ((mixed[0] + mixed[1]) + (mixed[2] + mixed[3])).reshape(NK * BLOCK, 512)


def solution(mesh):
    grid = Mesh(mesh.devices.reshape(NX, NY, NZ, NK), ALL)
    outer, ctx = ("x", "y"), ("z", "k")
    placed = (
        P(outer, None),
        P(outer, ctx),
        P(ctx, None),
        P(ctx, None),
        P(),
        P(),
        P(),
        P(),
        P(ctx, outer),
    )
    return jax.shard_map(
        shards, mesh=grid, in_specs=placed, out_specs=P(outer, ctx), check_vma=False
    )
```
